32 devices in a mesh: ma: 2 (over y), an: 16 (over z, x, core).
Axes of the slice: x: 2, y: 2, z: 4, core: 2. Of those that a mesh axis runs over, the one named last changes fastest.
Arguments:
- tokens: bfloat16 [64, 512, 768], P(('ma', 'an')), may hold values from -6 to 6
- tasks: int32 [64], P(('ma', 'an')), may hold values from 0 to 7
- segments: int32 [64, 512], P(('ma', 'an')), may hold values from 0 to 3, never falling along the last dimension, each value on 1 to 256 neighbouring positions
- buckets: int32 [1023], replicated, may hold values from 0 to 31
- w_query: bfloat16 [768, 768], replicated, may hold values from -0.21875 to 0.21875
- w_key: bfloat16 [768, 768], replicated, may hold values from -0.21875 to 0.21875
- w_value: bfloat16 [768, 768], replicated, may hold values from -0.21875 to 0.21875
- w_out: bfloat16 [768, 768], replicated, may hold values from -1.75 to 1.75
- w_up: bfloat16 [768, 3072], P('ma', 'an'), may hold values from -0.21875 to 0.21875
- w_down: bfloat16 [3072, 768], P('an', 'ma'), may hold values from -0.109375 to 0.109375
- bias_table: float32 [8, 32, 12], replicated, may hold values from -6 to 6
- gain_attn: float32 [768], replicated, may hold values from 0.5 to 1.5
- gain_ffn: float32 [768], replicated, may hold values from 0.5 to 1.5
- cotangent: bfloat16 [64, 512, 768], P(('ma', 'an')), may hold values from -6 to 6
Outputs:
- output: bfloat16 [64, 512, 768], P(('ma', 'an'))
- grad_tokens: float32 [64, 512, 768], P(('ma', 'an'))
- grad_query: float32 [768, 768], replicated
- grad_key: float32 [768, 768], replicated
- grad_value: float32 [768, 768], replicated
- grad_w_out: float32 [768, 768], replicated
- grad_up: float32 [768, 3072], P('ma', 'an')
- grad_down: float32 [3072, 768], P('an', 'ma')
- grad_table: float32 [8, 32, 12], replicated
- grad_gain_attn: float32 [768], replicated
- grad_gain_ffn: float32 [768], replicated
The draws below stay inside these ranges and needn't reach their ends.
Inputs may be any that keep to these rules, and one draw needn't show every extreme that they name: `segments`: within a row segment numbers never fall; a token attends only to tokens of its own segment.
All inputs are finite; a program needn't handle non-finite values.
Results may differ from the reference program's by a relative error of at most 0.015.
Values may be sent and summed in bfloat16 or wider, within the bound.
No kernel may reach another device: no remote copies, remote signals or barrier semaphores. Data moves between devices by JAX's collectives and lax.ppermute only.
A program may use at most 256 MiB of HBM per device.

```python
import math
import jax
import jax.numpy as jnp
import numpy as np
from jax import lax

D = 768
H = 12
DH = 64
FF = 3072
BUCKETS = 32
GROUPS = 8
L = 512
ROWS = 64


def plant(values, own_key, low, high):
    longest = values.shape.index(max(values.shape))
    spots = []
    for shift in (0, 1):
        where = [jax.random.randint(jax.random.fold_in(own_key, axis), (), 0, length) for axis, length in enumerate(values.shape)]
        where[longest] = (where[longest] + shift) % values.shape[longest]
        spots.append(tuple(where))
    return values.at[spots[0]].set(low).at[spots[1]].set(high)


def levels(key, extent, cuts, smallest, largest):
    loudness, own = 1.0, jax.random.fold_in(key, 6)
    for position, parts in cuts:
        draws = jnp.exp(jax.random.uniform(jax.random.fold_in(own, position), (parts,), jnp.float32, smallest / len(cuts), largest / len(cuts)))
        loudness = loudness * jnp.repeat(draws, extent[position] // parts).reshape([-1 if axis == position else 1 for axis in range(len(extent))])
    return loudness


def cumulative_ranks(count, lean):
    portions = [(1 << 20) // math.isqrt(grade ** lean) + 1 for grade in range(1, count + 1)]
    scale = 1 + sum(portions) // (1 << 30)
    return np.cumsum(np.array([max(1, weight // scale) for weight in portions]))


def ranked_ids(own_key, extent, number_of, lean):
    listing = cumulative_ranks(number_of, lean)
    ticket = jax.random.randint(jax.random.fold_in(own_key, 1), extent, 0, int(listing[number_of - 1]))
    standing = jnp.searchsorted(jnp.asarray(listing, jnp.int32), ticket, side="right")
    return jax.random.permutation(jax.random.fold_in(own_key, 2), number_of)[standing].astype(jnp.int32)


def split_up(amount, total, reach, slope):
    portions = [(1 << 20) // math.isqrt(standing ** slope) + 1 for standing in range(2, amount + 1)]
    surplus, holding = total - reach - (amount - 1), [1] * (amount - 1)
    while surplus > 0:
        candidates = [i for i in range(amount - 1) if holding[i] < reach]
        pool, left = sum([portions[i] for i in candidates]), surplus
        for i in candidates:
            more = min(reach - holding[i], max(1, left * portions[i] // pool), surplus)
            holding[i] = holding[i] + more
            surplus = surplus - more
    return np.array([reach] + holding)


def uneven(key, amount, total, most, skew):
    if amount == 2:
        one = jax.random.randint(key, (), max(1, total - most), min(most, total - 1) + 1)
        return jnp.stack([one, total - one])
    lengths = jnp.asarray(split_up(amount, total, most, skew), jnp.int32)
    twos = (amount - 1) // 2
    donor, receiver = lengths[1:1 + 2 * twos:2], lengths[2:2 + 2 * twos:2]
    slack = jnp.minimum(donor - 1, most - receiver)
    passed = jax.random.randint(jax.random.fold_in(key, 1), (twos,), 0, 1 << 20) % (slack + 1)
    lengths = lengths.at[1:1 + 2 * twos:2].set(donor - passed).at[2:2 + 2 * twos:2].set(receiver + passed)
    return lengths[jax.random.permutation(jax.random.fold_in(key, 2), amount)]


def centred(rng, shape, scale, limit, cuts=(), kind=jnp.bfloat16):
    drawn = jax.random.normal(rng, shape, jnp.float32) * scale
    if len(cuts) > 0:
        drawn = levels(rng, shape, cuts, -0.22, 0.18) * drawn
    return jnp.clip(drawn, min=-limit, max=limit).astype(kind)


def setup_inputs(seed: int = 0) -> dict:
    seeds = jax.random.split(jax.random.key(seed), 15)
    tokens = centred(seeds[0], (ROWS, L, D), 1.0, 6.0, ((0, 32),))
    tasks = plant(ranked_ids(seeds[1], (ROWS,), GROUPS, 2), jax.random.fold_in(seeds[1], 3), 0, GROUPS - 1).astype(jnp.int32)
    segments = jax.vmap(lambda own: jnp.searchsorted(jnp.cumsum(uneven(own, 4, L, L // 2, 0)), jnp.arange(L), side="right"))(jax.random.split(seeds[2], ROWS)).reshape((ROWS, L)).astype(jnp.int32)
    buckets = plant(jax.random.randint(seeds[3], (2 * L - 1,), 0, BUCKETS), jax.random.fold_in(seeds[3], 1), 0, BUCKETS - 1).astype(jnp.int32)
    w_query = centred(seeds[4], (D, D), D ** -0.5, 0.21875)
    w_key = centred(seeds[5], (D, D), D ** -0.5, 0.21875)
    w_value = centred(seeds[6], (D, D), D ** -0.5, 0.21875)
    w_out = centred(seeds[7], (D, D), (D // 64) ** -0.5, 1.75)
    w_up = centred(seeds[8], (D, FF), D ** -0.5, 0.21875, ((0, 2), (1, 16)))
    w_down = centred(seeds[9], (FF, D), FF ** -0.5, 0.109375, ((0, 16), (1, 2)))
    bias_table = centred(seeds[10], (GROUPS, BUCKETS, H), 1.0, 6.0, (), jnp.float32)
    gain_attn = jnp.clip(1.0 + 0.1 * jax.random.normal(seeds[11], (D,), jnp.float32), 0.5, 1.5)
    gain_ffn = jnp.clip(1.0 + 0.1 * jax.random.normal(seeds[12], (D,), jnp.float32), 0.5, 1.5)
    cotangent = centred(seeds[13], (ROWS, L, D), 1.0, 6.0, ((0, 32),))
    return {"tokens": tokens, "tasks": tasks, "segments": segments, "buckets": buckets, "w_query": w_query, "w_key": w_key, "w_value": w_value, "w_out": w_out, "w_up": w_up, "w_down": w_down, "bias_table": bias_table, "gain_attn": gain_attn, "gain_ffn": gain_ffn, "cotangent": cotangent}


@jax.custom_vjp
def low(v):
    return lax.optimization_barrier(v.astype(jnp.bfloat16)).astype(jnp.float32)

@jax.custom_vjp
def low_back(v):
    return v

def low_keep(v):
    return (low(v), None)

def low_pass(kept, grad):
    return (grad,)

def back_keep(v):
    return (v, None)

def back_low(kept, grad):
    return (low(grad),)
low.defvjp(low_keep, low_pass)
low_back.defvjp(back_keep, back_low)
epsilon = 1e-06
highest = lax.Precision.HIGHEST

def rms_scale(values, gain_vec):
    return values * lax.rsqrt(lax.optimization_barrier(jnp.mean(values * values, axis=-1, keepdims=True)) + epsilon) * gain_vec

def product(left_matrix, right_matrix):
    return jnp.dot(left_matrix, right_matrix, precision=highest, preferred_element_type=jnp.float32)

def attend_row(queries, key_rows, value_rows, bias_map, seg_ids):
    scores = jnp.einsum('ihd,jhd->hij', queries, key_rows, precision=highest) * DH ** (-0.5) + bias_map
    scores = low_back(scores)
    matching = seg_ids[:, None] == seg_ids[None, :]
    scores = jnp.where(matching[None], scores, -1e+30)
    weights_row = low(jax.nn.softmax(scores, axis=-1))
    return jnp.einsum('hij,jhd->ihd', weights_row, value_rows, precision=highest)

def encoder_layer(flat_tokens, params, tasks, segments, buckets):
    w_query, w_key, w_value, w_out, w_up, w_down, bias_table, gain_attn, gain_ffn = params
    row_count = tasks.shape[0]
    normed = low(rms_scale(flat_tokens, gain_attn))

    def project(weight):
        return low(low_back(product(normed, weight))).reshape(row_count, L, H, DH)
    queries = project(w_query)
    key_rows = project(w_key)
    value_rows = project(w_value)
    offsets = jnp.arange(L, dtype=jnp.int32)[None, :] - jnp.arange(L, dtype=jnp.int32)[:, None] + (L - 1)
    bucket_index = buckets[offsets]

    def one_row(pieces):
        row_queries, row_keys, row_values, task_id, seg_ids = pieces
        bias_map = jnp.transpose(bias_table[task_id], (1, 0))[:, bucket_index]
        return attend_row(row_queries, row_keys, row_values, bias_map, seg_ids)
    mixed_heads = lax.map(jax.checkpoint(one_row), (queries, key_rows, value_rows, tasks, segments))
    mixed_heads = low(low_back(mixed_heads.reshape(row_count * L, D)))
    middle = flat_tokens + low_back(product(mixed_heads, w_out))
    second = low(rms_scale(middle, gain_ffn))
    up_proj = low_back(product(second, w_up))
    hidden = low(jax.nn.gelu(up_proj, approximate=True))
    return middle + low_back(product(hidden, w_down))

def reference(tokens, tasks, segments, buckets, w_query, w_key, w_value, w_out, w_up, w_down, bias_table, gain_attn, gain_ffn, cotangent):
    row_count = tokens.shape[0]
    flat_tokens = tokens.astype(jnp.float32).reshape(row_count * L, D)
    params = (w_query.astype(jnp.float32), w_key.astype(jnp.float32), w_value.astype(jnp.float32), w_out.astype(jnp.float32), w_up.astype(jnp.float32), w_down.astype(jnp.float32), bias_table, gain_attn, gain_ffn)

    def forward(flat_in, weights_all):
        return encoder_layer(flat_in, weights_all, tasks, segments, buckets)
    result, pullback = jax.vjp(forward, flat_tokens, params)
    grad_flat, grads = pullback(cotangent.astype(jnp.float32).reshape(row_count * L, D))
    return (result.reshape(row_count, L, D).astype(jnp.bfloat16), grad_flat.reshape(row_count, L, D), grads[0], grads[1], grads[2], grads[3], grads[4], grads[5], grads[6], grads[7], grads[8])
```

```python
import jax
import jax.numpy as jnp
from jax import lax
from jax.sharding import PartitionSpec as P
from jax.experimental import pallas as pl
from jax.experimental.pallas import tpu as pltpu

epsilon = 1e-06
highest = lax.Precision.HIGHEST


def rms_scale(values, gain_vec):
    return (
        values * lax.rsqrt(jnp.mean(values * values, axis=-1, keepdims=True) + epsilon) * gain_vec
    )


def smooth_gate(values):
    return jax.nn.gelu(values, approximate=True)


BF=jnp.bfloat16
BLK=128
NT=(((1,),(1,)),((),()))
NN=(((1,),(0,)),((),()))

def fwd_body(q_ref,k_ref,v_ref,kseg_ref,qseg_ref,f_ref,u_ref,s_ref,o_ref):
    length=q_ref.shape[0]
    nb=length//BLK
    lane=lax.broadcasted_iota(jnp.int32,(length,BLK),1)
    q=q_ref[...]*BF(0.125)
    qaug=jnp.concatenate([q,qseg_ref[...]],axis=1)
    vt=v_ref[...].astype(jnp.float32).T.astype(BF)
    k=k_ref[...]
    outs=[]
    for h in range(2):
        kaug=jnp.concatenate([jnp.where((lane>=64)==(h==1),k,BF(0)),kseg_ref[...]],axis=1)
        toep=pltpu.roll(jnp.broadcast_to(f_ref[0,h:h+1,:],(BLK,6*BLK)),0,1,stride=1,stride_axis=0)
        vaug=jnp.concatenate([vt[64*h:64*h+64],jnp.ones((16,length),BF)],axis=0)
        parts=[]
        for s in range(nb//2):
            st=lax.dot_general(kaug,qaug[256*s:256*s+256],NT,preferred_element_type=jnp.float32)
            for half in range(2):
                qb=2*s+half
                blocks={}
                m=None
                for kb in range(nb):
                    o=kb-qb
                    if abs(o)>2: continue
                    b=st[BLK*kb:BLK*kb+BLK,BLK*half:BLK*half+BLK]+toep[:,384-BLK*o:512-BLK*o]
                    blocks[kb]=b
                    m=b if m is None else jnp.maximum(m,b)
                m=jnp.max(m,axis=0,keepdims=True)
                for kb in range(nb):
                    if kb in blocks:
                        u=jnp.exp(blocks[kb]-m).astype(BF)
                    else:
                        u=jnp.zeros((BLK,BLK),BF)
                    u_ref[0,h,BLK*kb:BLK*kb+BLK,BLK*qb:BLK*qb+BLK]=u
            ot=lax.dot_general(vaug,u_ref[0,h,:,256*s:256*s+256],NN,preferred_element_type=jnp.float32)
            r=1.0/ot[64:65]
            s_ref[0,h:h+1,256*s:256*s+256]=r
            parts.append(ot[:64]*r)
        outs.append(jnp.concatenate(parts,axis=1))
    o_ref[...]=jnp.concatenate(outs,axis=0).T.astype(BF)

def fwd(proj,kseg,qseg,f,rows,length,heads):
    pairs=heads//2
    n=rows*length
    def at(off): return pl.BlockSpec((length,BLK),lambda r,p,off=off:(r,p+off))
    return pl.pallas_call(fwd_body,grid=(rows,pairs),
        in_specs=[at(0),at(pairs),at(2*pairs),
                  pl.BlockSpec((length,BLK),lambda r,p:(r,0)),pl.BlockSpec((length,BLK),lambda r,p:(r,0)),
                  pl.BlockSpec((1,2,6*BLK),lambda r,p:(r*pairs+p,0,0))],
        out_specs=[pl.BlockSpec((1,2,length,length),lambda r,p:(r*pairs+p,0,0,0)),
                   pl.BlockSpec((1,2,length),lambda r,p:(r*pairs+p,0,0)),
                   pl.BlockSpec((length,BLK),lambda r,p:(r,p))],
        out_shape=[jax.ShapeDtypeStruct((rows*pairs,2,length,length),BF),
                   jax.ShapeDtypeStruct((rows*pairs,2,length),jnp.float32),
                   jax.ShapeDtypeStruct((n,heads*64),BF)],
        compiler_params=pltpu.CompilerParams(vmem_limit_bytes=48*1024*1024),
        name="attend")(proj,proj,proj,kseg,qseg,f)

def bwd_body(q_ref,k_ref,v_ref,u_ref,s_ref,o_ref,g_ref,dq_ref,dk_ref,dv_ref,df_ref,ds_ref):
    length=q_ref.shape[0]
    nb=length//BLK
    lane=lax.broadcasted_iota(jnp.int32,(length,BLK),1)
    q=q_ref[...]*BF(0.125)
    k=k_ref[...]; v=v_ref[...]
    kt=k.astype(jnp.float32).T.astype(BF)
    inv=jnp.concatenate([jnp.broadcast_to(s_ref[0,h:h+1,:],(64,length)) for h in range(2)],axis=0).T
    g=(g_ref[...].astype(jnp.float32)*inv)
    prod=g*o_ref[...].astype(jnp.float32)
    gl=g.astype(BF)
    phi=prod.astype(BF); plo=(prod-phi.astype(jnp.float32)).astype(BF)
    rr=lax.broadcasted_iota(jnp.int32,(2*BLK,BLK),0)
    cc=lax.broadcasted_iota(jnp.int32,(2*BLK,BLK),1)
    pick=jnp.where((((rr//64)%2)==(cc//2))&(cc<4),-1.0,0.0).astype(BF)
    cen=lax.dot_general(jnp.concatenate([phi,plo],axis=1),pick,NN,preferred_element_type=jnp.float32)
    chi=cen.astype(BF); clo=(cen-chi.astype(jnp.float32)).astype(BF)
    gaug=jnp.concatenate([gl,jnp.where(lane%2==0,chi,clo)],axis=1)
    zero=BF(0)
    dqt=[]
    dv=None; dk=None
    for h in range(2):
        mine=(lane>=64)==(h==1)
        vaug=jnp.concatenate([jnp.where(mine,v,zero),jnp.where((lane//2)==h,BF(1),zero)],axis=1)
        diag=[None]*5
        for s in range(nb//2):
            dp=lax.dot_general(vaug,gaug[256*s:256*s+256],NT,preferred_element_type=jnp.float32)
            for half in range(2):
                qb=2*s+half
                for kb in range(nb):
                    o=kb-qb
                    if abs(o)>2:
                        ds_ref[h,BLK*kb:BLK*kb+BLK,BLK*qb:BLK*qb+BLK]=jnp.zeros((BLK,BLK),BF)
                        continue
                    u=u_ref[0,h,BLK*kb:BLK*kb+BLK,BLK*qb:BLK*qb+BLK].astype(jnp.float32)
                    ds=u*dp[BLK*kb:BLK*kb+BLK,BLK*half:BLK*half+BLK]
                    ds_ref[h,BLK*kb:BLK*kb+BLK,BLK*qb:BLK*qb+BLK]=ds.astype(BF)
                    diag[o+2]=ds if diag[o+2] is None else diag[o+2]+ds
        dsm=ds_ref[h]
        t=lax.dot_general(u_ref[0,h],jnp.where(mine,gl,zero),NN,preferred_element_type=jnp.float32)
        dv=t if dv is None else dv+t
        t=lax.dot_general(dsm,jnp.where(mine,q,zero),NN,preferred_element_type=jnp.float32)
        dk=t if dk is None else dk+t
        dqt.append(lax.dot_general(kt[64*h:64*h+64],dsm,NN,preferred_element_type=jnp.float32))
        wide=jnp.concatenate([jnp.zeros((BLK,BLK),jnp.float32)]+[diag[o+2] for o in (2,1,0,-1,-2)],axis=1)
        step=BLK//2
        while step:
            wide=wide[:step]+pltpu.roll(wide[step:],6*BLK-step,1)
            step//=2
        df_ref[0,h:h+1,:]=wide
    dq_ref[...]=(jnp.concatenate(dqt,axis=0).T*0.125).astype(BF)
    dk_ref[...]=dk.astype(BF)
    dv_ref[...]=dv.astype(BF)

def bwd(proj,u,inv,mixed,gmixed,rows,length,heads):
    pairs=heads//2
    n=rows*length
    def at(off): return pl.BlockSpec((length,BLK),lambda r,p,off=off:(r,p+off))
    return pl.pallas_call(bwd_body,grid=(rows,pairs),
        in_specs=[at(0),at(pairs),at(2*pairs),
                  pl.BlockSpec((1,2,length,length),lambda r,p:(r*pairs+p,0,0,0)),
                  pl.BlockSpec((1,2,length),lambda r,p:(r*pairs+p,0,0)),
                  at(0),at(0)],
        out_specs=[at(0),at(0),at(0),pl.BlockSpec((1,2,6*BLK),lambda r,p:(r*pairs+p,0,0))],
        out_shape=[jax.ShapeDtypeStruct((n,heads*64),BF)]*3+[jax.ShapeDtypeStruct((rows*pairs,2,6*BLK),jnp.float32)],
        scratch_shapes=[pltpu.VMEM((2,length,length),BF)],
        compiler_params=pltpu.CompilerParams(vmem_limit_bytes=48*1024*1024),
        name="attend_grad")(proj,proj,proj,u,inv,mixed,gmixed)

def seg_cols(segments):
    seg=segments.reshape(-1,1)
    lane=jnp.arange(BLK)[None,:]
    kseg=(lane==seg).astype(BF)
    qseg=jnp.where((lane!=seg)&(lane<4),-1e30,0.0).astype(BF)
    return kseg,qseg
def offsets_in(table_rows,buckets):
    b=buckets[128:896][::-1]
    hot=(b[None,:]==jnp.arange(table_rows.shape[1])[:,None]).astype(jnp.float32)
    f=jnp.einsum("rbh,bk->rhk",table_rows,hot,precision=lax.Precision.HIGHEST)
    rows,heads,w=f.shape
    return f.reshape(rows*heads//2,2,w),hot


def local(
    tokens,
    tasks,
    segments,
    buckets,
    w_query,
    w_key,
    w_value,
    w_out,
    w_up,
    w_down,
    bias_table,
    gain_attn,
    gain_ffn,
    cotangent,
):
    row_count = tokens.shape[0]
    length = tokens.shape[1]
    width = tokens.shape[2]
    groups = bias_table.shape[0]
    bucket_count = bias_table.shape[1]
    heads = bias_table.shape[2]
    total = row_count * length
    flat_tokens = tokens.astype(jnp.float32).reshape(total, width)
    part_up, part_down = (
        lax.all_gather(w_up, "ma", axis=0, tiled=True),
        lax.all_gather(w_down, "ma", axis=1, tiled=True),
    )
    up_full, down_full = (
        lax.all_gather(part_up, "an", axis=1, tiled=True),
        lax.all_gather(part_down, "an", axis=0, tiled=True),
    )
    normed_f, norm_pull = jax.vjp(rms_scale, flat_tokens, gain_attn)
    normed = normed_f.astype(jnp.bfloat16)
    joined_w = jnp.concatenate((w_query, w_key, w_value), axis=1)
    projected = jnp.dot(normed, joined_w, preferred_element_type=jnp.float32).astype(jnp.bfloat16)
    task_onehot = (tasks[:, None] == jnp.arange(groups, dtype=jnp.int32)[None, :]).astype(
        jnp.float32
    )
    table_rows = jnp.einsum("rg,gbh->rbh", task_onehot, bias_table, precision=highest)
    key_cols, query_cols = seg_cols(segments)
    offset_bias, bucket_hot = offsets_in(table_rows, buckets)
    weights, inverse, mixed_flat = fwd(
        projected, key_cols, query_cols, offset_bias, row_count, length, heads
    )
    middle = flat_tokens + jnp.dot(mixed_flat, w_out, preferred_element_type=jnp.float32)
    second_f, second_pull = jax.vjp(rms_scale, middle, gain_ffn)
    second = second_f.astype(jnp.bfloat16)
    up_proj = jnp.dot(second, up_full, preferred_element_type=jnp.float32)
    hidden_f, gate_pull = jax.vjp(smooth_gate, up_proj)
    hidden = hidden_f.astype(jnp.bfloat16)
    ffn_out = jnp.dot(hidden, down_full, preferred_element_type=jnp.float32)
    output = (middle + ffn_out).astype(jnp.bfloat16).reshape(row_count, length, width)
    upstream = cotangent.astype(jnp.float32).reshape(total, width)
    upstream_low = cotangent.reshape(total, width)
    grad_down_full = jnp.einsum(
        "nf,nd->fd", hidden, upstream_low, preferred_element_type=jnp.float32
    )
    grad_hidden = jnp.einsum(
        "nd,fd->nf", upstream_low, down_full, preferred_element_type=jnp.float32
    )
    grad_up_pre = gate_pull(grad_hidden)[0].astype(jnp.bfloat16)
    grad_up_full = jnp.einsum("nd,nf->df", second, grad_up_pre, preferred_element_type=jnp.float32)
    grad_second = jnp.einsum("nf,df->nd", grad_up_pre, up_full, preferred_element_type=jnp.float32)
    grad_mid_part, grad_gain_ffn = second_pull(grad_second)
    grad_middle = upstream + grad_mid_part
    grad_attn_low = grad_middle.astype(jnp.bfloat16)
    grad_w_out = jnp.einsum(
        "nd,ne->de", mixed_flat, grad_attn_low, preferred_element_type=jnp.float32
    )
    grad_mixed = jnp.einsum("ne,de->nd", grad_attn_low, w_out, preferred_element_type=jnp.float32)
    grad_mixed = grad_mixed.astype(jnp.bfloat16)
    grad_queries, grad_keys, grad_values, grad_offset_rows = bwd(
        projected, weights, inverse, mixed_flat, grad_mixed, row_count, length, heads
    )
    grad_bucket_rows = jnp.einsum(
        "rhk,bk->rbh",
        grad_offset_rows.reshape(row_count, heads, -1),
        bucket_hot,
        precision=highest,
    )
    grad_table = jnp.einsum("rg,rbh->gbh", task_onehot, grad_bucket_rows, precision=highest)
    grad_projected = jnp.concatenate((grad_queries, grad_keys, grad_values), axis=1)
    grad_joined = jnp.einsum(
        "nd,ne->de", normed, grad_projected, preferred_element_type=jnp.float32
    )
    grad_normed = jnp.einsum(
        "ne,de->nd", grad_projected, joined_w, preferred_element_type=jnp.float32
    )
    grad_flat_part, grad_gain_attn = norm_pull(grad_normed)
    grad_tokens = (grad_middle + grad_flat_part).reshape(row_count, length, width)
    cols_up, cols_down = (
        lax.psum_scatter(
            grad_up_full.astype(jnp.bfloat16), "an", scatter_dimension=1, tiled=True
        ).astype(jnp.float32),
        lax.psum_scatter(
            grad_down_full.astype(jnp.bfloat16), "an", scatter_dimension=0, tiled=True
        ).astype(jnp.float32),
    )
    grad_up, grad_down = (
        lax.psum_scatter(
            cols_up.astype(jnp.bfloat16), "ma", scatter_dimension=0, tiled=True
        ).astype(jnp.float32),
        lax.psum_scatter(
            cols_down.astype(jnp.bfloat16), "ma", scatter_dimension=1, tiled=True
        ).astype(jnp.float32),
    )
    grad_query, grad_key, grad_value, grad_w_out, grad_table, grad_gain_attn, grad_gain_ffn = (
        lax.psum(
            (
                grad_joined[:, :width],
                grad_joined[:, width : 2 * width],
                grad_joined[:, 2 * width :],
                grad_w_out,
                grad_table,
                grad_gain_attn,
                grad_gain_ffn,
            ),
            ("ma", "an"),
        )
    )
    return (
        output,
        grad_tokens,
        grad_query,
        grad_key,
        grad_value,
        grad_w_out,
        grad_up,
        grad_down,
        grad_table,
        grad_gain_attn,
        grad_gain_ffn,
    )


def solution(mesh):
    in_specs = (
        P(("ma", "an"), None, None),
        P(("ma", "an")),
        P(("ma", "an"), None),
        P(),
        P(),
        P(),
        P(),
        P(),
        P("ma", "an"),
        P("an", "ma"),
        P(),
        P(),
        P(),
        P(("ma", "an"), None, None),
    )
    out_specs = (
        P(("ma", "an"), None, None),
        P(("ma", "an"), None, None),
        P(),
        P(),
        P(),
        P(),
        P("ma", "an"),
        P("an", "ma"),
        P(),
        P(),
        P(),
    )
    return jax.shard_map(local, mesh=mesh, in_specs=in_specs, out_specs=out_specs, check_vma=False)
```

```python
import jax
import jax.numpy as jnp
from jax import lax
from jax.sharding import PartitionSpec as P
from jax.experimental import pallas as pl
from jax.experimental.pallas import tpu as pltpu

epsilon = 1e-06
highest = lax.Precision.HIGHEST
F32 = jnp.float32
BF16 = jnp.bfloat16
BLOCK = 128
REACH = 2
WIDE = 6 * BLOCK
CONTRACT_LANES = (((1,), (1,)), ((), ()))
CONTRACT_ROWS = (((0,), (0,)), ((), ()))
PLAIN = (((1,), (0,)), ((), ()))
hold = lax.optimization_barrier


def dot(a, b, dims=PLAIN):
    return lax.dot_general(a, b, dims, preferred_element_type=F32)


def attend_body(p_ref, kseg_ref, qseg_ref, f_ref, *refs):
    u_ref, s_ref, o_ref = refs[-3:]
    length = p_ref.shape[0]
    blocks = length // BLOCK
    lane = lax.broadcasted_iota(jnp.int32, (length, BLOCK), 1)
    q_aug = jnp.concatenate([p_ref[:, :BLOCK] * BF16(0.125), qseg_ref[...]], axis=1)
    k = p_ref[:, BLOCK : 2 * BLOCK]
    v_t = p_ref[:, 2 * BLOCK :].astype(F32).T.astype(BF16)
    outs = []
    for h in range(2):
        k_aug = jnp.concatenate(
            [jnp.where((lane >= 64) == (h == 1), k, BF16(0)), kseg_ref[...]], axis=1
        )
        tiles = pltpu.roll(
            jnp.broadcast_to(f_ref[0, h : h + 1, :], (BLOCK, WIDE)), 0, 1, stride=1, stride_axis=0
        )
        v_aug = jnp.concatenate([v_t[64 * h : 64 * h + 64], jnp.ones((16, length), BF16)], axis=0)
        parts = []
        for s in range(blocks // 2):
            st = dot(k_aug, q_aug[256 * s : 256 * s + 256], CONTRACT_LANES)
            for half in range(2):
                qb = 2 * s + half
                scored = {}
                peak = None
                for kb in range(blocks):
                    o = kb - qb
                    if abs(o) > REACH:
                        continue
                    b = (
                        st[BLOCK * kb : BLOCK * kb + BLOCK, BLOCK * half : BLOCK * half + BLOCK]
                        + tiles[:, 384 - BLOCK * o : 512 - BLOCK * o]
                    )
                    scored[kb] = b
                    peak = b if peak is None else jnp.maximum(peak, b)
                peak = jnp.max(peak, axis=0, keepdims=True)
                for kb in range(blocks):
                    if kb in scored:
                        e = jnp.exp(scored[kb] - peak).astype(BF16)
                    else:
                        e = jnp.zeros((BLOCK, BLOCK), BF16)
                    u_ref[0, h, BLOCK * kb : BLOCK * kb + BLOCK, BLOCK * qb : BLOCK * qb + BLOCK] = e
            ot = dot(v_aug, u_ref[0, h, :, 256 * s : 256 * s + 256])
            r = 1.0 / ot[64:65]
            s_ref[0, h : h + 1, 256 * s : 256 * s + 256] = r
            parts.append(ot[:64] * r)
        outs.append(jnp.concatenate(parts, axis=1))
    o_ref[...] = jnp.concatenate(outs, axis=0).T.astype(BF16)


def attend(group, first, count, pairs, rows, length, proj, kseg, qseg, bias, mixed):
    steps = rows * count
    args = [proj, kseg, qseg, bias]
    specs = [
        pl.BlockSpec((None, length, 3 * BLOCK), lambda p, r: (group, r, p)),
        pl.BlockSpec((length, BLOCK), lambda p, r: (r, 0)),
        pl.BlockSpec((length, BLOCK), lambda p, r: (r, 0)),
        pl.BlockSpec((1, 2, WIDE), lambda p, r: (r * pairs + first + p, 0, 0)),
    ]
    alias = {}
    if mixed is not None:
        alias = {len(args): 2}
        args.append(mixed)
        specs.append(pl.BlockSpec(memory_space=pl.ANY))
    return pl.pallas_call(
        attend_body,
        grid=(count, rows),
        in_specs=specs,
        out_specs=[
            pl.BlockSpec((1, 2, length, length), lambda p, r: (p * rows + r, 0, 0, 0)),
            pl.BlockSpec((1, 2, length), lambda p, r: (p * rows + r, 0, 0)),
            pl.BlockSpec((length, BLOCK), lambda p, r: (r, first + p)),
        ],
        out_shape=[
            jax.ShapeDtypeStruct((steps, 2, length, length), BF16),
            jax.ShapeDtypeStruct((steps, 2, length), F32),
            jax.ShapeDtypeStruct((rows * length, pairs * BLOCK), BF16),
        ],
        input_output_aliases=alias,
        compiler_params=pltpu.CompilerParams(vmem_limit_bytes=14 * 1024 * 1024),
        cost_estimate=pl.CostEstimate(
            flops=steps * 16 * length * length * 64,
            bytes_accessed=steps * 5 * length * length,
            transcendentals=steps * 2 * length * length,
        ),
        name="attend",
    )(*args)


def attend_grad_body(p_ref, u_ref, s_ref, o_ref, g_ref, dp_ref, df_ref, ds_ref):
    length = p_ref.shape[0]
    blocks = length // BLOCK
    lane = lax.broadcasted_iota(jnp.int32, (length, BLOCK), 1)
    q = p_ref[:, :BLOCK] * BF16(0.125)
    k = p_ref[:, BLOCK : 2 * BLOCK]
    v = p_ref[:, 2 * BLOCK :]
    k_t = k.astype(F32).T.astype(BF16)
    inv = jnp.concatenate(
        [jnp.broadcast_to(s_ref[0, h : h + 1, :], (64, length)) for h in range(2)], axis=0
    ).T
    g = g_ref[...].astype(F32) * inv
    prod = g * o_ref[...].astype(F32)
    g_low = g.astype(BF16)
    prod_hi = prod.astype(BF16)
    prod_lo = (prod - prod_hi.astype(F32)).astype(BF16)
    row = lax.broadcasted_iota(jnp.int32, (2 * BLOCK, BLOCK), 0)
    col = lax.broadcasted_iota(jnp.int32, (2 * BLOCK, BLOCK), 1)
    pick = jnp.where((((row // 64) % 2) == (col // 2)) & (col < 4), -1.0, 0.0).astype(BF16)
    centre = dot(jnp.concatenate([prod_hi, prod_lo], axis=1), pick)
    centre_hi = centre.astype(BF16)
    centre_lo = (centre - centre_hi.astype(F32)).astype(BF16)
    g_aug = jnp.concatenate([g_low, jnp.where(lane % 2 == 0, centre_hi, centre_lo)], axis=1)
    zero = BF16(0)
    dq_t = []
    dv = None
    dk = None
    for h in range(2):
        mine = (lane >= 64) == (h == 1)
        v_aug = jnp.concatenate(
            [jnp.where(mine, v, zero), jnp.where((lane // 2) == h, BF16(1), zero)], axis=1
        )
        diag = [None] * (2 * REACH + 1)
        for s in range(blocks // 2):
            dp = dot(v_aug, g_aug[256 * s : 256 * s + 256], CONTRACT_LANES)
            for half in range(2):
                qb = 2 * s + half
                for kb in range(blocks):
                    o = kb - qb
                    krows = slice(BLOCK * kb, BLOCK * kb + BLOCK)
                    qcols = slice(BLOCK * qb, BLOCK * qb + BLOCK)
                    if abs(o) > REACH:
                        ds_ref[h, krows, qcols] = jnp.zeros((BLOCK, BLOCK), BF16)
                        continue
                    ds = (
                        u_ref[0, h, krows, qcols].astype(F32)
                        * dp[krows, BLOCK * half : BLOCK * half + BLOCK]
                    )
                    ds_ref[h, krows, qcols] = ds.astype(BF16)
                    diag[o + REACH] = ds if diag[o + REACH] is None else diag[o + REACH] + ds
        ds_all = ds_ref[h]
        t = dot(u_ref[0, h], jnp.where(mine, g_low, zero))
        dv = t if dv is None else dv + t
        t = dot(ds_all, jnp.where(mine, q, zero))
        dk = t if dk is None else dk + t
        dq_t.append(dot(k_t[64 * h : 64 * h + 64], ds_all))
        wide = jnp.concatenate([jnp.zeros((BLOCK, BLOCK), F32)] + diag[::-1], axis=1)
        step = BLOCK // 2
        while step:
            wide = wide[:step] + pltpu.roll(wide[step:], WIDE - step, 1)
            step //= 2
        df_ref[0, h : h + 1, :] = wide
    dq = jnp.concatenate(dq_t, axis=0).T * 0.125
    dp_ref[...] = jnp.concatenate([dq.astype(BF16), dk.astype(BF16), dv.astype(BF16)], axis=1)


def attend_grad(group, first, count, pairs, rows, length, proj, saved, inverse, mixed, grad_mixed):
    steps = rows * count
    return pl.pallas_call(
        attend_grad_body,
        grid=(count, rows),
        in_specs=[
            pl.BlockSpec((None, length, 3 * BLOCK), lambda p, r: (group, r, p)),
            pl.BlockSpec((1, 2, length, length), lambda p, r: (p * rows + r, 0, 0, 0)),
            pl.BlockSpec((1, 2, length), lambda p, r: (p * rows + r, 0, 0)),
            pl.BlockSpec((length, BLOCK), lambda p, r: (r, first + p)),
            pl.BlockSpec((length, BLOCK), lambda p, r: (r, first + p)),
        ],
        out_specs=[
            pl.BlockSpec((length, 3 * BLOCK), lambda p, r: (r, p)),
            pl.BlockSpec((1, 2, WIDE), lambda p, r: (p * rows + r, 0, 0)),
        ],
        out_shape=[
            jax.ShapeDtypeStruct((rows * length, count * 3 * BLOCK), BF16),
            jax.ShapeDtypeStruct((steps, 2, WIDE), F32),
        ],
        scratch_shapes=[pltpu.VMEM((2, length, length), BF16)],
        compiler_params=pltpu.CompilerParams(vmem_limit_bytes=16 * 1024 * 1024),
        cost_estimate=pl.CostEstimate(
            flops=steps * 32 * length * length * 64,
            bytes_accessed=steps * 5 * length * length,
            transcendentals=0,
        ),
        name="attend_grad",
    )(proj, saved, inverse, mixed, grad_mixed)


def pick(options, index):
    out = options[0]
    for k in range(1, len(options)):
        out = jnp.where(index == k, options[k], out)
    return out


def by_distance(slices, at):
    n = len(slices)
    return [pick(slices, lax.rem(at - t + n, n)) for t in range(n)]


def in_order(pieces, at):
    n = len(pieces)
    return [pick(pieces, lax.rem(at - k + n, n)) for k in range(n)]


def cut_rows(v, n):
    size = v.shape[0] // n
    return [v[size * k : size * k + size] for k in range(n)]


def cut_lanes(v, n):
    size = v.shape[-1] // n
    return [v[..., size * k : size * k + size] for k in range(n)]


def total(parts):
    out = parts[0].astype(F32)
    for p in parts[1:]:
        out = out + p.astype(F32)
    return out


class Links:
    def __init__(self, ma, an, width):
        z = min(4, an // 2)
        self.an = an
        self.size = {"y": ma, "z": z, "x": an // (2 * z), "c": 2}
        self.stride = {"c": 1, "x": 2, "z": 2 * self.size["x"]}
        self.tidy = width % (ma * BLOCK) == 0 and width % (8 * ma * an) == 0

    def places(self):
        an = lax.axis_index("an")
        found = [lax.axis_index("ma")]
        found += [(an // self.stride[a]) % self.size[a] for a in ("z", "x", "c")]
        return jnp.stack([f.astype(jnp.int32) for f in found])

    def fetch(self, value, axis, back):
        n = self.size[axis]
        if axis == "y":
            return lax.ppermute(value, "ma", [(i, (i + back) % n) for i in range(n)])
        s = self.stride[axis]
        pairs = []
        for i in range(self.an):
            at = (i // s) % n
            pairs.append((i, i + ((at + back) % n - at) * s))
        return lax.ppermute(value, "an", pairs)

    def gather(self, value, axis):
        return [value] + [self.fetch(value, axis, t) for t in range(1, self.size[axis])]

    def spread(self, parts, axis):
        n = self.size[axis]
        return [parts[0]] + [self.fetch(parts[t], axis, n - t) for t in range(1, n)]

    def stage(self, fn, arrays, shapes, name, steps=1):
        outs = [jax.ShapeDtypeStruct(s, BF16) for s in shapes]
        place = self.places()
        if not self.tidy:
            got = fn(*[place[i] for i in range(4)], *arrays)
            return [g.astype(BF16).reshape(o.shape) for g, o in zip(got, outs)]
        count = len(arrays)

        def body(place_ref, *refs):
            got = fn(*[place_ref[i] for i in range(4)], *[r[...] for r in refs[:count]])
            for g, r in zip(got, refs[count:]):
                r[...] = g.astype(BF16)

        def spec(a):
            rest = len(a.shape) - 1
            return pl.BlockSpec(
                (a.shape[0] // steps,) + a.shape[1:], lambda i, p, rest=rest: (i,) + (0,) * rest
            )

        return pl.pallas_call(
            body,
            grid_spec=pltpu.PrefetchScalarGridSpec(
                num_scalar_prefetch=1,
                grid=(steps,),
                in_specs=[spec(a) for a in arrays],
                out_specs=[spec(o) for o in outs],
            ),
            out_shape=outs,
            compiler_params=pltpu.CompilerParams(vmem_limit_bytes=16 * 1024 * 1024),
            name=name,
        )(place, *arrays)


def gather_1(net, pieces):
    rows, cols = pieces[0].shape
    half = rows // 2
    n = len(pieces)

    def fn(y, z, x, c, *pieces):
        v = jnp.stack(in_order(pieces, z))
        return [v[:, :half], v[:, half:]]

    a, b = net.stage(fn, pieces, [(n, half, cols)] * 2, "gather_z")
    return net.gather(a, "x"), net.gather(b, "y")


def gather_2(net, state):
    a, b = state
    n, half, cols = a[0].shape

    def fn(y, z, x, c, *parts):
        a_in = in_order(parts[: len(a)], x)
        b_in = in_order(parts[len(a) :], y)
        return [jnp.stack(a_in, axis=1), jnp.concatenate(b_in, axis=-1)]

    a, b = net.stage(
        fn, a + b, [(n, len(a), half, cols), (n, half, cols * len(b))], "gather_xy"
    )
    return net.gather(a, "y"), net.gather(b, "x")


def gather_3(net, state):
    a, b = state
    n, nx, half, cols = a[0].shape

    def fn(y, z, x, c, *parts):
        a_in = jnp.concatenate(in_order(parts[: len(a)], y), axis=-1)
        b_in = jnp.stack(in_order(parts[len(a) :], x), axis=1)
        return [jnp.concatenate([a_in, b_in], axis=2)]

    (own,) = net.stage(
        fn, a + b, [(n, nx, 2 * half, cols * len(a))], "gather_yx", steps=n if net.tidy else 1
    )
    return own


def scatter_1(net, own, theirs, first):
    shape = own.shape
    n = net.size[first]
    z_n = shape[0]

    def fn(y, z, x, c, own, theirs):
        v = total([own, theirs])
        if first == "y":
            return by_distance(cut_lanes(v, n), y)
        return by_distance([v[:, k] for k in range(n)], x)

    out = shape[:-1] + (shape[-1] // n,) if first == "y" else (shape[0],) + shape[2:]
    parts = net.stage(fn, [own, theirs], [out] * n, "scatter_" + first, steps=z_n if net.tidy else 1)
    return net.spread(parts, first)


def scatter_2(net, parts, second):
    shape = parts[0].shape
    n = net.size[second]

    def fn(y, z, x, c, *parts):
        v = total(parts)
        if second == "y":
            return by_distance(cut_lanes(v, n), y)
        return by_distance([v[:, k] for k in range(n)], x)

    out = shape[:-1] + (shape[-1] // n,) if second == "y" else (shape[0],) + shape[2:]
    parts = net.stage(fn, parts, [out] * n, "scatter_" + second, steps=shape[0] if net.tidy else 1)
    return net.spread(parts, second)


def scatter_3(net, parts):
    n = net.size["z"]

    def fn(y, z, x, c, *parts):
        v = total(parts)
        return by_distance([v[k] for k in range(n)], z)

    return net.spread(net.stage(fn, parts, [parts[0].shape[1:]] * n, "scatter_z"), "z")


def reduce_1(net, own, theirs, cut):
    rows, cols = own.shape
    ny, nx = net.size["y"], net.size["x"]

    def fn(y, z, x, c, own, theirs):
        v = total([own, theirs])
        return by_distance(cut_rows(v[:, :cut], ny), y) + by_distance(cut_rows(v[:, cut:], nx), x)

    parts = net.stage(
        fn,
        [own, theirs],
        [(rows // ny, cut)] * ny + [(rows // nx, cols - cut)] * nx,
        "reduce_yx",
    )
    return net.spread(parts[:ny], "y"), net.spread(parts[ny:], "x")


def reduce_2(net, state):
    a, b = state
    ny, nx = net.size["y"], net.size["x"]

    def fn(y, z, x, c, *parts):
        va, vb = total(parts[: len(a)]), total(parts[len(a) :])
        return by_distance(cut_rows(va, nx), x) + by_distance(cut_rows(vb, ny), y)

    parts = net.stage(
        fn,
        a + b,
        [(a[0].shape[0] // nx, a[0].shape[1])] * nx + [(b[0].shape[0] // ny, b[0].shape[1])] * ny,
        "reduce_xy",
    )
    return net.spread(parts[:nx], "x"), net.spread(parts[nx:], "y")


def reduce_3(net, state):
    a, b = state
    n = net.size["z"]

    def fn(y, z, x, c, *parts):
        v = jnp.concatenate([total(parts[: len(a)]), total(parts[len(a) :])], axis=1)
        return by_distance(cut_rows(v, n), z)

    shape = (a[0].shape[0] // n, a[0].shape[1] + b[0].shape[1])
    return net.spread(net.stage(fn, a + b, [shape] * n, "reduce_z"), "z")


def spread_0(net, payloads, cuts):
    counts = [len(p) for p in payloads]
    rows = payloads[0][0].shape[0]
    cols = sum(p[0].shape[1] for p in payloads)

    def fn(y, z, x, c, *parts):
        sums = []
        for n in counts:
            sums.append(total(parts[:n]))
            parts = parts[n:]
        return [
            jnp.concatenate(
                [v[:, :k] for v, k in zip(sums, cuts)] + [v[:, k:] for v, k in zip(sums, cuts)],
                axis=1,
            )
        ]

    (front,) = net.stage(fn, [p for ps in payloads for p in ps], [(rows, cols)], "spread_sum")
    return net.gather(front, "z")


def spread_1(net, pieces, cut):
    rows, cols = pieces[0].shape
    n = len(pieces)

    def fn(y, z, x, c, *pieces):
        v = jnp.concatenate([p.astype(F32) for p in in_order(pieces, z)], axis=0)
        return [v[:, :cut], v[:, cut:]]

    a, b = net.stage(fn, pieces, [(n * rows, cut), (n * rows, cols - cut)], "spread_z")
    return net.gather(a, "x"), net.gather(b, "y")


def spread_2(net, state):
    a, b = state

    def fn(y, z, x, c, *parts):
        va = jnp.concatenate(in_order(parts[: len(a)], x), axis=0)
        vb = jnp.concatenate(in_order(parts[len(a) :], y), axis=0)
        return [va, vb]

    shapes = [(len(p) * p[0].shape[0], p[0].shape[1]) for p in (a, b)]
    a, b = net.stage(fn, a + b, shapes, "spread_xy")
    return net.gather(a, "y"), net.gather(b, "x")


def spread_3(net, state):
    a, b = state

    def fn(y, z, x, c, *parts):
        va = jnp.concatenate(in_order(parts[: len(a)], y), axis=0)
        vb = jnp.concatenate(in_order(parts[len(a) :], x), axis=0)
        return [jnp.concatenate([va, vb], axis=1)]

    shape = (len(a) * a[0].shape[0], a[0].shape[1] + b[0].shape[1])
    (v,) = net.stage(fn, a + b, [shape], "spread_yx")
    return net.gather(v, "c")


def finish(net, own, other, cuts, weights, gain):
    half, cols = own.shape
    tile = BLOCK
    steps = half // tile
    widths = [sum(b - a for a, b in runs) for runs in cuts]

    def body(place_ref, own_ref, other_ref, wq_ref, wk_ref, wv_ref, gain_ref, *outs):
        mine = (pl.program_id(0) // steps) == place_ref[3]
        v = jnp.where(mine, own_ref[...].astype(F32), other_ref[...].astype(F32))
        made = [jnp.concatenate([v[:, a:b] for a, b in runs], axis=1) for runs in cuts]
        for out, m in zip(outs, made):
            out[...] = m
        acc = made[1] * wq_ref[...].astype(F32)
        acc = acc + made[2] * wk_ref[...].astype(F32) + made[3] * wv_ref[...].astype(F32)
        outs[-1][...] = jnp.sum(acc, axis=1, keepdims=True) / gain_ref[...]

    def row_spec(w):
        return pl.BlockSpec((tile, w), lambda i, p: (i, 0))

    return pl.pallas_call(
        body,
        grid_spec=pltpu.PrefetchScalarGridSpec(
            num_scalar_prefetch=1,
            grid=(2 * steps,),
            in_specs=[pl.BlockSpec((tile, cols), lambda i, p: (i % steps, 0))] * 2
            + [row_spec(w.shape[1]) for w in weights]
            + [row_spec(1)],
            out_specs=[row_spec(w) for w in widths] + [row_spec(1)],
        ),
        out_shape=[jax.ShapeDtypeStruct((2 * half, w), F32) for w in widths + [1]],
        compiler_params=pltpu.CompilerParams(vmem_limit_bytes=16 * 1024 * 1024),
        name="finish",
    )(net.places(), own, other, *weights, gain.reshape(-1, 1))


def project(normed, weights, groups):
    count, width = normed.shape
    cols = width // groups
    local_pairs = cols // BLOCK

    def body(n_ref, *refs):
        out = refs[-1]
        for i, w in enumerate(refs[:-1]):
            r = dot(n_ref[...], w[...]).astype(BF16)
            for p in range(local_pairs):
                at = (3 * p + i) * BLOCK
                out[0, :, at : at + BLOCK] = r[:, BLOCK * p : BLOCK * p + BLOCK]

    return pl.pallas_call(
        body,
        grid=(groups,),
        in_specs=[pl.BlockSpec((count, width), lambda i: (0, 0))]
        + [pl.BlockSpec((width, cols), lambda i: (0, i))] * 3,
        out_specs=pl.BlockSpec((1, count, 3 * cols), lambda i: (i, 0, 0)),
        out_shape=jax.ShapeDtypeStruct((groups, count, 3 * cols), BF16),
        compiler_params=pltpu.CompilerParams(vmem_limit_bytes=20 * 1024 * 1024),
        cost_estimate=pl.CostEstimate(
            flops=6 * count * width * width, bytes_accessed=14 * count * width, transcendentals=0
        ),
        name="project",
    )(normed, *weights)


def gelu_parts(pre):
    k0 = 0.7978845608028654
    k1 = 0.044715
    sq = pre * pre
    t = jnp.tanh(pre * (k0 + (k0 * k1) * sq))
    h = 0.5 * pre
    act = h + h * t
    slope = 0.5 + 0.5 * t + (h - h * (t * t)) * (k0 + (3.0 * k0 * k1) * sq)
    return act.astype(BF16), slope.astype(BF16)


def ffn_up(net, up_own, up_other, second, g):
    nz, nx, hb, width = up_own.shape
    count = second.shape[0]

    def body(place_ref, own_ref, other_ref, s_ref, g_ref, hid_ref, slope_ref, go_ref, gt_ref):
        c = place_ref[3]
        for at, w_ref, out in ((c, own_ref, go_ref), (1 - c, other_ref, gt_ref)):
            pre = dot(w_ref[0].reshape(nx * hb, width), s_ref[...], CONTRACT_LANES)
            act, slope = gelu_parts(pre)
            for i in range(nx):
                hid_ref[0, i, at] = act[hb * i : hb * i + hb]
                slope_ref[0, i, at] = slope[hb * i : hb * i + hb]
            out[0] = dot(act, g_ref[...]).astype(BF16).reshape(nx, hb, width)

    w_spec = pl.BlockSpec((1, nx, hb, width), lambda i, p: (i, 0, 0, 0))
    t_spec = pl.BlockSpec((count, width), lambda i, p: (0, 0))
    h_spec = pl.BlockSpec((1, nx, 2, hb, count), lambda i, p: (i, 0, 0, 0, 0))
    return pl.pallas_call(
        body,
        grid_spec=pltpu.PrefetchScalarGridSpec(
            num_scalar_prefetch=1,
            grid=(nz,),
            in_specs=[w_spec, w_spec, t_spec, t_spec],
            out_specs=[h_spec, h_spec, w_spec, w_spec],
        ),
        out_shape=[jax.ShapeDtypeStruct((nz, nx, 2, hb, count), BF16)] * 2
        + [jax.ShapeDtypeStruct(up_own.shape, BF16)] * 2,
        compiler_params=pltpu.CompilerParams(vmem_limit_bytes=30 * 1024 * 1024),
        cost_estimate=pl.CostEstimate(
            flops=8 * nz * nx * hb * count * width,
            bytes_accessed=20 * count * width,
            transcendentals=2 * nz * nx * hb * count,
        ),
        name="ffn_up",
    )(net.places(), up_own, up_other, second, g)


def ffn_back(net, up_own, up_other, down_full, slope, second, g):
    nz, nx, hb, width = up_own.shape
    count = second.shape[0]
    part = nx * hb
    down = down_full.reshape(nz, nx, 2, hb, width)

    def body(
        place_ref, own_ref, other_ref, d_ref, slope_ref, s_ref, g_ref, go_ref, gt_ref, gs_ref, gu_ref
    ):
        c = place_ref[3]
        for rel, at in ((0, c), (1, 1 - c)):
            w = jnp.concatenate([d_ref[0, i, at] for i in range(nx)], axis=0)
            gh = dot(w, g_ref[...], CONTRACT_LANES)
            sl = jnp.concatenate([slope_ref[0, i, at] for i in range(nx)], axis=0)
            gu = (gh * sl.astype(F32)).astype(BF16)
            gu_ref[part * rel : part * rel + part] = gu
            out = (go_ref, gt_ref)[rel]
            out[0] = dot(gu, s_ref[...]).astype(BF16).reshape(nx, hb, width)
        w = jnp.concatenate(
            [own_ref[0].reshape(part, width), other_ref[0].reshape(part, width)], axis=0
        )
        add = dot(gu_ref[...], w, CONTRACT_ROWS)

        @pl.when(pl.program_id(0) == 0)
        def _():
            gs_ref[...] = add

        @pl.when(pl.program_id(0) != 0)
        def _():
            gs_ref[...] += add

    w_spec = pl.BlockSpec((1, nx, hb, width), lambda i, p: (i, 0, 0, 0))
    d_spec = pl.BlockSpec((1, nx, 2, hb, width), lambda i, p: (i, 0, 0, 0, 0))
    t_spec = pl.BlockSpec((count, width), lambda i, p: (0, 0))
    h_spec = pl.BlockSpec((1, nx, 2, hb, count), lambda i, p: (i, 0, 0, 0, 0))
    return pl.pallas_call(
        body,
        grid_spec=pltpu.PrefetchScalarGridSpec(
            num_scalar_prefetch=1,
            grid=(nz,),
            in_specs=[w_spec, w_spec, d_spec, h_spec, t_spec, t_spec],
            out_specs=[w_spec, w_spec, t_spec],
            scratch_shapes=[pltpu.VMEM((2 * part, count), BF16)],
        ),
        out_shape=[jax.ShapeDtypeStruct(up_own.shape, BF16)] * 2
        + [jax.ShapeDtypeStruct((count, width), F32)],
        compiler_params=pltpu.CompilerParams(vmem_limit_bytes=36 * 1024 * 1024),
        cost_estimate=pl.CostEstimate(
            flops=12 * nz * nx * hb * count * width,
            bytes_accessed=30 * count * width,
            transcendentals=0,
        ),
        name="ffn_back",
    )(net.places(), up_own, up_other, down, slope, second, g)


def ffn_out(hidden, down_full, middle):
    nz = hidden.shape[0]
    count, width = middle.shape
    part = down_full.shape[0] // nz
    flat = hidden.reshape(nz * part, count)

    def body(h_ref, w_ref, m_ref, out_ref, acc_ref):
        add = dot(h_ref[...], w_ref[...], CONTRACT_ROWS)
        step = pl.program_id(0)

        @pl.when(step == 0)
        def _():
            acc_ref[...] = m_ref[...] + add

        @pl.when(step != 0)
        def _():
            acc_ref[...] += add

        @pl.when(step == nz - 1)
        def _():
            out_ref[...] = acc_ref[...].astype(BF16)

    return pl.pallas_call(
        body,
        grid=(nz,),
        in_specs=[
            pl.BlockSpec((part, count), lambda i: (i, 0)),
            pl.BlockSpec((part, width), lambda i: (i, 0)),
            pl.BlockSpec((count, width), lambda i: (0, 0)),
        ],
        out_specs=pl.BlockSpec((count, width), lambda i: (0, 0)),
        out_shape=jax.ShapeDtypeStruct((count, width), BF16),
        scratch_shapes=[pltpu.VMEM((count, width), F32)],
        compiler_params=pltpu.CompilerParams(vmem_limit_bytes=20 * 1024 * 1024),
        cost_estimate=pl.CostEstimate(
            flops=2 * nz * part * count * width, bytes_accessed=20 * count * width, transcendentals=0
        ),
        name="ffn_out",
    )(flat, down_full, middle)


def weight_grad(net, left, right, at, cols, buffers):
    count, rows = left.shape
    half = rows // 2
    width = right.shape[1]
    given = [] if buffers is None else list(buffers)

    def body(place_ref, mine_ref, other_ref, r_ref, *refs):
        for l, out in ((mine_ref, refs[-2]), (other_ref, refs[-1])):
            out[...] = dot(l[...], r_ref[...], CONTRACT_ROWS).astype(BF16)

    out_spec = pl.BlockSpec((half, width), lambda i, p: (0, at // width))
    return pl.pallas_call(
        body,
        grid_spec=pltpu.PrefetchScalarGridSpec(
            num_scalar_prefetch=1,
            grid=(1,),
            in_specs=[
                pl.BlockSpec((count, half), lambda i, p: (0, p[3])),
                pl.BlockSpec((count, half), lambda i, p: (0, 1 - p[3])),
                pl.BlockSpec((count, width), lambda i, p: (0, 0)),
            ]
            + [pl.BlockSpec(memory_space=pl.ANY)] * len(given),
            out_specs=[out_spec, out_spec],
        ),
        out_shape=[jax.ShapeDtypeStruct((half, cols), BF16)] * 2,
        input_output_aliases={4 + i: i for i in range(len(given))},
        compiler_params=pltpu.CompilerParams(vmem_limit_bytes=16 * 1024 * 1024),
        cost_estimate=pl.CostEstimate(
            flops=2 * count * rows * width, bytes_accessed=6 * count * width, transcendentals=0
        ),
        name="weight_grad",
    )(net.places(), left, left, right, *given)


def token_grad(dproj, weights, tokens, inv, gain, grad_middle):
    count, width = tokens.shape
    tile = min(256, count)

    def body(*refs):
        d_refs = refs[: len(dproj)]
        w_refs = refs[len(dproj) : len(dproj) + 3]
        t_ref, inv_ref, gain_ref, gm_ref, out_ref = refs[len(dproj) + 3 :]
        gn = None
        for i, w in enumerate(w_refs):
            cols = []
            for d in d_refs:
                for p in range(d.shape[1] // (3 * BLOCK)):
                    at = (3 * p + i) * BLOCK
                    cols.append(d[:, at : at + BLOCK])
            r = dot(jnp.concatenate(cols, axis=1), w[...], CONTRACT_LANES)
            gn = r if gn is None else gn + r
        scaled = gn * gain_ref[...]
        x = t_ref[...].astype(F32)
        r = inv_ref[...]
        mean = jnp.mean(scaled * x, axis=1, keepdims=True)
        out_ref[...] = gm_ref[...] + r * scaled - x * (r * r * r * mean)

    def rows_of(w):
        return pl.BlockSpec((tile, w), lambda i: (i, 0))

    return pl.pallas_call(
        body,
        grid=(count // tile,),
        in_specs=[rows_of(d.shape[1]) for d in dproj]
        + [pl.BlockSpec(w.shape, lambda i: (0, 0)) for w in weights]
        + [rows_of(width), rows_of(1), pl.BlockSpec((1, width), lambda i: (0, 0)), rows_of(width)],
        out_specs=rows_of(width),
        out_shape=jax.ShapeDtypeStruct((count, width), F32),
        compiler_params=pltpu.CompilerParams(vmem_limit_bytes=20 * 1024 * 1024),
        cost_estimate=pl.CostEstimate(
            flops=6 * count * width * width, bytes_accessed=24 * count * width, transcendentals=0
        ),
        name="token_grad",
    )(*dproj, *weights, tokens, inv, gain.reshape(1, -1), grad_middle)


def local(
    net,
    tokens,
    tasks,
    segments,
    buckets,
    w_query,
    w_key,
    w_value,
    w_out,
    w_up,
    w_down,
    bias_table,
    gain_attn,
    gain_ffn,
    cotangent,
):
    rows, length, width = tokens.shape
    groups, bucket_count, heads = bias_table.shape
    pairs = heads // 2
    count = rows * length
    parts = 3
    part = pairs // parts

    up_state = net.gather(w_up.T, "z")
    down_y = net.gather(w_down, "y")
    (down_block,) = net.stage(
        lambda y, z, x, c, *p: [jnp.concatenate(in_order(p, y), axis=1)],
        down_y,
        [(w_down.shape[0], width)],
        "gather_y",
    )
    down_full = lax.all_gather(down_block, "an", axis=0, tiled=True)

    flat = tokens.reshape(count, width)
    x = flat.astype(F32)
    x_inv = lax.rsqrt(jnp.mean(x * x, axis=-1, keepdims=True) + epsilon)
    normed = (x * x_inv * gain_attn).astype(BF16)
    proj = project(normed, (w_query, w_key, w_value), parts)

    task_hot = (tasks[:, None] == jnp.arange(groups, dtype=jnp.int32)[None, :]).astype(F32)
    table_rows = jnp.einsum("rg,gbh->rbh", task_hot, bias_table, precision=highest)
    middle_offset = length - 1 + 3 * BLOCK
    near = buckets[middle_offset - WIDE + 1 : middle_offset + 1][::-1]
    bucket_hot = (near[None, :] == jnp.arange(bucket_count, dtype=jnp.int32)[:, None]).astype(F32)
    bias = jnp.einsum("rbh,bk->rhk", table_rows, bucket_hot, precision=highest)
    bias = bias.reshape(rows * pairs, 2, WIDE)
    seg = segments.reshape(count, 1)
    lane = jnp.arange(BLOCK, dtype=jnp.int32)[None, :]
    kseg = (lane == seg).astype(BF16)
    qseg = jnp.where((lane != seg) & (lane < 4), -1e30, 0.0).astype(BF16)

    saved = [None] * parts
    inverse = [None] * parts
    mixed = None

    def attend_part(i, proj, mixed):
        return attend(i, part * i, part, pairs, rows, length, proj, kseg, qseg, bias, mixed)

    up_state, proj = hold((up_state, proj))
    up_state = gather_1(net, up_state)
    saved[0], inverse[0], mixed = attend_part(0, proj, None)
    up_state, mixed, proj = hold((up_state, mixed, proj))
    up_state = gather_2(net, up_state)
    saved[1], inverse[1], mixed = attend_part(1, proj, mixed)
    saved[2], inverse[2], mixed = attend_part(2, proj, mixed)
    up_state, mixed = hold((up_state, mixed))
    up_own = gather_3(net, up_state)
    up_other = net.fetch(up_own, "c", 1)
    middle = x + dot(mixed, w_out)
    mid_inv = lax.rsqrt(jnp.mean(middle * middle, axis=-1, keepdims=True) + epsilon)
    second = (middle * mid_inv * gain_ffn).astype(BF16)

    g = cotangent.reshape(count, width)
    hidden, slope, gd_own, gd_other = ffn_up(net, up_own, up_other, second, g)
    gd_theirs = net.fetch(gd_other, "c", 1)
    gu_own, gu_other, grad_second = ffn_back(net, up_own, up_other, down_full, slope, second, g)
    gd_theirs, gu_other, grad_second = hold((gd_theirs, gu_other, grad_second))
    gu_theirs = net.fetch(gu_other, "c", 1)
    sd = scatter_1(net, gd_own, gd_theirs, "y")
    scaled = grad_second * gain_ffn
    mean = jnp.mean(scaled * middle, axis=-1, keepdims=True)
    grad_gain_ffn = jnp.sum(grad_second * (middle * mid_inv), axis=0)
    grad_middle = g.astype(F32) + mid_inv * scaled - middle * (mid_inv * mid_inv * mid_inv * mean)
    ga = grad_middle.astype(BF16)
    grad_mixed = dot(ga, w_out, CONTRACT_LANES).astype(BF16)
    gu_theirs, grad_mixed, ga = hold((gu_theirs, grad_mixed, ga))
    su = scatter_1(net, gu_own, gu_theirs, "x")

    def back_part(i, grad_mixed):
        return attend_grad(
            i, part * i, part, pairs, rows, length, proj, saved[i], inverse[i], mixed, grad_mixed
        )

    cols1 = width * parts
    dproj = [None] * parts
    doff = [None] * parts
    dproj[0], doff[0] = back_part(0, grad_mixed)
    r1 = weight_grad(net, mixed, ga, 0, cols1, None)
    r1 = weight_grad(net, normed, dproj[0], width, cols1, r1)
    sd, r1, grad_mixed = hold((sd, r1, grad_mixed))
    sd = scatter_2(net, sd, "x")
    dproj[1], doff[1] = back_part(1, grad_mixed)
    r1 = weight_grad(net, normed, dproj[1], 2 * width, cols1, r1)
    su, r1, grad_mixed = hold((su, r1, grad_mixed))
    r1_theirs = net.fetch(r1[1], "c", 1)
    su = scatter_2(net, su, "y")
    dproj[2], doff[2] = back_part(2, grad_mixed)
    sd, r1_theirs, dproj[2], doff[2] = hold((sd, r1_theirs, dproj[2], doff[2]))
    cut1 = cols1 // 2
    state1 = reduce_1(net, r1[0], r1_theirs, cut1)
    sd = scatter_3(net, sd)

    cols2 = width + BLOCK
    r2 = weight_grad(net, normed, dproj[2], 0, cols2, None)
    per_row = jnp.concatenate([d.reshape(part, rows, 2, WIDE) for d in doff], axis=0)
    per_row = per_row.transpose(1, 0, 2, 3).reshape(rows, heads, WIDE)
    grad_bucket = jnp.einsum("rhk,bk->rbh", per_row, bucket_hot, precision=highest)
    grad_table = jnp.einsum("rg,rbh->gbh", task_hot, grad_bucket, precision=highest)
    small = jnp.concatenate([grad_table.reshape(-1, width), grad_gain_ffn[None]], axis=0)
    table_cols = small.shape[0] - 1
    small = jnp.pad(small.T, ((0, 0), (0, BLOCK - small.shape[0]))).astype(BF16)
    c = net.places()[3]
    half = width // 2
    r2 = [
        lax.dynamic_update_slice(
            r, lax.dynamic_slice_in_dim(small, at * half, half, axis=0), (0, width)
        )
        for r, at in zip(r2, (c, 1 - c))
    ]
    r2_theirs = net.fetch(r2[1], "c", 1)
    su, state1, r2_theirs = hold((su, state1, r2_theirs))
    cut2 = width // 2
    state1 = reduce_2(net, state1)
    state2 = reduce_1(net, r2[0], r2_theirs, cut2)
    su = scatter_3(net, su)
    dproj, state1 = hold((dproj, state1))
    grad_tokens = token_grad(
        dproj, (w_query, w_key, w_value), flat, x_inv, gain_attn, grad_middle
    )
    state1, state2, hidden, grad_tokens = hold((state1, state2, hidden, grad_tokens))
    state1 = reduce_3(net, state1)
    state2 = reduce_2(net, state2)
    output = ffn_out(hidden, down_full, middle)
    state1, state2, output = hold((state1, state2, output))
    state2 = reduce_3(net, state2)
    cut = cut1 + cut2
    last = spread_0(net, [state1, state2], [cut1, cut2])
    last = spread_1(net, last, cut)
    last = spread_2(net, last)
    own, other = spread_3(net, last)

    def runs(first, stop):
        found = []
        for begin, end, at in (
            (0, cut1, 0),
            (cut1, cols1, cut),
            (cols1, cols1 + cut2, cut1),
            (cols1 + cut2, cols1 + cols2, cut + cols1 - cut1),
        ):
            a, b = max(first, begin), min(stop, end)
            if a < b:
                found.append((a - begin + at, b - begin + at))
        return found

    def head_runs(i):
        found = []
        for p in range(pairs):
            start = width + (3 * p + i) * BLOCK
            found += runs(start, start + BLOCK)
        return found

    everything = width + 3 * width
    grad_w_out, grad_query, grad_key, grad_value, small, grad_gain_attn = finish(
        net,
        own,
        other,
        [runs(0, width), head_runs(0), head_runs(1), head_runs(2)]
        + [runs(everything, everything + BLOCK)],
        (w_query, w_key, w_value),
        gain_attn,
    )
    small = small.T
    grad_table = small[:table_cols].reshape(groups, bucket_count, heads)
    grad_down = total(sd)
    grad_up = total(su).T
    return (
        output.reshape(rows, length, width),
        grad_tokens.reshape(rows, length, width),
        grad_query,
        grad_key,
        grad_value,
        grad_w_out,
        grad_up,
        grad_down,
        grad_table,
        grad_gain_attn.reshape(-1),
        small[table_cols],
    )


def solution(mesh):
    in_specs = (
        P(("ma", "an"), None, None),
        P(("ma", "an")),
        P(("ma", "an"), None),
        P(),
        P(),
        P(),
        P(),
        P(),
        P("ma", "an"),
        P("an", "ma"),
        P(),
        P(),
        P(),
        P(("ma", "an"), None, None),
    )
    out_specs = (
        P(("ma", "an"), None, None),
        P(("ma", "an"), None, None),
        P(),
        P(),
        P(),
        P(),
        P("ma", "an"),
        P("an", "ma"),
        P(),
        P(),
        P(),
    )

    def whole(*args):
        net = Links(mesh.shape["ma"], mesh.shape["an"], args[0].shape[-1])
        return local(net, *args)

    return jax.shard_map(whole, mesh=mesh, in_specs=in_specs, out_specs=out_specs, check_vma=False)
```

```python
import jax
import jax.numpy as jnp
from jax import lax
from jax.sharding import PartitionSpec as P
from jax.experimental import pallas as pl
from jax.experimental.pallas import tpu as pltpu

epsilon = 1e-06
highest = lax.Precision.HIGHEST
F32 = jnp.float32
BF16 = jnp.bfloat16
BLOCK = 128
REACH = 2
WIDE = 6 * BLOCK
CONTRACT_LANES = (((1,), (1,)), ((), ()))
CONTRACT_ROWS = (((0,), (0,)), ((), ()))
PLAIN = (((1,), (0,)), ((), ()))
hold = lax.optimization_barrier
brief = pl.CostEstimate(flops=1000, bytes_accessed=1000, transcendentals=0)


def far(x):
    return pltpu.with_memory_space_constraint(x, pltpu.HBM)


def dot(a, b, dims=PLAIN):
    return lax.dot_general(a, b, dims, preferred_element_type=F32)


def attend_body(p_ref, kseg_ref, qseg_ref, f_ref, *refs):
    u_ref, s_ref, o_ref, ot_ref = refs[-4:]
    length = p_ref.shape[0]
    blocks = length // BLOCK
    lane = lax.broadcasted_iota(jnp.int32, (length, BLOCK), 1)
    q_aug = jnp.concatenate([p_ref[:, :BLOCK] * BF16(0.125), qseg_ref[...]], axis=1)
    k = p_ref[:, BLOCK : 2 * BLOCK]
    v_t = p_ref[:, 2 * BLOCK :].astype(F32).T.astype(BF16)
    k_aug = [
        jnp.concatenate([jnp.where((lane >= 64) == (h == 1), k, BF16(0)), kseg_ref[...]], axis=1)
        for h in range(2)
    ]
    v_aug = [
        jnp.concatenate([v_t[64 * h : 64 * h + 64], jnp.ones((16, length), BF16)], axis=0)
        for h in range(2)
    ]
    tiles = [
        pltpu.roll(
            jnp.broadcast_to(f_ref[0, h : h + 1, :], (BLOCK, WIDE)), 0, 1, stride=1, stride_axis=0
        )
        for h in range(2)
    ]

    def score(h, s):
        return dot(k_aug[h], q_aug[256 * s : 256 * s + 256], CONTRACT_LANES)

    def weigh(h, s, st):
        for half in range(2):
            qb = 2 * s + half
            scored = {}
            peak = None
            for kb in range(blocks):
                o = kb - qb
                if abs(o) > REACH:
                    continue
                b = (
                    st[BLOCK * kb : BLOCK * kb + BLOCK, BLOCK * half : BLOCK * half + BLOCK]
                    + tiles[h][:, 384 - BLOCK * o : 512 - BLOCK * o]
                )
                scored[kb] = b
                peak = b if peak is None else jnp.maximum(peak, b)
            peak = jnp.max(peak, axis=0, keepdims=True)
            for kb in range(blocks):
                if kb in scored:
                    e = jnp.exp(scored[kb] - peak).astype(BF16)
                else:
                    e = jnp.zeros((BLOCK, BLOCK), BF16)
                u_ref[0, h, BLOCK * kb : BLOCK * kb + BLOCK, BLOCK * qb : BLOCK * qb + BLOCK] = e

    def mix(h, s):
        ot = dot(v_aug[h], u_ref[0, h, :, 256 * s : 256 * s + 256])
        r = 1.0 / ot[64:65]
        s_ref[0, h : h + 1, 256 * s : 256 * s + 256] = r
        return ot[:64] * r

    units = [(h, s) for h in range(2) for s in range(blocks // 2)]
    made = {}
    ahead = score(*units[0])
    for i, unit in enumerate(units):
        st = ahead
        if i + 1 < len(units):
            ahead = score(*units[i + 1])
        weigh(*unit, st)
        if i > 0:
            made[units[i - 1]] = mix(*units[i - 1])
    made[units[-1]] = mix(*units[-1])
    outs = [
        jnp.concatenate([made[h, s] for s in range(blocks // 2)], axis=1) for h in range(2)
    ]
    o_t = jnp.concatenate(outs, axis=0)
    o_ref[...] = o_t.T.astype(BF16)
    ot_ref[...] = o_t.astype(BF16)


def pair_spec(length, per_group, first):
    return pl.BlockSpec(
        (None, length, 3 * BLOCK),
        lambda p, r: ((first + p) // per_group, r, (first + p) % per_group),
    )


def attend(first, count, pairs, rows, length, proj, kseg, qseg, bias, made):
    steps = rows * pairs
    args = [far(proj), kseg, qseg, bias]
    specs = [
        pair_spec(length, pairs // proj.shape[0], first),
        pl.BlockSpec((length, BLOCK), lambda p, r: (r, 0)),
        pl.BlockSpec((length, BLOCK), lambda p, r: (r, 0)),
        pl.BlockSpec((1, 2, WIDE), lambda p, r: (r * pairs + first + p, 0, 0)),
    ]
    alias = {}
    if made is not None:
        alias = {len(args) + i: i for i in range(4)}
        args += [far(made[0]), made[1], made[2], made[3]]
        specs += [pl.BlockSpec(memory_space=pl.ANY)] * 4
    return pl.pallas_call(
        attend_body,
        grid=(count, rows),
        in_specs=specs,
        out_specs=[
            pl.BlockSpec((1, 2, length, length), lambda p, r: ((first + p) * rows + r, 0, 0, 0)),
            pl.BlockSpec((1, 2, length), lambda p, r: ((first + p) * rows + r, 0, 0)),
            pl.BlockSpec((length, BLOCK), lambda p, r: (r, first + p)),
            pl.BlockSpec((BLOCK, length), lambda p, r: (first + p, r)),
        ],
        out_shape=[
            pltpu.HBM((steps, 2, length, length), BF16),
            jax.ShapeDtypeStruct((steps, 2, length), F32),
            jax.ShapeDtypeStruct((rows * length, pairs * BLOCK), BF16),
            jax.ShapeDtypeStruct((pairs * BLOCK, rows * length), BF16),
        ],
        input_output_aliases=alias,
        compiler_params=pltpu.CompilerParams(vmem_limit_bytes=16 * 1024 * 1024),
        cost_estimate=brief,
        name="attend",
    )(*args)


def attend_grad_body(
    place_ref, p_ref, u_ref, s_ref, o_ref, g_ref, mine_ref, theirs_ref, *refs
):
    dp_ref, df_ref, go_ref, gx_ref, ds_ref, acc_ref = refs[-6:]
    length = p_ref.shape[0]
    blocks = length // BLOCK
    lane = lax.broadcasted_iota(jnp.int32, (length, BLOCK), 1)
    q = p_ref[:, :BLOCK] * BF16(0.125)
    k = p_ref[:, BLOCK : 2 * BLOCK]
    v = p_ref[:, 2 * BLOCK :]
    k_t = k.astype(F32).T.astype(BF16)
    inv = jnp.concatenate(
        [jnp.broadcast_to(s_ref[0, h : h + 1, :], (64, length)) for h in range(2)], axis=0
    ).T
    g = g_ref[...].astype(F32) * inv
    prod = g * o_ref[...].astype(F32)
    g_low = g.astype(BF16)
    prod_hi = prod.astype(BF16)
    prod_lo = (prod - prod_hi.astype(F32)).astype(BF16)
    row = lax.broadcasted_iota(jnp.int32, (2 * BLOCK, BLOCK), 0)
    col = lax.broadcasted_iota(jnp.int32, (2 * BLOCK, BLOCK), 1)
    pick = jnp.where((((row // 64) % 2) == (col // 2)) & (col < 4), -1.0, 0.0).astype(BF16)
    centre = dot(jnp.concatenate([prod_hi, prod_lo], axis=1), pick)
    centre_hi = centre.astype(BF16)
    centre_lo = (centre - centre_hi.astype(F32)).astype(BF16)
    g_aug = jnp.concatenate([g_low, jnp.where(lane % 2 == 0, centre_hi, centre_lo)], axis=1)
    zero = BF16(0)
    mine = [(lane >= 64) == (h == 1) for h in range(2)]
    v_aug = [
        jnp.concatenate(
            [jnp.where(mine[h], v, zero), jnp.where((lane // 2) == h, BF16(1), zero)], axis=1
        )
        for h in range(2)
    ]
    diag = [[None] * (2 * REACH + 1) for _ in range(2)]
    dq_t, dv, dk = [], [], []

    def score(h, s):
        return dot(v_aug[h], g_aug[256 * s : 256 * s + 256], CONTRACT_LANES)

    def weigh(h, s, dp):
        for half in range(2):
            qb = 2 * s + half
            for kb in range(blocks):
                o = kb - qb
                krows = slice(BLOCK * kb, BLOCK * kb + BLOCK)
                qcols = slice(BLOCK * qb, BLOCK * qb + BLOCK)
                if abs(o) > REACH:
                    ds_ref[h, krows, qcols] = jnp.zeros((BLOCK, BLOCK), BF16)
                    continue
                ds = (
                    u_ref[0, h, krows, qcols].astype(F32)
                    * dp[krows, BLOCK * half : BLOCK * half + BLOCK]
                )
                ds_ref[h, krows, qcols] = ds.astype(BF16)
                d = diag[h][o + REACH]
                diag[h][o + REACH] = ds if d is None else d + ds

    def back(h):
        dv.append(dot(u_ref[0, h], jnp.where(mine[h], g_low, zero)))
        dk.append(dot(ds_ref[h], jnp.where(mine[h], q, zero)))
        dq_t.append(dot(k_t[64 * h : 64 * h + 64], ds_ref[h]))
        wide = jnp.concatenate([jnp.zeros((BLOCK, BLOCK), F32)] + diag[h][::-1], axis=1)
        step = BLOCK // 2
        while step:
            wide = wide[:step] + pltpu.roll(wide[step:], WIDE - step, 1)
            step //= 2
        df_ref[0, h : h + 1, :] = wide

    units = [(h, s) for h in range(2) for s in range(blocks // 2)]
    ahead = score(*units[0])
    for i, unit in enumerate(units):
        dp = ahead
        if i + 1 < len(units):
            ahead = score(*units[i + 1])
        weigh(*unit, dp)
        if i + 1 < len(units) and units[i + 1][0] != unit[0] and i > 0:
            back(unit[0])
    back(units[-1][0])
    dv = dv[0] + dv[1]
    dk = dk[0] + dk[1]
    dq = jnp.concatenate(dq_t, axis=0).T * 0.125
    d_all = jnp.concatenate([dq.astype(BF16), dk.astype(BF16), dv.astype(BF16)], axis=1)
    dp_ref[...] = d_all
    half = mine_ref.shape[0]
    row_step = pl.program_id(1)
    add = dot(jnp.concatenate([mine_ref[...], theirs_ref[...]], axis=0), d_all)

    @pl.when(row_step == 0)
    def _():
        acc_ref[...] = add

    @pl.when(row_step != 0)
    def _():
        acc_ref[...] += add

    @pl.when(row_step == pl.num_programs(1) - 1)
    def _():
        go_ref[...] = acc_ref[:half].astype(BF16)
        gx_ref[...] = acc_ref[half:].astype(BF16)


def attend_grad(
    net, first, count, pairs, rows, length, proj, made, grad_mixed, normed_t, cols, buffers, at
):
    saved, inverse, mixed, _ = made
    steps = rows * count
    half = normed_t.shape[0] // 2
    wide = 3 * BLOCK
    args = [far(proj), far(saved), inverse, mixed, grad_mixed, far(normed_t), far(normed_t)]
    specs = [
        pl.BlockSpec(
            (None, length, wide),
            lambda p, r, w, per=pairs // proj.shape[0]: ((first + p) // per, r, (first + p) % per),
        ),
        pl.BlockSpec((1, 2, length, length), lambda p, r, w: ((first + p) * rows + r, 0, 0, 0)),
        pl.BlockSpec((1, 2, length), lambda p, r, w: ((first + p) * rows + r, 0, 0)),
        pl.BlockSpec((length, BLOCK), lambda p, r, w: (r, first + p)),
        pl.BlockSpec((length, BLOCK), lambda p, r, w: (r, first + p)),
        pl.BlockSpec((half, length), lambda p, r, w: (w[3], r)),
        pl.BlockSpec((half, length), lambda p, r, w: (1 - w[3], r)),
    ]
    alias = {}
    if buffers is not None:
        alias = {1 + len(args) + i: 2 + i for i in range(2)}
        args += [far(b) for b in buffers]
        specs += [pl.BlockSpec(memory_space=pl.ANY)] * 2
    g_spec = pl.BlockSpec((half, wide), lambda p, r, w: (0, at // wide + p))
    return pl.pallas_call(
        attend_grad_body,
        grid_spec=pltpu.PrefetchScalarGridSpec(
            num_scalar_prefetch=1,
            grid=(count, rows),
            in_specs=specs,
            out_specs=[
                pl.BlockSpec((length, wide), lambda p, r, w: (r, p)),
                pl.BlockSpec((1, 2, WIDE), lambda p, r, w: (p * rows + r, 0, 0)),
                g_spec,
                g_spec,
            ],
            scratch_shapes=[
                pltpu.VMEM((2, length, length), BF16),
                pltpu.VMEM((2 * half, wide), F32),
            ],
        ),
        out_shape=[
            pltpu.HBM((rows * length, count * wide), BF16),
            jax.ShapeDtypeStruct((steps, 2, WIDE), F32),
            pltpu.HBM((half, cols), BF16),
            pltpu.HBM((half, cols), BF16),
        ],
        input_output_aliases=alias,
        compiler_params=pltpu.CompilerParams(vmem_limit_bytes=24 * 1024 * 1024),
        cost_estimate=brief,
        name="attend_grad",
    )(net.places(), *args)


def pick(options, index):
    out = options[0]
    for k in range(1, len(options)):
        out = jnp.where(index == k, options[k], out)
    return out


def by_distance(slices, at):
    n = len(slices)
    return [pick(slices, lax.rem(at - t + n, n)) for t in range(n)]


def in_order(pieces, at):
    n = len(pieces)
    return [pick(pieces, lax.rem(at - k + n, n)) for k in range(n)]


def cut_rows(v, n):
    size = v.shape[0] // n
    return [v[size * k : size * k + size] for k in range(n)]


def cut_lanes(v, n):
    size = v.shape[-1] // n
    return [v[..., size * k : size * k + size] for k in range(n)]


def total(parts):
    out = parts[0].astype(F32)
    for p in parts[1:]:
        out = out + p.astype(F32)
    return out


class Links:
    def __init__(self, ma, an, width):
        z = min(4, an // 2)
        self.an = an
        self.size = {"y": ma, "z": z, "x": an // (2 * z), "c": 2}
        self.stride = {"c": 1, "x": 2, "z": 2 * self.size["x"]}
        self.tidy = width % (ma * BLOCK) == 0 and width % (8 * ma * an) == 0

    def places(self):
        an = lax.axis_index("an")
        found = [lax.axis_index("ma")]
        found += [(an // self.stride[a]) % self.size[a] for a in ("z", "x", "c")]
        return jnp.stack([f.astype(jnp.int32) for f in found])

    def fetch(self, value, axis, back):
        n = self.size[axis]
        if axis == "y":
            return lax.ppermute(value, "ma", [(i, (i + back) % n) for i in range(n)])
        s = self.stride[axis]
        pairs = []
        for i in range(self.an):
            at = (i // s) % n
            pairs.append((i, i + ((at + back) % n - at) * s))
        return lax.ppermute(value, "an", pairs)

    def gather(self, value, axis):
        return [value] + [self.fetch(value, axis, t) for t in range(1, self.size[axis])]

    def spread(self, parts, axis):
        n = self.size[axis]
        return [parts[0]] + [self.fetch(parts[t], axis, n - t) for t in range(1, n)]

    def step(self, fn, arrays, shapes, name, along, steps=1, away=False):
        arrays, along = hold((list(arrays), along))
        return hold((self.stage(fn, arrays, shapes, name, steps, away), along))

    def stage(self, fn, arrays, shapes, name, steps, away):
        outs = [jax.ShapeDtypeStruct(s, BF16) for s in shapes]
        place = self.places()
        if not self.tidy:
            got = fn(*[place[i] for i in range(4)], *arrays)
            return [g.astype(BF16).reshape(o.shape) for g, o in zip(got, outs)]
        count = len(arrays)

        def body(place_ref, *refs):
            got = fn(*[place_ref[i] for i in range(4)], *[r[...] for r in refs[:count]])
            for g, r in zip(got, refs[count:]):
                r[...] = g.astype(BF16)

        def spec(a):
            rest = len(a.shape) - 1
            return pl.BlockSpec(
                (a.shape[0] // steps,) + a.shape[1:], lambda i, p, rest=rest: (i,) + (0,) * rest
            )

        return pl.pallas_call(
            body,
            grid_spec=pltpu.PrefetchScalarGridSpec(
                num_scalar_prefetch=1,
                grid=(steps,),
                in_specs=[spec(a) for a in arrays],
                out_specs=[spec(o) for o in outs],
            ),
            out_shape=[pltpu.HBM(o.shape, o.dtype) for o in outs] if away else outs,
            compiler_params=pltpu.CompilerParams(vmem_limit_bytes=16 * 1024 * 1024),
            cost_estimate=brief,
            name=name,
        )(place, *arrays)


def gather_1(net, pieces, along):
    rows, cols = pieces[0].shape
    half = rows // 2
    n = len(pieces)

    def fn(y, z, x, c, *pieces):
        v = jnp.stack(in_order(pieces, z))
        return [v[:, :half], v[:, half:]]

    (a, b), along = net.step(fn, pieces, [(n, half, cols)] * 2, "gather_z", along)
    return (net.gather(a, "x"), net.gather(b, "y")), along


def gather_2(net, state, along):
    a, b = state
    n, half, cols = a[0].shape

    def fn(y, z, x, c, *parts):
        a_in = in_order(parts[: len(a)], x)
        b_in = in_order(parts[len(a) :], y)
        return [jnp.stack(a_in, axis=1), jnp.concatenate(b_in, axis=-1)]

    (a, b), along = net.step(
        fn, a + b, [(n, len(a), half, cols), (n, half, cols * len(b))], "gather_xy", along
    )
    return (net.gather(a, "y"), net.gather(b, "x")), along


def gather_3(net, state, along):
    a, b = state
    n, nx, half, cols = a[0].shape

    def fn(y, z, x, c, *parts):
        a_in = jnp.concatenate(in_order(parts[: len(a)], y), axis=-1)
        b_in = jnp.stack(in_order(parts[len(a) :], x), axis=1)
        return [jnp.concatenate([a_in, b_in], axis=2)]

    shape = (n, nx, 2 * half, cols * len(a))
    (own,), along = net.step(fn, a + b, [shape], "gather_yx", along, steps=n if net.tidy else 1)
    return net.gather(own, "c"), along


def scatter_1(net, own, theirs, along):
    nz, two, nx, hb, width = own.shape
    half = hb // 2
    ny = net.size["y"]

    def fn(y, z, x, c, own, theirs):
        v = total([own, theirs])
        a, b = v[..., :half, :], v[..., half:, :]
        return by_distance(cut_lanes(a, ny), y) + by_distance([b[:, :, k] for k in range(nx)], x)

    shapes = [(nz, two, nx, half, width // ny)] * ny + [(nz, two, half, width)] * nx
    parts, along = net.step(
        fn, [own, theirs], shapes, "scatter_yx", along, steps=nz if net.tidy else 1
    )
    return (net.spread(parts[:ny], "y"), net.spread(parts[ny:], "x")), along


def scatter_2(net, state, along):
    a, b = state
    nz, two, nx, half, cols = a[0].shape
    ny = net.size["y"]

    def fn(y, z, x, c, *parts):
        va, vb = total(parts[:ny]), total(parts[ny:])
        return by_distance([va[:, :, k] for k in range(nx)], x) + by_distance(cut_lanes(vb, ny), y)

    shapes = [(nz, two, half, cols)] * (nx + ny)
    parts, along = net.step(fn, a + b, shapes, "scatter_xy", along)
    return (net.spread(parts[:nx], "x"), net.spread(parts[nx:], "y")), along


def scatter_3(net, state, along):
    a, b = state
    nz, two, half, cols = a[0].shape

    def fn(y, z, x, c, *parts):
        v = jnp.concatenate([total(parts[: len(a)]), total(parts[len(a) :])], axis=2)
        return by_distance([v[k] for k in range(nz)], z)

    parts, along = net.step(fn, a + b, [(two, 2 * half, cols)] * nz, "scatter_z", along)
    return net.spread(parts, "z"), along


def reduce_1(net, own, theirs, cut, along, away):
    rows, cols = own.shape
    ny, nx = net.size["y"], net.size["x"]

    def fn(y, z, x, c, own, theirs):
        v = total([own, theirs])
        return by_distance(cut_rows(v[:, :cut], ny), y) + by_distance(cut_rows(v[:, cut:], nx), x)

    shapes = [(rows // ny, cut)] * ny + [(rows // nx, cols - cut)] * nx
    parts, along = net.step(fn, [own, theirs], shapes, "reduce_yx", along, away=away)
    return (net.spread(parts[:ny], "y"), net.spread(parts[ny:], "x")), along


def reduce_2(net, state, along, away):
    a, b = state
    ny, nx = net.size["y"], net.size["x"]

    def fn(y, z, x, c, *parts):
        va, vb = total(parts[: len(a)]), total(parts[len(a) :])
        return by_distance(cut_rows(va, nx), x) + by_distance(cut_rows(vb, ny), y)

    shapes = [(a[0].shape[0] // nx, a[0].shape[1])] * nx
    shapes += [(b[0].shape[0] // ny, b[0].shape[1])] * ny
    parts, along = net.step(fn, a + b, shapes, "reduce_xy", along, away=away)
    return (net.spread(parts[:nx], "x"), net.spread(parts[nx:], "y")), along


def reduce_3(net, state, along):
    a, b = state
    n = net.size["z"]

    def fn(y, z, x, c, *parts):
        v = jnp.concatenate([total(parts[: len(a)]), total(parts[len(a) :])], axis=1)
        return by_distance(cut_rows(v, n), z)

    shape = (a[0].shape[0] // n, a[0].shape[1] + b[0].shape[1])
    parts, along = net.step(fn, a + b, [shape] * n, "reduce_z", along)
    return net.spread(parts, "z"), along


def spread_0(net, payloads, cuts, along):
    counts = [len(p) for p in payloads]
    rows = payloads[0][0].shape[0]
    cols = sum(p[0].shape[1] for p in payloads)

    def fn(y, z, x, c, *parts):
        sums = []
        for n in counts:
            sums.append(total(parts[:n]))
            parts = parts[n:]
        return [
            jnp.concatenate(
                [v[:, :k] for v, k in zip(sums, cuts)] + [v[:, k:] for v, k in zip(sums, cuts)],
                axis=1,
            )
        ]

    pieces = [p for ps in payloads for p in ps]
    (front,), along = net.step(fn, pieces, [(rows, cols)], "spread_sum", along)
    return net.gather(front, "z"), along


def spread_1(net, pieces, cut, along):
    rows, cols = pieces[0].shape
    n = len(pieces)

    def fn(y, z, x, c, *pieces):
        v = jnp.concatenate([p.astype(F32) for p in in_order(pieces, z)], axis=0)
        return [v[:, :cut], v[:, cut:]]

    shapes = [(n * rows, cut), (n * rows, cols - cut)]
    (a, b), along = net.step(fn, pieces, shapes, "spread_z", along)
    return (net.gather(a, "x"), net.gather(b, "y")), along


def spread_2(net, state, along):
    a, b = state

    def fn(y, z, x, c, *parts):
        va = jnp.concatenate(in_order(parts[: len(a)], x), axis=0)
        vb = jnp.concatenate(in_order(parts[len(a) :], y), axis=0)
        return [va, vb]

    shapes = [(len(p) * p[0].shape[0], p[0].shape[1]) for p in (a, b)]
    (a, b), along = net.step(fn, a + b, shapes, "spread_xy", along)
    return (net.gather(a, "y"), net.gather(b, "x")), along


def spread_3(net, state, along):
    a, b = state

    def fn(y, z, x, c, *parts):
        va = jnp.concatenate(in_order(parts[: len(a)], y), axis=0)
        vb = jnp.concatenate(in_order(parts[len(a) :], x), axis=0)
        return [jnp.concatenate([va, vb], axis=1)]

    shape = (len(a) * a[0].shape[0], a[0].shape[1] + b[0].shape[1])
    (v,), along = net.step(fn, a + b, [shape], "spread_yx", along)
    return net.gather(v, "c"), along


def finish(net, own, other, cuts, weights, gain, sizes, heads_from, into):
    half, cols = own.shape
    tile = BLOCK
    steps = half // tile
    live = [k for k, runs in enumerate(cuts) if runs]
    widths = [sum(b - a for a, b in cuts[k]) for k in live]

    def body(place_ref, own_ref, other_ref, wq_ref, wk_ref, wv_ref, gain_ref, *refs):
        outs = refs[-len(live) - 1 :]
        mine = (pl.program_id(0) // steps) == place_ref[3]
        v = jnp.where(mine, own_ref[...].astype(F32), other_ref[...].astype(F32))
        made = [jnp.concatenate([v[:, a:b] for a, b in cuts[k]], axis=1) for k in live]
        for out, m in zip(outs, made):
            out[...] = m
        acc = made[0] * wq_ref[...].astype(F32)
        acc = acc + made[1] * wk_ref[...].astype(F32) + made[2] * wv_ref[...].astype(F32)
        part = jnp.sum(acc, axis=1, keepdims=True) / gain_ref[...]
        outs[-1][...] = part if into is None else part + refs[0][...]

    def cols_spec(w, at):
        return pl.BlockSpec((tile, w), lambda i, p: (i, at // w))

    at = [heads_from if k < 3 else 0 for k in live]
    one = pl.BlockSpec((tile, 1), lambda i, p: (i, 0))
    args = [own, other, *[far(w) for w in weights], gain.reshape(-1, 1)]
    specs = [pl.BlockSpec((tile, cols), lambda i, p: (i % steps, 0))] * 2
    specs += [cols_spec(widths[0], heads_from)] * 3 + [one]
    alias = {}
    if into is not None:
        args += [into[1], *[far(a) for a in into[0]]]
        specs += [one] + [pl.BlockSpec(memory_space=pl.ANY)] * 3
        alias = {len(args) - 3 + 1 + k: k for k in range(3)}
    return pl.pallas_call(
        body,
        grid_spec=pltpu.PrefetchScalarGridSpec(
            num_scalar_prefetch=1,
            grid=(2 * steps,),
            in_specs=specs,
            out_specs=[cols_spec(w, a) for w, a in zip(widths, at)] + [one],
        ),
        out_shape=[pltpu.HBM((2 * half, sizes[k]), F32) for k in live]
        + [jax.ShapeDtypeStruct((2 * half, 1), F32)],
        input_output_aliases=alias,
        compiler_params=pltpu.CompilerParams(vmem_limit_bytes=20 * 1024 * 1024),
        cost_estimate=brief,
        name="finish",
    )(net.places(), *args)


def project(tokens, gain, weights, groups):
    count, width = tokens.shape
    tile = min(256, count)
    pairs_here = width // BLOCK // groups

    def body(t_ref, gain_ref, *refs):
        out, nt_ref = refs[-2:]
        x = t_ref[...].astype(F32)
        inv = lax.rsqrt(jnp.mean(x * x, axis=1, keepdims=True) + epsilon)
        normed = x * inv * gain_ref[...]
        low = normed.astype(BF16)
        nt_ref[...] = normed.T.astype(BF16)
        for i, w in enumerate(refs[:-2]):
            r = dot(low, w[...]).astype(BF16)
            for p in range(groups * pairs_here):
                at = (3 * (p % pairs_here) + i) * BLOCK
                out[p // pairs_here, :, at : at + BLOCK] = r[:, BLOCK * p : BLOCK * p + BLOCK]

    return pl.pallas_call(
        body,
        grid=(count // tile,),
        in_specs=[
            pl.BlockSpec((tile, width), lambda i: (i, 0)),
            pl.BlockSpec((1, width), lambda i: (0, 0)),
        ]
        + [pl.BlockSpec((width, width), lambda i: (0, 0))] * 3,
        out_specs=[
            pl.BlockSpec((groups, tile, 3 * width // groups), lambda i: (0, i, 0)),
            pl.BlockSpec((width, tile), lambda i: (0, i)),
        ],
        out_shape=[
            pltpu.HBM((groups, count, 3 * width // groups), BF16),
            pltpu.HBM((width, count), BF16),
        ],
        compiler_params=pltpu.CompilerParams(vmem_limit_bytes=24 * 1024 * 1024),
        cost_estimate=brief,
        name="project",
    )(far(tokens), gain.reshape(1, -1), *[far(w) for w in weights])


def gelu_parts(pre):
    k0 = 0.7978845608028654
    k1 = 0.044715
    sq = pre * pre
    s = 0.5 * jnp.tanh(pre * (k0 + (k0 * k1) * sq)) + 0.5
    act = pre * s
    slope = s + (act - act * s) * (2.0 * k0 + (6.0 * k0 * k1) * sq)
    return act, slope


def before_ffn(mixed, w_out, tokens, gain, g):
    count, width = mixed.shape
    tile = min(256, count)

    def body(mixed_ref, w_ref, t_ref, gain_ref, g_ref, mid_ref, s_ref, st_ref, gt_ref):
        mid = t_ref[...].astype(F32) + dot(mixed_ref[...], w_ref[...])
        inv = lax.rsqrt(jnp.mean(mid * mid, axis=1, keepdims=True) + epsilon)
        second = mid * inv * gain_ref[...]
        mid_ref[...] = mid
        s_ref[...] = second.astype(BF16)
        st_ref[...] = second.T.astype(BF16)
        gt_ref[...] = g_ref[...].astype(F32).T.astype(BF16)

    def rows_of(w):
        return pl.BlockSpec((tile, w), lambda i: (i, 0))

    cols = pl.BlockSpec((width, tile), lambda i: (0, i))
    return pl.pallas_call(
        body,
        grid=(count // tile,),
        in_specs=[
            rows_of(width),
            pl.BlockSpec((width, width), lambda i: (0, 0)),
            rows_of(width),
            pl.BlockSpec((1, width), lambda i: (0, 0)),
            rows_of(width),
        ],
        out_specs=[rows_of(width), rows_of(width), cols, cols],
        out_shape=[
            pltpu.HBM((count, width), F32),
            pltpu.HBM((count, width), BF16),
            pltpu.HBM((width, count), BF16),
            pltpu.HBM((width, count), BF16),
        ],
        compiler_params=pltpu.CompilerParams(vmem_limit_bytes=20 * 1024 * 1024),
        cost_estimate=brief,
        name="before_ffn",
    )(mixed, far(w_out), far(tokens), gain.reshape(1, -1), far(g))


def ffn(net, ups, downs, second, second_t, g, g_t, middle):
    nz, nx, hb, width = ups[0].shape
    count = g.shape[0]
    part = nx * hb
    tile = 256 if count % 256 == 0 else count
    lanes = 256 if width % 256 == 0 else width

    def body(
        place_ref, u0_ref, u1_ref, d0_ref, d1_ref, st_far, gt_far, g_far, s_far, m_far,
        out_ref, go_ref, gx_ref, gs_ref, act_ref, gu_ref, acc_ref,
        st_ref, gt_ref, g_ref, s_ref, m_ref, sems,
    ):
        step = pl.program_id(0)
        st_copy, gt_copy, g_copy, s_copy, m_copy = [
            pltpu.make_async_copy(a, b, sems.at[i])
            for i, (a, b) in enumerate(
                (
                    (st_far, st_ref),
                    (gt_far, gt_ref),
                    (g_far, g_ref),
                    (s_far, s_ref),
                    (m_far, m_ref),
                )
            )
        ]

        @pl.when(step == 0)
        def _():
            for copy in (st_copy, gt_copy, g_copy, s_copy, m_copy):
                copy.start()
            st_copy.wait()
            gt_copy.wait()

        up_all, down_all = [
            jnp.concatenate([r[...].reshape(part, width) for r in refs], axis=0)
            for refs in ((u0_ref, u1_ref), (d0_ref, d1_ref))
        ]
        starts = list(range(0, count, tile))

        def both(t):
            return dot(up_all, st_ref[:, t : t + tile]), dot(down_all, gt_ref[:, t : t + tile])

        @pl.when(step == 0)
        def _():
            acc_ref[...] = jnp.zeros_like(acc_ref)
            gs_ref[...] = jnp.zeros_like(gs_ref)

        def sums(t):
            at = slice(t, t + tile)
            acc_ref[at] += dot(act_ref[:, at], down_all, CONTRACT_ROWS)
            gs_ref[at] += dot(gu_ref[:, at], up_all, CONTRACT_ROWS)

        ahead = both(starts[0])
        for n, t in enumerate(starts):
            pre, gh = ahead
            if n + 1 < len(starts):
                ahead = both(starts[n + 1])
            act, slope = gelu_parts(pre)
            act_ref[:, t : t + tile] = act.astype(BF16)
            gu_ref[:, t : t + tile] = (gh * slope).astype(BF16)
            if n > 0:
                sums(starts[n - 1])
        sums(starts[-1])

        @pl.when(step == 0)
        def _():
            g_copy.wait()
            s_copy.wait()

        for k in range(0, width, lanes):
            cols = slice(k, k + lanes)
            gd = dot(act_ref[...], g_ref[:, cols]).astype(BF16)
            gu = dot(gu_ref[...], s_ref[:, cols]).astype(BF16)
            for rel in range(2):
                for i in range(nx):
                    at = part * rel + hb * i
                    out = (go_ref, gx_ref)[rel]
                    out[0, i, :, cols] = gd[at : at + hb]
                    out[1, i, :, cols] = gu[at : at + hb]

        @pl.when(step == nz - 1)
        def _():
            m_copy.wait()
            out_ref[...] = (m_ref[...] + acc_ref[...]).astype(BF16)

    away = pl.BlockSpec(memory_space=pltpu.HBM)

    one = pl.BlockSpec((None, nx, hb, width), lambda i, p: (i, 0, 0, 0))
    two = pl.BlockSpec((None, 2, nx, hb, width), lambda i, p: (i, 0, 0, 0, 0))
    flat = pl.BlockSpec((count, width), lambda i, p: (0, 0))
    return pl.pallas_call(
        body,
        grid_spec=pltpu.PrefetchScalarGridSpec(
            num_scalar_prefetch=1,
            grid=(nz,),
            in_specs=[one] * 4 + [away] * 5,
            out_specs=[flat, two, two, flat],
            scratch_shapes=[
                pltpu.VMEM((2 * part, count), BF16),
                pltpu.VMEM((2 * part, count), BF16),
                pltpu.VMEM((count, width), F32),
                pltpu.VMEM((width, count), BF16),
                pltpu.VMEM((width, count), BF16),
                pltpu.VMEM((count, width), BF16),
                pltpu.VMEM((count, width), BF16),
                pltpu.VMEM((count, width), F32),
                pltpu.SemaphoreType.DMA((5,)),
            ],
        ),
        out_shape=[
            pltpu.HBM((count, width), BF16),
            pltpu.HBM((nz, 2, nx, hb, width), BF16),
            pltpu.HBM((nz, 2, nx, hb, width), BF16),
            pltpu.HBM((count, width), F32),
        ],
        compiler_params=pltpu.CompilerParams(vmem_limit_bytes=48 * 1024 * 1024),
        cost_estimate=brief,
        name="ffn",
    )(net.places(), *[far(v) for v in (*ups, *downs, second_t, g_t, g, second, middle)])


def after_ffn(net, grad_second, middle, gain, g, w_out, mixed_t, cols):
    count, width = middle.shape
    half = width // 2
    tile = min(256, count)

    def body(
        place_ref, gs_ref, m_ref, gain_ref, g_ref, w_ref, mine_ref, theirs_ref,
        gm_ref, gx_ref, gg_ref, wo_ref, wx_ref, acc_ref,
    ):
        gs = gs_ref[...]
        m = m_ref[...]
        r = lax.rsqrt(jnp.mean(m * m, axis=1, keepdims=True) + epsilon)
        scaled = gs * gain_ref[...]
        mean = jnp.mean(scaled * m, axis=1, keepdims=True)
        gm = g_ref[...].astype(F32) + r * scaled - m * (r * r * r * mean)
        ga = gm.astype(BF16)
        gm_ref[...] = gm
        gx_ref[...] = dot(ga, w_ref[...], CONTRACT_LANES).astype(BF16)
        add = jnp.sum(gs * (m * r), axis=0, keepdims=True)
        step = pl.program_id(0)

        @pl.when(step == 0)
        def _():
            gg_ref[...] = add

        @pl.when(step != 0)
        def _():
            gg_ref[...] += add

        for k, (left, out) in enumerate(((mine_ref, wo_ref), (theirs_ref, wx_ref))):
            rows = slice(half * k, half * k + half)
            more = dot(left[...], ga)

            @pl.when(step == 0)
            def _():
                acc_ref[rows] = more

            @pl.when(step != 0)
            def _():
                acc_ref[rows] += more

            @pl.when(step == pl.num_programs(0) - 1)
            def _():
                out[...] = acc_ref[rows].astype(BF16)

    def rows_of(w):
        return pl.BlockSpec((tile, w), lambda i, p: (i, 0))

    row = pl.BlockSpec((1, width), lambda i, p: (0, 0))
    grad = pl.BlockSpec((half, width), lambda i, p: (0, 0))
    return pl.pallas_call(
        body,
        grid_spec=pltpu.PrefetchScalarGridSpec(
            num_scalar_prefetch=1,
            grid=(count // tile,),
            in_specs=[
                rows_of(width),
                rows_of(width),
                row,
                rows_of(width),
                pl.BlockSpec((width, width), lambda i, p: (0, 0)),
                pl.BlockSpec((half, tile), lambda i, p: (p[3], i)),
                pl.BlockSpec((half, tile), lambda i, p: (1 - p[3], i)),
            ],
            out_specs=[rows_of(width), rows_of(width), row, grad, grad],
            scratch_shapes=[pltpu.VMEM((width, width), F32)],
        ),
        out_shape=[
            pltpu.HBM((count, width), F32),
            jax.ShapeDtypeStruct((count, width), BF16),
            jax.ShapeDtypeStruct((1, width), F32),
            pltpu.HBM((half, cols), BF16),
            pltpu.HBM((half, cols), BF16),
        ],
        compiler_params=pltpu.CompilerParams(vmem_limit_bytes=24 * 1024 * 1024),
        cost_estimate=brief,
        name="after_ffn",
    )(net.places(), far(grad_second), far(middle), gain.reshape(1, -1), far(g), far(w_out), mixed_t, mixed_t)


def token_grad(dproj, weights, tokens, gain, grad_middle):
    count, width = tokens.shape
    tile = min(256, count)

    def body(*refs):
        d_refs = refs[: len(dproj)]
        w_refs = refs[len(dproj) : len(dproj) + 3]
        t_ref, gain_ref, gm_ref, out_ref = refs[len(dproj) + 3 :]
        gn = None
        for i, w in enumerate(w_refs):
            cols = []
            for d in d_refs:
                for p in range(d.shape[1] // (3 * BLOCK)):
                    at = (3 * p + i) * BLOCK
                    cols.append(d[:, at : at + BLOCK])
            r = dot(jnp.concatenate(cols, axis=1), w[...], CONTRACT_LANES)
            gn = r if gn is None else gn + r
        scaled = gn * gain_ref[...]
        x = t_ref[...].astype(F32)
        r = lax.rsqrt(jnp.mean(x * x, axis=1, keepdims=True) + epsilon)
        mean = jnp.mean(scaled * x, axis=1, keepdims=True)
        out_ref[...] = gm_ref[...] + r * scaled - x * (r * r * r * mean)

    def rows_of(w):
        return pl.BlockSpec((tile, w), lambda i: (i, 0))

    return pl.pallas_call(
        body,
        grid=(count // tile,),
        in_specs=[rows_of(d.shape[1]) for d in dproj]
        + [pl.BlockSpec(w.shape, lambda i: (0, 0)) for w in weights]
        + [rows_of(width), pl.BlockSpec((1, width), lambda i: (0, 0)), rows_of(width)],
        out_specs=rows_of(width),
        out_shape=pltpu.HBM((count, width), F32),
        compiler_params=pltpu.CompilerParams(vmem_limit_bytes=20 * 1024 * 1024),
        cost_estimate=brief,
        name="token_grad",
    )(*[far(d) for d in dproj], *[far(w) for w in weights], far(tokens), gain.reshape(1, -1), far(grad_middle))


def local(
    net,
    tokens,
    tasks,
    segments,
    buckets,
    w_query,
    w_key,
    w_value,
    w_out,
    w_up,
    w_down,
    bias_table,
    gain_attn,
    gain_ffn,
    cotangent,
):
    rows, length, width = tokens.shape
    groups, bucket_count, heads = bias_table.shape
    pairs = heads // 2
    count = rows * length
    parts = 3
    part = pairs // parts

    up_state = net.gather(w_up.T, "z")
    flat = tokens.reshape(count, width)
    proj, normed_t = project(flat, gain_attn, (w_query, w_key, w_value), parts)

    task_hot = (tasks[:, None] == jnp.arange(groups, dtype=jnp.int32)[None, :]).astype(F32)
    table_rows = jnp.einsum("rg,gbh->rbh", task_hot, bias_table, precision=highest)
    middle_offset = length - 1 + 3 * BLOCK
    near = buckets[middle_offset - WIDE + 1 : middle_offset + 1][::-1]
    bucket_hot = (near[None, :] == jnp.arange(bucket_count, dtype=jnp.int32)[:, None]).astype(F32)
    bias = jnp.einsum("rbh,bk->rhk", table_rows, bucket_hot, precision=highest)
    bias = bias.reshape(rows * pairs, 2, WIDE)
    seg = segments.reshape(count, 1)
    lane = jnp.arange(BLOCK, dtype=jnp.int32)[None, :]
    kseg = (lane == seg).astype(BF16)
    qseg = jnp.where((lane != seg) & (lane < 4), -1e30, 0.0).astype(BF16)

    def attend_part(first, pairs_here, proj, made):
        return attend(first, pairs_here, pairs, rows, length, proj, kseg, qseg, bias, made)

    up_state, (proj, w_down) = gather_1(net, up_state, (proj, w_down))
    down_state = net.gather(w_down, "z")
    made = attend_part(0, part, proj, None)
    up_state, (made, proj) = gather_2(net, up_state, (made, proj))
    made = attend_part(part, part, proj, made)
    down_state, (made, proj) = gather_1(net, down_state, (made, proj))
    made = attend_part(2 * part, pairs - 2 * part, proj, made)
    ups, made = gather_3(net, up_state, made)
    down_state, made = gather_2(net, down_state, made)
    mixed, mixed_t = made[2:]
    g = cotangent.reshape(count, width)
    middle, second, second_t, g_t = before_ffn(mixed, w_out, flat, gain_ffn, g)
    downs, second = gather_3(net, down_state, second)

    ups, downs, second = hold((ups, downs, second))
    output, gf_own, gf_other, grad_second = ffn(
        net, ups, downs, second, second_t, g, g_t, middle
    )
    gf_other, grad_second = hold((gf_other, grad_second))
    gf_theirs = net.fetch(gf_other, "c", 1)
    cols1 = width * parts
    cols2 = width + BLOCK
    cut1 = cols1 // 2
    cut2 = width // 2
    grad_middle, grad_mixed, grad_gain_ffn, *r1 = after_ffn(
        net, grad_second, middle, gain_ffn, g, w_out, mixed_t, cols1
    )
    sf, grad_mixed = scatter_1(net, gf_own, gf_theirs, grad_mixed)

    def back_part(i, grad_mixed, cols, buffers, at):
        d, off, *r = attend_grad(
            net, part * i, part, pairs, rows, length, proj, made, grad_mixed, normed_t, cols, buffers, at
        )
        return d, off, r

    dproj = [None] * parts
    doff = [None] * parts
    dproj[0], doff[0], r1 = back_part(0, grad_mixed, cols1, r1, width)
    dproj[1], doff[1], r1 = back_part(1, grad_mixed, cols1, r1, 2 * width)
    grad_mixed, r1, sf = hold((grad_mixed, r1, sf))
    r1_theirs = net.fetch(r1[1], "c", 1)
    sf, (grad_mixed, r1) = scatter_2(net, sf, (grad_mixed, r1))
    state1, grad_mixed = reduce_1(net, r1[0], r1_theirs, cut1, grad_mixed, True)
    dproj[2], doff[2], r2 = back_part(2, grad_mixed, cols2, None, 0)
    state1, (doff, r2, dproj) = reduce_2(net, state1, (doff, r2, dproj), False)

    per_row = jnp.concatenate([d.reshape(part, rows, 2, WIDE) for d in doff], axis=0)
    per_row = per_row.transpose(1, 0, 2, 3).reshape(rows, heads, WIDE)
    grad_bucket = jnp.einsum("rhk,bk->rbh", per_row, bucket_hot, precision=highest)
    grad_table = jnp.einsum("rg,rbh->gbh", task_hot, grad_bucket, precision=highest)
    small = jnp.concatenate([grad_table.reshape(-1, width), grad_gain_ffn], axis=0)
    table_cols = small.shape[0] - 1
    small = jnp.pad(small.T, ((0, 0), (0, BLOCK - small.shape[0]))).astype(BF16)
    c = net.places()[3]
    half = width // 2
    r2 = [
        lax.dynamic_update_slice(
            r, lax.dynamic_slice_in_dim(small, at * half, half, axis=0), (0, width)
        )
        for r, at in zip(r2, (c, 1 - c))
    ]
    r2, dproj = hold((r2, dproj))
    r2_theirs = net.fetch(r2[1], "c", 1)
    sf, (r2, dproj) = scatter_3(net, sf, (r2, dproj))
    state1, (r2, dproj) = reduce_3(net, state1, (r2, dproj))
    state2, dproj = reduce_1(net, r2[0], r2_theirs, cut2, dproj, False)
    grad_tokens = token_grad(
        dproj, (w_query, w_key, w_value), flat, gain_attn, grad_middle
    )
    sf, grad_tokens = hold((sf, grad_tokens))
    grad_ffn = total(sf)
    grad_down, grad_up = grad_ffn[0], grad_ffn[1].T
    last1, grad_tokens = spread_0(net, [state1], [cut1], grad_tokens)
    state2, grad_tokens = reduce_2(net, state2, grad_tokens, False)
    state2, grad_tokens = reduce_3(net, state2, grad_tokens)
    last1, grad_tokens = spread_1(net, last1, cut1, grad_tokens)
    last2, grad_tokens = spread_0(net, [state2], [cut2], grad_tokens)
    last1, grad_tokens = spread_2(net, last1, grad_tokens)
    last2, grad_tokens = spread_1(net, last2, cut2, grad_tokens)

    last1, grad_tokens = spread_3(net, last1, grad_tokens)
    last2, grad_tokens = spread_2(net, last2, grad_tokens)

    def head_runs(first, count_here, i):
        return [
            (first + (3 * p + i) * BLOCK, first + (3 * p + i + 1) * BLOCK)
            for p in range(count_here)
        ]

    front = pairs - (pairs - 2 * part)
    weights = (w_query, w_key, w_value)
    *grads, grad_w_out, gain_sum = finish(
        net,
        *last1,
        [head_runs(width, front, i) for i in range(3)] + [[(0, width)]],
        weights,
        gain_attn,
        [width] * 4,
        0,
        None,
    )
    last2, gain_sum = spread_3(net, last2, gain_sum)
    *grads, small, gain_sum = finish(
        net,
        *last2,
        [head_runs(0, pairs - front, i) for i in range(3)] + [[(width, width + BLOCK)]],
        weights,
        gain_attn,
        [width] * 3 + [BLOCK],
        front * BLOCK,
        (grads, gain_sum),
    )
    grad_query, grad_key, grad_value = grads
    small = small.T
    grad_table = small[:table_cols].reshape(groups, bucket_count, heads)
    return (
        output.reshape(rows, length, width),
        grad_tokens.reshape(rows, length, width),
        grad_query,
        grad_key,
        grad_value,
        grad_w_out,
        grad_up,
        grad_down,
        grad_table,
        gain_sum.reshape(-1),
        small[table_cols],
    )


def solution(mesh):
    in_specs = (
        P(("ma", "an"), None, None),
        P(("ma", "an")),
        P(("ma", "an"), None),
        P(),
        P(),
        P(),
        P(),
        P(),
        P("ma", "an"),
        P("an", "ma"),
        P(),
        P(),
        P(),
        P(("ma", "an"), None, None),
    )
    out_specs = (
        P(("ma", "an"), None, None),
        P(("ma", "an"), None, None),
        P(),
        P(),
        P(),
        P(),
        P("ma", "an"),
        P("an", "ma"),
        P(),
        P(),
        P(),
    )

    def whole(*args):
        net = Links(mesh.shape["ma"], mesh.shape["an"], args[0].shape[-1])
        return local(net, *args)

    return jax.shard_map(whole, mesh=mesh, in_specs=in_specs, out_specs=out_specs, check_vma=False)
```

```python
import jax
import jax.numpy as jnp
from jax import lax
from jax.sharding import PartitionSpec as P
from jax.experimental import pallas as pl
from jax.experimental.pallas import tpu as pltpu

epsilon = 1e-06
highest = lax.Precision.HIGHEST
F32 = jnp.float32
BF16 = jnp.bfloat16
BLOCK = 128
REACH = 2
WIDE = 6 * BLOCK
CONTRACT_LANES = (((1,), (1,)), ((), ()))
CONTRACT_ROWS = (((0,), (0,)), ((), ()))
PLAIN = (((1,), (0,)), ((), ()))
hold = lax.optimization_barrier
brief = pl.CostEstimate(flops=1000, bytes_accessed=1000, transcendentals=0)


def far(x):
    return pltpu.with_memory_space_constraint(x, pltpu.HBM)


def dot(a, b, dims=PLAIN):
    return lax.dot_general(a, b, dims, preferred_element_type=F32)


def attend_body(p_ref, kseg_ref, qseg_ref, f_ref, *refs):
    u_ref, s_ref, o_ref, ot_ref = refs[-4:]
    length = p_ref.shape[0]
    blocks = length // BLOCK
    lane = lax.broadcasted_iota(jnp.int32, (length, BLOCK), 1)
    q_aug = jnp.concatenate([p_ref[:, :BLOCK] * BF16(0.125), qseg_ref[...]], axis=1)
    k = p_ref[:, BLOCK : 2 * BLOCK]
    v_t = p_ref[:, 2 * BLOCK :].astype(F32).T.astype(BF16)
    k_aug = [
        jnp.concatenate([jnp.where((lane >= 64) == (h == 1), k, BF16(0)), kseg_ref[...]], axis=1)
        for h in range(2)
    ]
    v_aug = [
        jnp.concatenate([v_t[64 * h : 64 * h + 64], jnp.ones((16, length), BF16)], axis=0)
        for h in range(2)
    ]
    tiles = [
        pltpu.roll(
            jnp.broadcast_to(f_ref[0, h : h + 1, :], (BLOCK, WIDE)), 0, 1, stride=1, stride_axis=0
        )
        for h in range(2)
    ]

    def score(h, s):
        return dot(k_aug[h], q_aug[256 * s : 256 * s + 256], CONTRACT_LANES)

    def weigh(h, s, st):
        for half in range(2):
            qb = 2 * s + half
            scored = {}
            peak = None
            for kb in range(blocks):
                o = kb - qb
                if abs(o) > REACH:
                    continue
                b = (
                    st[BLOCK * kb : BLOCK * kb + BLOCK, BLOCK * half : BLOCK * half + BLOCK]
                    + tiles[h][:, 384 - BLOCK * o : 512 - BLOCK * o]
                )
                scored[kb] = b
                peak = b if peak is None else jnp.maximum(peak, b)
            peak = jnp.max(peak, axis=0, keepdims=True)
            for kb in range(blocks):
                if kb in scored:
                    e = jnp.exp(scored[kb] - peak).astype(BF16)
                else:
                    e = jnp.zeros((BLOCK, BLOCK), BF16)
                u_ref[0, h, BLOCK * kb : BLOCK * kb + BLOCK, BLOCK * qb : BLOCK * qb + BLOCK] = e

    def mix(h, s):
        ot = dot(v_aug[h], u_ref[0, h, :, 256 * s : 256 * s + 256])
        r = 1.0 / ot[64:65]
        s_ref[0, h : h + 1, 256 * s : 256 * s + 256] = r
        return ot[:64] * r

    units = [(h, s) for h in range(2) for s in range(blocks // 2)]
    made = {}
    ahead = score(*units[0])
    for i, unit in enumerate(units):
        st = ahead
        if i + 1 < len(units):
            ahead = score(*units[i + 1])
        weigh(*unit, st)
        if i > 0:
            made[units[i - 1]] = mix(*units[i - 1])
    made[units[-1]] = mix(*units[-1])
    outs = [
        jnp.concatenate([made[h, s] for s in range(blocks // 2)], axis=1) for h in range(2)
    ]
    o_t = jnp.concatenate(outs, axis=0)
    o_ref[...] = o_t.T.astype(BF16)
    ot_ref[...] = o_t.astype(BF16)


def pair_spec(length, per_group, first):
    return pl.BlockSpec(
        (None, length, 3 * BLOCK),
        lambda p, r: ((first + p) // per_group, r, (first + p) % per_group),
    )


def attend(first, count, pairs, rows, length, proj, kseg, qseg, bias, made):
    steps = rows * pairs
    args = [far(proj), kseg, qseg, bias]
    specs = [
        pair_spec(length, pairs // proj.shape[0], first),
        pl.BlockSpec((length, BLOCK), lambda p, r: (r, 0)),
        pl.BlockSpec((length, BLOCK), lambda p, r: (r, 0)),
        pl.BlockSpec((1, 2, WIDE), lambda p, r: (r * pairs + first + p, 0, 0)),
    ]
    alias = {}
    if made is not None:
        alias = {len(args) + i: i for i in range(4)}
        args += [far(made[0]), made[1], made[2], made[3]]
        specs += [pl.BlockSpec(memory_space=pl.ANY)] * 4
    return pl.pallas_call(
        attend_body,
        grid=(count, rows),
        in_specs=specs,
        out_specs=[
            pl.BlockSpec((1, 2, length, length), lambda p, r: ((first + p) * rows + r, 0, 0, 0)),
            pl.BlockSpec((1, 2, length), lambda p, r: ((first + p) * rows + r, 0, 0)),
            pl.BlockSpec((length, BLOCK), lambda p, r: (r, first + p)),
            pl.BlockSpec((BLOCK, length), lambda p, r: (first + p, r)),
        ],
        out_shape=[
            pltpu.HBM((steps, 2, length, length), BF16),
            jax.ShapeDtypeStruct((steps, 2, length), F32),
            jax.ShapeDtypeStruct((rows * length, pairs * BLOCK), BF16),
            jax.ShapeDtypeStruct((pairs * BLOCK, rows * length), BF16),
        ],
        input_output_aliases=alias,
        compiler_params=pltpu.CompilerParams(vmem_limit_bytes=16 * 1024 * 1024),
        cost_estimate=brief,
        name="attend",
    )(*args)


def attend_grad_body(
    place_ref, p_ref, u_ref, s_ref, o_ref, g_ref, mine_ref, theirs_ref, *refs
):
    dp_ref, df_ref, go_ref, gx_ref, ds_ref, acc_ref = refs[-6:]
    length = p_ref.shape[0]
    blocks = length // BLOCK
    lane = lax.broadcasted_iota(jnp.int32, (length, BLOCK), 1)
    q = p_ref[:, :BLOCK] * BF16(0.125)
    k = p_ref[:, BLOCK : 2 * BLOCK]
    v = p_ref[:, 2 * BLOCK :]
    k_t = k.astype(F32).T.astype(BF16)
    inv = jnp.concatenate(
        [jnp.broadcast_to(s_ref[0, h : h + 1, :], (64, length)) for h in range(2)], axis=0
    ).T
    g = g_ref[...].astype(F32) * inv
    prod = g * o_ref[...].astype(F32)
    g_low = g.astype(BF16)
    prod_hi = prod.astype(BF16)
    prod_lo = (prod - prod_hi.astype(F32)).astype(BF16)
    row = lax.broadcasted_iota(jnp.int32, (2 * BLOCK, BLOCK), 0)
    col = lax.broadcasted_iota(jnp.int32, (2 * BLOCK, BLOCK), 1)
    pick = jnp.where((((row // 64) % 2) == (col // 2)) & (col < 4), -1.0, 0.0).astype(BF16)
    centre = dot(jnp.concatenate([prod_hi, prod_lo], axis=1), pick)
    centre_hi = centre.astype(BF16)
    centre_lo = (centre - centre_hi.astype(F32)).astype(BF16)
    g_aug = jnp.concatenate([g_low, jnp.where(lane % 2 == 0, centre_hi, centre_lo)], axis=1)
    zero = BF16(0)
    mine = [(lane >= 64) == (h == 1) for h in range(2)]
    v_aug = [
        jnp.concatenate(
            [jnp.where(mine[h], v, zero), jnp.where((lane // 2) == h, BF16(1), zero)], axis=1
        )
        for h in range(2)
    ]
    diag = [[None] * (2 * REACH + 1) for _ in range(2)]
    dq_t, dv, dk = [], [], []

    def score(h, s):
        return dot(v_aug[h], g_aug[256 * s : 256 * s + 256], CONTRACT_LANES)

    def weigh(h, s, dp):
        for half in range(2):
            qb = 2 * s + half
            for kb in range(blocks):
                o = kb - qb
                krows = slice(BLOCK * kb, BLOCK * kb + BLOCK)
                qcols = slice(BLOCK * qb, BLOCK * qb + BLOCK)
                if abs(o) > REACH:
                    ds_ref[h, krows, qcols] = jnp.zeros((BLOCK, BLOCK), BF16)
                    continue
                ds = (
                    u_ref[0, h, krows, qcols].astype(F32)
                    * dp[krows, BLOCK * half : BLOCK * half + BLOCK]
                )
                ds_ref[h, krows, qcols] = ds.astype(BF16)
                d = diag[h][o + REACH]
                diag[h][o + REACH] = ds if d is None else d + ds

    def values(h):
        dv.append(dot(u_ref[0, h], jnp.where(mine[h], g_low, zero)))

    def keys(h):
        dk.append(dot(ds_ref[h], jnp.where(mine[h], q, zero)))

    def queries(h):
        dq_t.append(dot(k_t[64 * h : 64 * h + 64], ds_ref[h]))

    def offsets(h):
        wide = jnp.concatenate([jnp.zeros((BLOCK, BLOCK), F32)] + diag[h][::-1], axis=1)
        step = BLOCK // 2
        while step:
            wide = wide[:step] + pltpu.roll(wide[step:], WIDE - step, 1)
            step //= 2
        df_ref[0, h : h + 1, :] = wide

    strips = range(blocks // 2)
    dps = [[score(h, s) for s in strips] for h in range(2)]
    values(0)
    for s in strips:
        weigh(0, s, dps[0][s])
    values(1)
    keys(0)
    queries(0)
    for s in strips:
        weigh(1, s, dps[1][s])
    offsets(0)
    keys(1)
    queries(1)
    offsets(1)
    dv = dv[0] + dv[1]
    dk = dk[0] + dk[1]
    dq = jnp.concatenate(dq_t, axis=0).T * 0.125
    d_all = jnp.concatenate([dq.astype(BF16), dk.astype(BF16), dv.astype(BF16)], axis=1)
    dp_ref[...] = d_all
    half = mine_ref.shape[0]
    row_step = pl.program_id(1)
    add = dot(jnp.concatenate([mine_ref[...], theirs_ref[...]], axis=0), d_all)

    @pl.when(row_step == 0)
    def _():
        acc_ref[...] = add

    @pl.when(row_step != 0)
    def _():
        acc_ref[...] += add

    @pl.when(row_step == pl.num_programs(1) - 1)
    def _():
        go_ref[...] = acc_ref[:half].astype(BF16)
        gx_ref[...] = acc_ref[half:].astype(BF16)


def attend_grad(
    net, first, count, pairs, rows, length, proj, made, grad_mixed, normed_t, cols, buffers, at
):
    saved, inverse, mixed, _ = made
    steps = rows * count
    half = normed_t.shape[0] // 2
    wide = 3 * BLOCK
    args = [far(proj), far(saved), inverse, mixed, grad_mixed, far(normed_t), far(normed_t)]
    specs = [
        pl.BlockSpec(
            (None, length, wide),
            lambda p, r, w, per=pairs // proj.shape[0]: ((first + p) // per, r, (first + p) % per),
        ),
        pl.BlockSpec((1, 2, length, length), lambda p, r, w: ((first + p) * rows + r, 0, 0, 0)),
        pl.BlockSpec((1, 2, length), lambda p, r, w: ((first + p) * rows + r, 0, 0)),
        pl.BlockSpec((length, BLOCK), lambda p, r, w: (r, first + p)),
        pl.BlockSpec((length, BLOCK), lambda p, r, w: (r, first + p)),
        pl.BlockSpec((half, length), lambda p, r, w: (w[3], r)),
        pl.BlockSpec((half, length), lambda p, r, w: (1 - w[3], r)),
    ]
    alias = {}
    if buffers is not None:
        alias = {1 + len(args) + i: 2 + i for i in range(2)}
        args += [far(b) for b in buffers]
        specs += [pl.BlockSpec(memory_space=pl.ANY)] * 2
    g_spec = pl.BlockSpec((half, wide), lambda p, r, w: (0, at // wide + p))
    return pl.pallas_call(
        attend_grad_body,
        grid_spec=pltpu.PrefetchScalarGridSpec(
            num_scalar_prefetch=1,
            grid=(count, rows),
            in_specs=specs,
            out_specs=[
                pl.BlockSpec((length, wide), lambda p, r, w: (r, p)),
                pl.BlockSpec((1, 2, WIDE), lambda p, r, w: (p * rows + r, 0, 0)),
                g_spec,
                g_spec,
            ],
            scratch_shapes=[
                pltpu.VMEM((2, length, length), BF16),
                pltpu.VMEM((2 * half, wide), F32),
            ],
        ),
        out_shape=[
            pltpu.HBM((rows * length, count * wide), BF16),
            jax.ShapeDtypeStruct((steps, 2, WIDE), F32),
            pltpu.HBM((half, cols), BF16),
            pltpu.HBM((half, cols), BF16),
        ],
        input_output_aliases=alias,
        compiler_params=pltpu.CompilerParams(vmem_limit_bytes=24 * 1024 * 1024),
        cost_estimate=brief,
        name="attend_grad",
    )(net.places(), *args)


def pick(options, index):
    out = options[0]
    for k in range(1, len(options)):
        out = jnp.where(index == k, options[k], out)
    return out


def by_distance(slices, at):
    n = len(slices)
    return [pick(slices, lax.rem(at - t + n, n)) for t in range(n)]


def in_order(pieces, at):
    n = len(pieces)
    return [pick(pieces, lax.rem(at - k + n, n)) for k in range(n)]


def by_flip(slices, at):
    return [pick(slices, lax.bitwise_xor(at, k)) for k in range(len(slices))]


def cut_rows(v, n):
    size = v.shape[0] // n
    return [v[size * k : size * k + size] for k in range(n)]


def cut_lanes(v, n):
    size = v.shape[-1] // n
    return [v[..., size * k : size * k + size] for k in range(n)]


def total(parts):
    out = parts[0].astype(F32)
    for p in parts[1:]:
        out = out + p.astype(F32)
    return out


class Links:
    def __init__(self, ma, an, width):
        z = min(4, an // 2)
        self.an = an
        self.size = {"y": ma, "z": z, "x": an // (2 * z), "c": 2}
        self.stride = {"c": 1, "x": 2, "z": 2 * self.size["x"]}
        self.tidy = width % (ma * BLOCK) == 0 and width % (8 * ma * an) == 0

    def places(self):
        an = lax.axis_index("an")
        found = [lax.axis_index("ma")]
        found += [(an // self.stride[a]) % self.size[a] for a in ("z", "x", "c")]
        return jnp.stack([f.astype(jnp.int32) for f in found])

    def fetch(self, value, axis, back):
        n = self.size[axis]
        if axis == "y":
            return lax.ppermute(value, "ma", [(i, (i + back) % n) for i in range(n)])
        s = self.stride[axis]
        pairs = []
        for i in range(self.an):
            at = (i // s) % n
            pairs.append((i, i + ((at + back) % n - at) * s))
        return lax.ppermute(value, "an", pairs)

    def flip(self, value, axis, bits):
        s = self.stride[axis]
        pairs = []
        for i in range(self.an):
            at = (i // s) % self.size[axis]
            pairs.append((i, i + ((at ^ bits) - at) * s))
        return lax.ppermute(value, "an", pairs)

    def gather(self, value, axis):
        return [value] + [self.fetch(value, axis, t) for t in range(1, self.size[axis])]

    def spread(self, parts, axis):
        n = self.size[axis]
        return [parts[0]] + [self.fetch(parts[t], axis, n - t) for t in range(1, n)]

    def step(self, fn, arrays, shapes, name, along, steps=1, away=False):
        arrays, along = hold((list(arrays), along))
        return hold((self.stage(fn, arrays, shapes, name, steps, away), along))

    def stage(self, fn, arrays, shapes, name, steps, away):
        outs = [jax.ShapeDtypeStruct(s, BF16) for s in shapes]
        place = self.places()
        if not self.tidy:
            got = fn(*[place[i] for i in range(4)], *arrays)
            return [g.astype(BF16).reshape(o.shape) for g, o in zip(got, outs)]
        count = len(arrays)

        def body(place_ref, *refs):
            got = fn(*[place_ref[i] for i in range(4)], *[r[...] for r in refs[:count]])
            for g, r in zip(got, refs[count:]):
                r[...] = g.astype(BF16)

        def spec(a):
            rest = len(a.shape) - 1
            return pl.BlockSpec(
                (a.shape[0] // steps,) + a.shape[1:], lambda i, p, rest=rest: (i,) + (0,) * rest
            )

        return pl.pallas_call(
            body,
            grid_spec=pltpu.PrefetchScalarGridSpec(
                num_scalar_prefetch=1,
                grid=(steps,),
                in_specs=[spec(a) for a in arrays],
                out_specs=[spec(o) for o in outs],
            ),
            out_shape=[pltpu.HBM(o.shape, o.dtype) for o in outs] if away else outs,
            compiler_params=pltpu.CompilerParams(vmem_limit_bytes=16 * 1024 * 1024),
            cost_estimate=brief,
            name=name,
        )(place, *arrays)


def gather_1(net, pieces, along):
    rows, cols = pieces[0].shape
    half = rows // 2
    n = len(pieces)

    def fn(y, z, x, c, *pieces):
        v = jnp.stack(in_order(pieces, z))
        return [v[:, :half], v[:, half:]]

    (a, b), along = net.step(fn, pieces, [(n, half, cols)] * 2, "gather_z", along)
    return (net.gather(a, "x"), net.gather(b, "y")), along


def gather_2(net, state, along):
    a, b = state
    n, half, cols = a[0].shape

    def fn(y, z, x, c, *parts):
        a_in = in_order(parts[: len(a)], x)
        b_in = in_order(parts[len(a) :], y)
        return [jnp.stack(a_in, axis=1), jnp.concatenate(b_in, axis=-1)]

    (a, b), along = net.step(
        fn, a + b, [(n, len(a), half, cols), (n, half, cols * len(b))], "gather_xy", along
    )
    return (net.gather(a, "y"), net.gather(b, "x")), along


def gather_3(net, state, along):
    a, b = state
    n, nx, half, cols = a[0].shape

    def fn(y, z, x, c, *parts):
        a_in = jnp.concatenate(in_order(parts[: len(a)], y), axis=-1)
        b_in = jnp.stack(in_order(parts[len(a) :], x), axis=1)
        return [jnp.concatenate([a_in, b_in], axis=2)]

    shape = (n, nx, 2 * half, cols * len(a))
    (own,), along = net.step(fn, a + b, [shape], "gather_yx", along, steps=n if net.tidy else 1)
    return net.gather(own, "c"), along


def scatter_1(net, own, theirs, along):
    nz, two, nx, hb, width = own.shape
    half = hb // 2
    ny = net.size["y"]

    def fn(y, z, x, c, own, theirs):
        v = total([own, theirs])
        a, b = v[..., :half, :], v[..., half:, :]
        return by_distance(cut_lanes(a, ny), y) + by_distance([b[:, :, k] for k in range(nx)], x)

    shapes = [(nz, two, nx, half, width // ny)] * ny + [(nz, two, half, width)] * nx
    parts, along = net.step(
        fn, [own, theirs], shapes, "scatter_yx", along, steps=nz if net.tidy else 1
    )
    return (net.spread(parts[:ny], "y"), net.spread(parts[ny:], "x")), along


def scatter_2(net, state, along):
    a, b = state
    nz, two, nx, half, cols = a[0].shape
    ny = net.size["y"]

    def fn(y, z, x, c, *parts):
        va, vb = total(parts[:ny]), total(parts[ny:])
        return by_distance([va[:, :, k] for k in range(nx)], x) + by_distance(cut_lanes(vb, ny), y)

    shapes = [(nz, two, half, cols)] * (nx + ny)
    parts, along = net.step(fn, a + b, shapes, "scatter_xy", along)
    return (net.spread(parts[:nx], "x"), net.spread(parts[nx:], "y")), along


def scatter_3(net, state, along):
    a, b = state
    nz, two, half, cols = a[0].shape

    def fn(y, z, x, c, *parts):
        v = jnp.concatenate([total(parts[: len(a)]), total(parts[len(a) :])], axis=2)
        return halves([v[k] for k in range(nz)], z)

    parts, along = net.step(fn, a + b, [(nz // 2, two, 2 * half, cols)] * 2, "scatter_z", along)
    return (parts[0], net.flip(parts[1], "z", 1)), along


def halves(slices, at):
    p = by_flip(slices, at)
    return [jnp.stack([p[0], p[2]]), jnp.stack([p[1], p[3]])]


def fold_z(net, state, along):
    kept, got = state

    def fn(y, z, x, c, kept, got):
        v = total([kept, got])
        return [v[0], v[1]]

    parts, along = net.step(fn, [kept, got], [kept.shape[1:]] * 2, "fold_z", along)
    return [parts[0], net.flip(parts[1], "z", 2)], along


def reduce_1(net, own, theirs, cut, along, away):
    rows, cols = own.shape
    ny, nx = net.size["y"], net.size["x"]

    def fn(y, z, x, c, own, theirs):
        v = total([own, theirs])
        return by_distance(cut_rows(v[:, :cut], ny), y) + by_distance(cut_rows(v[:, cut:], nx), x)

    shapes = [(rows // ny, cut)] * ny + [(rows // nx, cols - cut)] * nx
    parts, along = net.step(fn, [own, theirs], shapes, "reduce_yx", along, away=away)
    return (net.spread(parts[:ny], "y"), net.spread(parts[ny:], "x")), along


def reduce_2(net, state, along, away):
    a, b = state
    ny, nx = net.size["y"], net.size["x"]

    def fn(y, z, x, c, *parts):
        va, vb = total(parts[: len(a)]), total(parts[len(a) :])
        return by_distance(cut_rows(va, nx), x) + by_distance(cut_rows(vb, ny), y)

    shapes = [(a[0].shape[0] // nx, a[0].shape[1])] * nx
    shapes += [(b[0].shape[0] // ny, b[0].shape[1])] * ny
    parts, along = net.step(fn, a + b, shapes, "reduce_xy", along, away=away)
    return (net.spread(parts[:nx], "x"), net.spread(parts[nx:], "y")), along


def reduce_3(net, state, along):
    a, b = state
    n = net.size["z"]

    def fn(y, z, x, c, *parts):
        v = jnp.concatenate([total(parts[: len(a)]), total(parts[len(a) :])], axis=1)
        return halves(cut_rows(v, n), z)

    shape = (n // 2, a[0].shape[0] // n, a[0].shape[1] + b[0].shape[1])
    parts, along = net.step(fn, a + b, [shape] * 2, "reduce_z", along)
    return (parts[0], net.flip(parts[1], "z", 1)), along


def spread_0(net, parts, along):
    def fn(y, z, x, c, *parts):
        return [total(parts)]

    (front,), along = net.step(fn, parts, [parts[0].shape], "spread_sum", along)
    return [front, net.flip(front, "z", 2)], along


def spread_z(net, pieces, along):
    def fn(y, z, x, c, *pieces):
        return [jnp.stack(pieces)]

    (pair,), along = net.step(fn, pieces, [(2,) + pieces[0].shape], "spread_pair", along)
    return [pair, net.flip(pair, "z", 1)], along


def spread_1(net, pairs, cut, along):
    _, rows, cols = pairs[0].shape

    def fn(y, z, x, c, *pairs):
        found = [p[k].astype(F32) for k in range(2) for p in pairs]
        v = jnp.concatenate(by_flip(found, z), axis=0)
        return [v[:, :cut], v[:, cut:]]

    shapes = [(4 * rows, cut), (4 * rows, cols - cut)]
    (a, b), along = net.step(fn, pairs, shapes, "spread_z", along)
    return (net.gather(a, "x"), net.gather(b, "y")), along


def spread_2(net, state, along):
    a, b = state

    def fn(y, z, x, c, *parts):
        va = jnp.concatenate(in_order(parts[: len(a)], x), axis=0)
        vb = jnp.concatenate(in_order(parts[len(a) :], y), axis=0)
        return [va, vb]

    shapes = [(len(p) * p[0].shape[0], p[0].shape[1]) for p in (a, b)]
    (a, b), along = net.step(fn, a + b, shapes, "spread_xy", along)
    return (net.gather(a, "y"), net.gather(b, "x")), along


def spread_3(net, state, along):
    a, b = state

    def fn(y, z, x, c, *parts):
        va = jnp.concatenate(in_order(parts[: len(a)], y), axis=0)
        vb = jnp.concatenate(in_order(parts[len(a) :], x), axis=0)
        return [jnp.concatenate([va, vb], axis=1)]

    shape = (len(a) * a[0].shape[0], a[0].shape[1] + b[0].shape[1])
    (v,), along = net.step(fn, a + b, [shape], "spread_yx", along)
    return net.gather(v, "c"), along


def finish(net, value, rel, cuts, weights, gain, width, heads_from, into, so_far):
    half, cols = value.shape
    tile = BLOCK
    steps = half // tile
    widths = [sum(b - a for a, b in runs) for runs in cuts]
    narrow = widths[3] == BLOCK

    def body(place_ref, v_ref, wq_ref, wk_ref, wv_ref, gain_ref, *refs):
        outs = refs[-5:]
        v = v_ref[...].astype(F32)
        made = [jnp.concatenate([v[:, a:b] for a, b in runs], axis=1) for runs in cuts]
        for k, (out, m) in enumerate(zip(outs, made)):
            out[...] = m.T[:8] if k == 3 and narrow else m
        acc = made[0] * wq_ref[...].astype(F32)
        acc = acc + made[1] * wk_ref[...].astype(F32) + made[2] * wv_ref[...].astype(F32)
        part = jnp.broadcast_to(jnp.sum(acc, axis=1, keepdims=True), (tile, BLOCK)).T[:1]
        part = part / gain_ref[...]
        outs[4][...] = part if so_far is None else part + refs[0][...]

    def row(i, p):
        return (p[3] if rel == 0 else 1 - p[3]) * steps + i

    def cols_spec(w, at):
        return pl.BlockSpec((tile, w), lambda i, p: (row(i, p), at // w))

    def lanes_spec(rows):
        return pl.BlockSpec((rows, tile), lambda i, p: (0, row(i, p)))

    args = [value, *[far(w) for w in weights], gain.reshape(1, -1)]
    specs = [pl.BlockSpec((tile, cols), lambda i, p: (i, 0))]
    specs += [cols_spec(widths[0], heads_from)] * 3 + [lanes_spec(1)]
    alias = {}
    if so_far is not None:
        args.append(so_far)
        specs.append(lanes_spec(1))
    if into:
        alias = {1 + len(args) + k: k for k in range(len(into))}
        args += list(into)
        specs += [pl.BlockSpec(memory_space=pl.ANY)] * len(into)
    return pl.pallas_call(
        body,
        grid_spec=pltpu.PrefetchScalarGridSpec(
            num_scalar_prefetch=1,
            grid=(steps,),
            in_specs=specs,
            out_specs=[cols_spec(w, heads_from) for w in widths[:3]]
            + [lanes_spec(8) if narrow else cols_spec(widths[3], 0), lanes_spec(1)],
        ),
        out_shape=[pltpu.HBM((2 * half, width), F32)] * 3
        + [
            jax.ShapeDtypeStruct((8, 2 * half), F32) if narrow else pltpu.HBM((2 * half, width), F32),
            jax.ShapeDtypeStruct((1, 2 * half), F32),
        ],
        input_output_aliases=alias,
        compiler_params=pltpu.CompilerParams(vmem_limit_bytes=20 * 1024 * 1024),
        cost_estimate=brief,
        name="finish",
    )(net.places(), *args)


def project(tokens, gain, weights, groups):
    count, width = tokens.shape
    tile = min(256, count)
    pairs_here = width // BLOCK // groups

    def body(t_ref, gain_ref, *refs):
        out, nt_ref = refs[-2:]
        x = t_ref[...].astype(F32)
        inv = lax.rsqrt(jnp.mean(x * x, axis=1, keepdims=True) + epsilon)
        normed = x * inv * gain_ref[...]
        low = normed.astype(BF16)
        nt_ref[...] = normed.T.astype(BF16)
        for i, w in enumerate(refs[:-2]):
            r = dot(low, w[...]).astype(BF16)
            for p in range(groups * pairs_here):
                at = (3 * (p % pairs_here) + i) * BLOCK
                out[p // pairs_here, :, at : at + BLOCK] = r[:, BLOCK * p : BLOCK * p + BLOCK]

    return pl.pallas_call(
        body,
        grid=(count // tile,),
        in_specs=[
            pl.BlockSpec((tile, width), lambda i: (i, 0)),
            pl.BlockSpec((1, width), lambda i: (0, 0)),
        ]
        + [pl.BlockSpec((width, width), lambda i: (0, 0))] * 3,
        out_specs=[
            pl.BlockSpec((groups, tile, 3 * width // groups), lambda i: (0, i, 0)),
            pl.BlockSpec((width, tile), lambda i: (0, i)),
        ],
        out_shape=[
            pltpu.HBM((groups, count, 3 * width // groups), BF16),
            pltpu.HBM((width, count), BF16),
        ],
        compiler_params=pltpu.CompilerParams(vmem_limit_bytes=24 * 1024 * 1024),
        cost_estimate=brief,
        name="project",
    )(far(tokens), gain.reshape(1, -1), *[far(w) for w in weights])


def gelu_parts(pre):
    k0 = 0.7978845608028654
    k1 = 0.044715
    sq = pre * pre
    s = 0.5 * jnp.tanh(pre * (k0 + (k0 * k1) * sq)) + 0.5
    act = pre * s
    slope = s + (act - act * s) * (2.0 * k0 + (6.0 * k0 * k1) * sq)
    return act, slope


def before_ffn(mixed, w_out, tokens, gain, g):
    count, width = mixed.shape
    tile = min(256, count)

    def body(mixed_ref, w_ref, t_ref, gain_ref, g_ref, mid_ref, s_ref, st_ref, gt_ref):
        mid = t_ref[...].astype(F32) + dot(mixed_ref[...], w_ref[...])
        inv = lax.rsqrt(jnp.mean(mid * mid, axis=1, keepdims=True) + epsilon)
        second = mid * inv * gain_ref[...]
        mid_ref[...] = mid.astype(BF16)
        s_ref[...] = second.astype(BF16)
        st_ref[...] = second.T.astype(BF16)
        gt_ref[...] = g_ref[...].astype(F32).T.astype(BF16)

    def rows_of(w):
        return pl.BlockSpec((tile, w), lambda i: (i, 0))

    cols = pl.BlockSpec((width, tile), lambda i: (0, i))
    return pl.pallas_call(
        body,
        grid=(count // tile,),
        in_specs=[
            rows_of(width),
            pl.BlockSpec((width, width), lambda i: (0, 0)),
            rows_of(width),
            pl.BlockSpec((1, width), lambda i: (0, 0)),
            rows_of(width),
        ],
        out_specs=[rows_of(width), rows_of(width), cols, cols],
        out_shape=[
            pltpu.HBM((count, width), BF16),
            pltpu.HBM((count, width), BF16),
            pltpu.HBM((width, count), BF16),
            pltpu.HBM((width, count), BF16),
        ],
        compiler_params=pltpu.CompilerParams(vmem_limit_bytes=20 * 1024 * 1024),
        cost_estimate=brief,
        name="before_ffn",
    )(mixed, far(w_out), far(tokens), gain.reshape(1, -1), far(g))


def ffn(net, ups, downs, second, second_t, g, g_t, middle):
    nz, nx, hb, width = ups[0].shape
    count = g.shape[0]
    part = nx * hb
    tile = 256 if count % 256 == 0 else count
    lanes = 256 if width % 256 == 0 else width

    def body(
        place_ref, u0_ref, u1_ref, d0_ref, d1_ref, st_far, gt_far, g_far, s_far, m_far,
        out_ref, go_ref, gx_ref, gs_ref, act_ref, gu_ref, acc_ref, gsum_ref,
        st_ref, gt_ref, g_ref, s_ref, m_ref, sems,
    ):
        step = pl.program_id(0)
        st_copy, gt_copy, g_copy, s_copy, m_copy = [
            pltpu.make_async_copy(a, b, sems.at[i])
            for i, (a, b) in enumerate(
                (
                    (st_far, st_ref),
                    (gt_far, gt_ref),
                    (g_far, g_ref),
                    (s_far, s_ref),
                    (m_far, m_ref),
                )
            )
        ]

        @pl.when(step == 0)
        def _():
            for copy in (st_copy, gt_copy, g_copy, s_copy, m_copy):
                copy.start()
            st_copy.wait()
            gt_copy.wait()

        up_all, down_all = [
            jnp.concatenate([r[...].reshape(part, width) for r in refs], axis=0)
            for refs in ((u0_ref, u1_ref), (d0_ref, d1_ref))
        ]
        starts = list(range(0, count, tile))

        def both(t):
            return dot(up_all, st_ref[:, t : t + tile]), dot(down_all, gt_ref[:, t : t + tile])

        @pl.when(step == 0)
        def _():
            acc_ref[...] = jnp.zeros_like(acc_ref)
            gsum_ref[...] = jnp.zeros_like(gsum_ref)

        def sums(t):
            at = slice(t, t + tile)
            acc_ref[at] += dot(act_ref[:, at], down_all, CONTRACT_ROWS)
            gsum_ref[at] += dot(gu_ref[:, at], up_all, CONTRACT_ROWS)

        ahead = both(starts[0])
        for n, t in enumerate(starts):
            pre, gh = ahead
            if n + 1 < len(starts):
                ahead = both(starts[n + 1])
            act, slope = gelu_parts(pre)
            act_ref[:, t : t + tile] = act.astype(BF16)
            gu_ref[:, t : t + tile] = (gh * slope).astype(BF16)
            if n > 0:
                sums(starts[n - 1])
        sums(starts[-1])

        @pl.when(step == 0)
        def _():
            g_copy.wait()
            s_copy.wait()

        for k in range(0, width, lanes):
            cols = slice(k, k + lanes)
            gd = dot(act_ref[...], g_ref[:, cols]).astype(BF16)
            gu = dot(gu_ref[...], s_ref[:, cols]).astype(BF16)
            for rel in range(2):
                for i in range(nx):
                    at = part * rel + hb * i
                    out = (go_ref, gx_ref)[rel]
                    out[0, i, :, cols] = gd[at : at + hb]
                    out[1, i, :, cols] = gu[at : at + hb]

        @pl.when(step == nz - 1)
        def _():
            m_copy.wait()
            out_ref[...] = (m_ref[...].astype(F32) + acc_ref[...]).astype(BF16)
            gs_ref[...] = gsum_ref[...].astype(BF16)

    away = pl.BlockSpec(memory_space=pltpu.HBM)

    one = pl.BlockSpec((None, nx, hb, width), lambda i, p: (i, 0, 0, 0))
    two = pl.BlockSpec((None, 2, nx, hb, width), lambda i, p: (i, 0, 0, 0, 0))
    flat = pl.BlockSpec((count, width), lambda i, p: (0, 0))
    return pl.pallas_call(
        body,
        grid_spec=pltpu.PrefetchScalarGridSpec(
            num_scalar_prefetch=1,
            grid=(nz,),
            in_specs=[one] * 4 + [away] * 5,
            out_specs=[flat, two, two, flat],
            scratch_shapes=[
                pltpu.VMEM((2 * part, count), BF16),
                pltpu.VMEM((2 * part, count), BF16),
                pltpu.VMEM((count, width), F32),
                pltpu.VMEM((count, width), F32),
                pltpu.VMEM((width, count), BF16),
                pltpu.VMEM((width, count), BF16),
                pltpu.VMEM((count, width), BF16),
                pltpu.VMEM((count, width), BF16),
                pltpu.VMEM((count, width), BF16),
                pltpu.SemaphoreType.DMA((5,)),
            ],
        ),
        out_shape=[
            pltpu.HBM((count, width), BF16),
            pltpu.HBM((nz, 2, nx, hb, width), BF16),
            pltpu.HBM((nz, 2, nx, hb, width), BF16),
            pltpu.HBM((count, width), BF16),
        ],
        compiler_params=pltpu.CompilerParams(vmem_limit_bytes=42 * 1024 * 1024),
        cost_estimate=brief,
        name="ffn",
    )(net.places(), *ups, *downs, *[far(v) for v in (second_t, g_t, g, second, middle)])


def after_ffn(net, grad_second, middle, gain, g, w_out, mixed_t, cols):
    count, width = middle.shape
    half = width // 2
    tile = min(256, count)

    def body(
        place_ref, gs_ref, m_ref, gain_ref, g_ref, w_ref, mine_ref, theirs_ref,
        gm_ref, gx_ref, gg_ref, wo_ref, wx_ref, acc_ref,
    ):
        gs = gs_ref[...].astype(F32)
        m = m_ref[...].astype(F32)
        r = lax.rsqrt(jnp.mean(m * m, axis=1, keepdims=True) + epsilon)
        scaled = gs * gain_ref[...]
        mean = jnp.mean(scaled * m, axis=1, keepdims=True)
        gm = g_ref[...].astype(F32) + r * scaled - m * (r * r * r * mean)
        ga = gm.astype(BF16)
        gm_ref[...] = ga
        gx_ref[...] = dot(ga, w_ref[...], CONTRACT_LANES).astype(BF16)
        add = jnp.sum(gs * (m * r), axis=0, keepdims=True)
        step = pl.program_id(0)

        @pl.when(step == 0)
        def _():
            gg_ref[...] = add

        @pl.when(step != 0)
        def _():
            gg_ref[...] += add

        add_o = dot(jnp.concatenate([mine_ref[...], theirs_ref[...]], axis=0), ga)

        @pl.when(step == 0)
        def _():
            acc_ref[...] = add_o

        @pl.when(step != 0)
        def _():
            acc_ref[...] += add_o

        @pl.when(step == pl.num_programs(0) - 1)
        def _():
            wo_ref[...] = acc_ref[:half].astype(BF16)
            wx_ref[...] = acc_ref[half:].astype(BF16)

    def rows_of(w):
        return pl.BlockSpec((tile, w), lambda i, p: (i, 0))

    row = pl.BlockSpec((1, width), lambda i, p: (0, 0))
    grad = pl.BlockSpec((half, width), lambda i, p: (0, 0))
    return pl.pallas_call(
        body,
        grid_spec=pltpu.PrefetchScalarGridSpec(
            num_scalar_prefetch=1,
            grid=(count // tile,),
            in_specs=[
                rows_of(width),
                rows_of(width),
                row,
                rows_of(width),
                pl.BlockSpec((width, width), lambda i, p: (0, 0)),
                pl.BlockSpec((half, tile), lambda i, p: (p[3], i)),
                pl.BlockSpec((half, tile), lambda i, p: (1 - p[3], i)),
            ],
            out_specs=[rows_of(width), rows_of(width), row, grad, grad],
            scratch_shapes=[pltpu.VMEM((width, width), F32)],
        ),
        out_shape=[
            pltpu.HBM((count, width), BF16),
            jax.ShapeDtypeStruct((count, width), BF16),
            jax.ShapeDtypeStruct((1, width), F32),
            pltpu.HBM((half, cols), BF16),
            pltpu.HBM((half, cols), BF16),
        ],
        compiler_params=pltpu.CompilerParams(vmem_limit_bytes=24 * 1024 * 1024),
        cost_estimate=brief,
        name="after_ffn",
    )(net.places(), far(grad_second), far(middle), gain.reshape(1, -1), far(g), far(w_out), mixed_t, mixed_t)


def token_grad(dproj, weights, tokens, gain, grad_middle):
    count, width = tokens.shape
    tile = min(256, count)

    def body(*refs):
        d_refs = refs[: len(dproj)]
        w_refs = refs[len(dproj) : len(dproj) + 3]
        t_ref, gain_ref, gm_ref, out_ref = refs[len(dproj) + 3 :]
        gn = None
        for i, w in enumerate(w_refs):
            cols = []
            for d in d_refs:
                for p in range(d.shape[1] // (3 * BLOCK)):
                    at = (3 * p + i) * BLOCK
                    cols.append(d[:, at : at + BLOCK])
            r = dot(jnp.concatenate(cols, axis=1), w[...], CONTRACT_LANES)
            gn = r if gn is None else gn + r
        scaled = gn * gain_ref[...]
        x = t_ref[...].astype(F32)
        r = lax.rsqrt(jnp.mean(x * x, axis=1, keepdims=True) + epsilon)
        mean = jnp.mean(scaled * x, axis=1, keepdims=True)
        out_ref[...] = gm_ref[...].astype(F32) + r * scaled - x * (r * r * r * mean)

    def rows_of(w):
        return pl.BlockSpec((tile, w), lambda i: (i, 0))

    return pl.pallas_call(
        body,
        grid=(count // tile,),
        in_specs=[rows_of(d.shape[1]) for d in dproj]
        + [pl.BlockSpec(w.shape, lambda i: (0, 0)) for w in weights]
        + [rows_of(width), pl.BlockSpec((1, width), lambda i: (0, 0)), rows_of(width)],
        out_specs=rows_of(width),
        out_shape=pltpu.HBM((count, width), F32),
        compiler_params=pltpu.CompilerParams(vmem_limit_bytes=20 * 1024 * 1024),
        cost_estimate=brief,
        name="token_grad",
    )(*[far(d) for d in dproj], *[far(w) for w in weights], far(tokens), gain.reshape(1, -1), far(grad_middle))


def local(
    net,
    tokens,
    tasks,
    segments,
    buckets,
    w_query,
    w_key,
    w_value,
    w_out,
    w_up,
    w_down,
    bias_table,
    gain_attn,
    gain_ffn,
    cotangent,
):
    rows, length, width = tokens.shape
    groups, bucket_count, heads = bias_table.shape
    pairs = heads // 2
    count = rows * length
    parts = 3
    part = pairs // parts

    up_state = net.gather(w_up.T, "z")
    flat = tokens.reshape(count, width)
    proj, normed_t = project(flat, gain_attn, (w_query, w_key, w_value), parts)

    task_hot = (tasks[:, None] == jnp.arange(groups, dtype=jnp.int32)[None, :]).astype(F32)
    table_rows = jnp.einsum("rg,gbh->rbh", task_hot, bias_table, precision=highest)
    middle_offset = length - 1 + 3 * BLOCK
    near = buckets[middle_offset - WIDE + 1 : middle_offset + 1][::-1]
    bucket_hot = (near[None, :] == jnp.arange(bucket_count, dtype=jnp.int32)[:, None]).astype(F32)
    bias = jnp.einsum("rbh,bk->rhk", table_rows, bucket_hot, precision=highest)
    bias = bias.reshape(rows * pairs, 2, WIDE)
    seg = segments.reshape(count, 1)
    lane = jnp.arange(BLOCK, dtype=jnp.int32)[None, :]
    kseg = (lane == seg).astype(BF16)
    qseg = jnp.where((lane != seg) & (lane < 4), -1e30, 0.0).astype(BF16)

    def attend_part(first, pairs_here, proj, made):
        return attend(first, pairs_here, pairs, rows, length, proj, kseg, qseg, bias, made)

    up_state, (proj, w_down) = gather_1(net, up_state, (proj, w_down))
    down_state = net.gather(w_down, "z")
    sixth = max(1, pairs // 6)
    made = attend_part(0, sixth, proj, None)
    up_state, (made, proj) = gather_2(net, up_state, (made, proj))
    made = attend_part(sixth, 2 * sixth, proj, made)
    down_state, (made, proj) = gather_1(net, down_state, (made, proj))
    made = attend_part(3 * sixth, sixth, proj, made)
    ups, (made, proj) = gather_3(net, up_state, (made, proj))
    made = attend_part(4 * sixth, sixth, proj, made)
    down_state, (made, proj) = gather_2(net, down_state, (made, proj))
    made = attend_part(5 * sixth, pairs - 5 * sixth, proj, made)
    mixed, mixed_t = made[2:]
    g = cotangent.reshape(count, width)
    middle, second, second_t, g_t = before_ffn(mixed, w_out, flat, gain_ffn, g)
    downs, second = gather_3(net, down_state, second)

    ups, downs, second = hold((ups, downs, second))
    output, gf_own, gf_other, grad_second = ffn(
        net, ups, downs, second, second_t, g, g_t, middle
    )
    gf_other, grad_second = hold((gf_other, grad_second))
    gf_theirs = net.fetch(gf_other, "c", 1)
    cols1 = width * parts
    cols2 = width + BLOCK
    cut1 = cols1 // 2
    cut2 = width // 2
    grad_middle, grad_mixed, grad_gain_ffn, *r1 = after_ffn(
        net, grad_second, middle, gain_ffn, g, w_out, mixed_t, cols1
    )
    sf, grad_mixed = scatter_1(net, gf_own, gf_theirs, grad_mixed)

    def back_part(i, grad_mixed, cols, buffers, at):
        d, off, *r = attend_grad(
            net, part * i, part, pairs, rows, length, proj, made, grad_mixed, normed_t, cols, buffers, at
        )
        return d, off, r

    dproj = [None] * parts
    doff = [None] * parts
    dproj[0], doff[0], r1 = back_part(0, grad_mixed, cols1, r1, width)
    dproj[1], doff[1], r1 = back_part(1, grad_mixed, cols1, r1, 2 * width)
    grad_mixed, r1, sf = hold((grad_mixed, r1, sf))
    r1_theirs = net.fetch(r1[1], "c", 1)
    state1, grad_mixed = reduce_1(net, r1[0], r1_theirs, cut1, grad_mixed, True)
    dproj[2], doff[2], r2 = back_part(2, grad_mixed, cols2, None, 0)
    state1, (doff, r2, dproj) = reduce_2(net, state1, (doff, r2, dproj), False)

    per_row = jnp.concatenate([d.reshape(part, rows, 2, WIDE) for d in doff], axis=0)
    per_row = per_row.transpose(1, 0, 2, 3).reshape(rows, heads, WIDE)
    grad_bucket = jnp.einsum("rhk,bk->rbh", per_row, bucket_hot, precision=highest)
    grad_table = jnp.einsum("rg,rbh->gbh", task_hot, grad_bucket, precision=highest)
    small = jnp.concatenate([grad_table.reshape(-1, width), grad_gain_ffn], axis=0)
    table_cols = small.shape[0] - 1
    small = jnp.pad(small.T, ((0, 0), (0, BLOCK - small.shape[0]))).astype(BF16)
    c = net.places()[3]
    half = width // 2
    r2 = [
        lax.dynamic_update_slice(
            r, lax.dynamic_slice_in_dim(small, at * half, half, axis=0), (0, width)
        )
        for r, at in zip(r2, (c, 1 - c))
    ]
    r2, dproj = hold((r2, dproj))
    r2_theirs = net.fetch(r2[1], "c", 1)
    state1, (r2, dproj) = reduce_3(net, state1, (r2, dproj))
    state2, dproj = reduce_1(net, r2[0], r2_theirs, cut2, dproj, False)
    state1, dproj = fold_z(net, state1, dproj)
    state2, dproj = reduce_2(net, state2, dproj, False)
    sf, dproj = scatter_2(net, sf, dproj)
    grad_tokens = token_grad(
        dproj, (w_query, w_key, w_value), flat, gain_attn, grad_middle
    )
    def head_runs(first, count_here, i):
        return [
            (first + (3 * p + i) * BLOCK, first + (3 * p + i + 1) * BLOCK)
            for p in range(count_here)
        ]

    front = pairs - (pairs - 2 * part)
    weights = (w_query, w_key, w_value)
    cuts1 = [head_runs(width, front, i) for i in range(3)] + [[(0, width)]]
    cuts2 = [head_runs(0, pairs - front, i) for i in range(3)] + [[(width, width + BLOCK)]]

    def finish_1(value, rel, into):
        return finish(net, value, rel, cuts1, weights, gain_attn, width, 0, into, None)

    def finish_2(value, rel, into):
        return finish(
            net, value, rel, cuts2, weights, gain_attn, width, front * BLOCK, into, made1[4]
        )

    last1, grad_tokens = spread_0(net, state1, grad_tokens)
    state2, grad_tokens = reduce_3(net, state2, grad_tokens)
    last1, grad_tokens = spread_z(net, last1, grad_tokens)
    state2, grad_tokens = fold_z(net, state2, grad_tokens)
    last1, grad_tokens = spread_1(net, last1, cut1, grad_tokens)
    sf, grad_tokens = scatter_3(net, sf, grad_tokens)
    last2, grad_tokens = spread_0(net, state2, grad_tokens)
    last1, grad_tokens = spread_2(net, last1, grad_tokens)
    last2, grad_tokens = spread_z(net, last2, grad_tokens)
    sf, grad_tokens = fold_z(net, sf, grad_tokens)
    last2, grad_tokens = spread_1(net, last2, cut2, grad_tokens)
    last1, grad_tokens = spread_3(net, last1, grad_tokens)
    made1 = finish_1(last1[0], 0, None)
    last2, (grad_tokens, made1) = spread_2(net, last2, (grad_tokens, made1))
    made1 = finish_1(last1[1], 1, made1)
    last2, (grad_tokens, sf, made1) = spread_3(net, last2, (grad_tokens, sf, made1))
    made2 = finish_2(last2[0], 0, made1[:3])
    grad_ffn = total(sf)
    grad_down, grad_up = grad_ffn[0], grad_ffn[1].T

    made2 = finish_2(last2[1], 1, made2)
    grad_query, grad_key, grad_value, small, gain_sum = made2
    grad_w_out = made1[3]
    grad_table = small[:table_cols].reshape(groups, bucket_count, heads)
    return (
        output.reshape(rows, length, width),
        grad_tokens.reshape(rows, length, width),
        grad_query,
        grad_key,
        grad_value,
        grad_w_out,
        grad_up,
        grad_down,
        grad_table,
        gain_sum.reshape(-1),
        small[table_cols],
    )


def solution(mesh):
    in_specs = (
        P(("ma", "an"), None, None),
        P(("ma", "an")),
        P(("ma", "an"), None),
        P(),
        P(),
        P(),
        P(),
        P(),
        P("ma", "an"),
        P("an", "ma"),
        P(),
        P(),
        P(),
        P(("ma", "an"), None, None),
    )
    out_specs = (
        P(("ma", "an"), None, None),
        P(("ma", "an"), None, None),
        P(),
        P(),
        P(),
        P(),
        P("ma", "an"),
        P("an", "ma"),
        P(),
        P(),
        P(),
    )

    def whole(*args):
        net = Links(mesh.shape["ma"], mesh.shape["an"], args[0].shape[-1])
        return local(net, *args)

    return jax.shard_map(whole, mesh=mesh, in_specs=in_specs, out_specs=out_specs, check_vma=False)
```

```python
import jax
import jax.numpy as jnp
from jax import lax
from jax.sharding import PartitionSpec as P
from jax.experimental import pallas as pl
from jax.experimental.pallas import tpu as pltpu

epsilon = 1e-06
highest = lax.Precision.HIGHEST
F32 = jnp.float32
BF16 = jnp.bfloat16
BLOCK = 128
REACH = 2
WIDE = 6 * BLOCK
CONTRACT_LANES = (((1,), (1,)), ((), ()))
CONTRACT_ROWS = (((0,), (0,)), ((), ()))
PLAIN = (((1,), (0,)), ((), ()))
hold = lax.optimization_barrier
brief = pl.CostEstimate(flops=1000, bytes_accessed=1000, transcendentals=0)


def far(x):
    return pltpu.with_memory_space_constraint(x, pltpu.HBM)


def dot(a, b, dims=PLAIN):
    return lax.dot_general(a, b, dims, preferred_element_type=F32)


def attend_body(p_ref, kseg_ref, qseg_ref, f_ref, *refs):
    u_ref, s_ref, o_ref, ot_ref = refs[-4:]
    length = p_ref.shape[0]
    blocks = length // BLOCK
    lane = lax.broadcasted_iota(jnp.int32, (length, BLOCK), 1)
    q_aug = jnp.concatenate([p_ref[:, :BLOCK] * BF16(0.125), qseg_ref[...]], axis=1)
    k = p_ref[:, BLOCK : 2 * BLOCK]
    v_t = p_ref[:, 2 * BLOCK :].astype(F32).T.astype(BF16)
    k_aug = [
        jnp.concatenate([jnp.where((lane >= 64) == (h == 1), k, BF16(0)), kseg_ref[...]], axis=1)
        for h in range(2)
    ]
    v_aug = [
        jnp.concatenate([v_t[64 * h : 64 * h + 64], jnp.ones((16, length), BF16)], axis=0)
        for h in range(2)
    ]
    tiles = [
        pltpu.roll(
            jnp.broadcast_to(f_ref[0, h : h + 1, :], (BLOCK, WIDE)), 0, 1, stride=1, stride_axis=0
        )
        for h in range(2)
    ]

    def score(h, s):
        return dot(k_aug[h], q_aug[256 * s : 256 * s + 256], CONTRACT_LANES)

    def weigh(h, s, st):
        for half in range(2):
            qb = 2 * s + half
            scored = {}
            peak = None
            for kb in range(blocks):
                o = kb - qb
                if abs(o) > REACH:
                    continue
                b = (
                    st[BLOCK * kb : BLOCK * kb + BLOCK, BLOCK * half : BLOCK * half + BLOCK]
                    + tiles[h][:, 384 - BLOCK * o : 512 - BLOCK * o]
                )
                scored[kb] = b
                peak = b if peak is None else jnp.maximum(peak, b)
            peak = jnp.max(peak, axis=0, keepdims=True)
            for kb in range(blocks):
                if kb in scored:
                    e = jnp.exp(scored[kb] - peak).astype(BF16)
                else:
                    e = jnp.zeros((BLOCK, BLOCK), BF16)
                u_ref[0, h, BLOCK * kb : BLOCK * kb + BLOCK, BLOCK * qb : BLOCK * qb + BLOCK] = e

    def mix(h, s):
        ot = dot(v_aug[h], u_ref[0, h, :, 256 * s : 256 * s + 256])
        r = 1.0 / ot[64:65]
        s_ref[0, h : h + 1, 256 * s : 256 * s + 256] = r
        return ot[:64] * r

    units = [(h, s) for h in range(2) for s in range(blocks // 2)]
    made = {}
    ahead = score(*units[0])
    for i, unit in enumerate(units):
        st = ahead
        if i + 1 < len(units):
            ahead = score(*units[i + 1])
        weigh(*unit, st)
        if i > 0:
            made[units[i - 1]] = mix(*units[i - 1])
    made[units[-1]] = mix(*units[-1])
    outs = [
        jnp.concatenate([made[h, s] for s in range(blocks // 2)], axis=1) for h in range(2)
    ]
    o_t = jnp.concatenate(outs, axis=0)
    o_ref[...] = o_t.T.astype(BF16)
    ot_ref[...] = o_t.astype(BF16)


def pair_spec(length, per_group, first):
    return pl.BlockSpec(
        (None, length, 3 * BLOCK),
        lambda p, r: ((first + p) // per_group, r, (first + p) % per_group),
    )


def attend(first, count, pairs, rows, length, proj, kseg, qseg, bias, made):
    steps = rows * pairs
    args = [far(proj), kseg, qseg, bias]
    specs = [
        pair_spec(length, pairs // proj.shape[0], first),
        pl.BlockSpec((length, BLOCK), lambda p, r: (r, 0)),
        pl.BlockSpec((length, BLOCK), lambda p, r: (r, 0)),
        pl.BlockSpec((1, 2, WIDE), lambda p, r: (r * pairs + first + p, 0, 0)),
    ]
    alias = {}
    if made is not None:
        alias = {len(args) + i: i for i in range(4)}
        args += [far(made[0]), made[1], made[2], made[3]]
        specs += [pl.BlockSpec(memory_space=pl.ANY)] * 4
    return pl.pallas_call(
        attend_body,
        grid=(count, rows),
        in_specs=specs,
        out_specs=[
            pl.BlockSpec((1, 2, length, length), lambda p, r: ((first + p) * rows + r, 0, 0, 0)),
            pl.BlockSpec((1, 2, length), lambda p, r: ((first + p) * rows + r, 0, 0)),
            pl.BlockSpec((length, BLOCK), lambda p, r: (r, first + p)),
            pl.BlockSpec((BLOCK, length), lambda p, r: (first + p, r)),
        ],
        out_shape=[
            pltpu.HBM((steps, 2, length, length), BF16),
            jax.ShapeDtypeStruct((steps, 2, length), F32),
            jax.ShapeDtypeStruct((rows * length, pairs * BLOCK), BF16),
            jax.ShapeDtypeStruct((pairs * BLOCK, rows * length), BF16),
        ],
        input_output_aliases=alias,
        compiler_params=pltpu.CompilerParams(vmem_limit_bytes=16 * 1024 * 1024),
        cost_estimate=brief,
        name="attend",
    )(*args)


def attend_grad_body(
    place_ref, p_ref, u_ref, s_ref, o_ref, g_ref, mine_ref, theirs_ref, *refs
):
    dp_ref, df_ref, go_ref, gx_ref, ds_ref, acc_ref = refs[-6:]
    length = p_ref.shape[0]
    blocks = length // BLOCK
    lane = lax.broadcasted_iota(jnp.int32, (length, BLOCK), 1)
    q = p_ref[:, :BLOCK] * BF16(0.125)
    k = p_ref[:, BLOCK : 2 * BLOCK]
    v = p_ref[:, 2 * BLOCK :]
    k_t = k.astype(F32).T.astype(BF16)
    inv = jnp.concatenate(
        [jnp.broadcast_to(s_ref[0, h : h + 1, :], (64, length)) for h in range(2)], axis=0
    ).T
    g = g_ref[...].astype(F32) * inv
    prod = g * o_ref[...].astype(F32)
    g_low = g.astype(BF16)
    prod_hi = prod.astype(BF16)
    prod_lo = (prod - prod_hi.astype(F32)).astype(BF16)
    row = lax.broadcasted_iota(jnp.int32, (2 * BLOCK, BLOCK), 0)
    col = lax.broadcasted_iota(jnp.int32, (2 * BLOCK, BLOCK), 1)
    pick = jnp.where((((row // 64) % 2) == (col // 2)) & (col < 4), -1.0, 0.0).astype(BF16)
    centre = dot(jnp.concatenate([prod_hi, prod_lo], axis=1), pick)
    centre_hi = centre.astype(BF16)
    centre_lo = (centre - centre_hi.astype(F32)).astype(BF16)
    g_aug = jnp.concatenate([g_low, jnp.where(lane % 2 == 0, centre_hi, centre_lo)], axis=1)
    zero = BF16(0)
    mine = [(lane >= 64) == (h == 1) for h in range(2)]
    v_aug = [
        jnp.concatenate(
            [jnp.where(mine[h], v, zero), jnp.where((lane // 2) == h, BF16(1), zero)], axis=1
        )
        for h in range(2)
    ]
    diag = [[None] * (2 * REACH + 1) for _ in range(2)]
    dq_t, dv, dk = [], [], []

    def score(h, s):
        return dot(v_aug[h], g_aug[256 * s : 256 * s + 256], CONTRACT_LANES)

    def weigh(h, s, dp):
        for half in range(2):
            qb = 2 * s + half
            for kb in range(blocks):
                o = kb - qb
                krows = slice(BLOCK * kb, BLOCK * kb + BLOCK)
                qcols = slice(BLOCK * qb, BLOCK * qb + BLOCK)
                if abs(o) > REACH:
                    ds_ref[h, krows, qcols] = jnp.zeros((BLOCK, BLOCK), BF16)
                    continue
                ds = (
                    u_ref[0, h, krows, qcols].astype(F32)
                    * dp[krows, BLOCK * half : BLOCK * half + BLOCK]
                )
                ds_ref[h, krows, qcols] = ds.astype(BF16)
                d = diag[h][o + REACH]
                diag[h][o + REACH] = ds if d is None else d + ds

    def values(h):
        dv.append(dot(u_ref[0, h], jnp.where(mine[h], g_low, zero)))

    def keys(h):
        dk.append(dot(ds_ref[h], jnp.where(mine[h], q, zero)))

    def queries(h):
        dq_t.append(dot(k_t[64 * h : 64 * h + 64], ds_ref[h]))

    def offsets(h):
        wide = jnp.concatenate([jnp.zeros((BLOCK, BLOCK), F32)] + diag[h][::-1], axis=1)
        step = BLOCK // 2
        while step:
            wide = wide[:step] + pltpu.roll(wide[step:], WIDE - step, 1)
            step //= 2
        df_ref[0, h : h + 1, :] = wide

    strips = range(blocks // 2)
    dps = [[score(h, s) for s in strips] for h in range(2)]
    values(0)
    for s in strips:
        weigh(0, s, dps[0][s])
    values(1)
    keys(0)
    queries(0)
    for s in strips:
        weigh(1, s, dps[1][s])
    offsets(0)
    keys(1)
    queries(1)
    offsets(1)
    dv = dv[0] + dv[1]
    dk = dk[0] + dk[1]
    dq = jnp.concatenate(dq_t, axis=0).T * 0.125
    d_all = jnp.concatenate([dq.astype(BF16), dk.astype(BF16), dv.astype(BF16)], axis=1)
    dp_ref[...] = d_all
    half = mine_ref.shape[0]
    row_step = pl.program_id(1)
    add = dot(jnp.concatenate([mine_ref[...], theirs_ref[...]], axis=0), d_all)

    @pl.when(row_step == 0)
    def _():
        acc_ref[...] = add

    @pl.when(row_step != 0)
    def _():
        acc_ref[...] += add

    @pl.when(row_step == pl.num_programs(1) - 1)
    def _():
        go_ref[...] = acc_ref[:half].astype(BF16)
        gx_ref[...] = acc_ref[half:].astype(BF16)


def attend_grad(
    net, first, count, pairs, rows, length, proj, made, grad_mixed, normed_t, cols, buffers, at
):
    saved, inverse, mixed, _ = made
    steps = rows * count
    half = normed_t.shape[0] // 2
    wide = 3 * BLOCK
    args = [far(proj), far(saved), inverse, mixed, grad_mixed, far(normed_t), far(normed_t)]
    specs = [
        pl.BlockSpec(
            (None, length, wide),
            lambda p, r, w, per=pairs // proj.shape[0]: ((first + p) // per, r, (first + p) % per),
        ),
        pl.BlockSpec((1, 2, length, length), lambda p, r, w: ((first + p) * rows + r, 0, 0, 0)),
        pl.BlockSpec((1, 2, length), lambda p, r, w: ((first + p) * rows + r, 0, 0)),
        pl.BlockSpec((length, BLOCK), lambda p, r, w: (r, first + p)),
        pl.BlockSpec((length, BLOCK), lambda p, r, w: (r, first + p)),
        pl.BlockSpec((half, length), lambda p, r, w: (w[3], r)),
        pl.BlockSpec((half, length), lambda p, r, w: (1 - w[3], r)),
    ]
    alias = {}
    if buffers is not None:
        alias = {1 + len(args) + i: 2 + i for i in range(2)}
        args += [far(b) for b in buffers]
        specs += [pl.BlockSpec(memory_space=pl.ANY)] * 2
    g_spec = pl.BlockSpec((half, wide), lambda p, r, w: (0, at // wide + p))
    return pl.pallas_call(
        attend_grad_body,
        grid_spec=pltpu.PrefetchScalarGridSpec(
            num_scalar_prefetch=1,
            grid=(count, rows),
            in_specs=specs,
            out_specs=[
                pl.BlockSpec((length, wide), lambda p, r, w: (r, p)),
                pl.BlockSpec((1, 2, WIDE), lambda p, r, w: (p * rows + r, 0, 0)),
                g_spec,
                g_spec,
            ],
            scratch_shapes=[
                pltpu.VMEM((2, length, length), BF16),
                pltpu.VMEM((2 * half, wide), F32),
            ],
        ),
        out_shape=[
            pltpu.HBM((rows * length, count * wide), BF16),
            jax.ShapeDtypeStruct((steps, 2, WIDE), F32),
            pltpu.HBM((half, cols), BF16),
            pltpu.HBM((half, cols), BF16),
        ],
        input_output_aliases=alias,
        compiler_params=pltpu.CompilerParams(vmem_limit_bytes=24 * 1024 * 1024),
        cost_estimate=brief,
        name="attend_grad",
    )(net.places(), *args)


def pick(options, index):
    out = options[0]
    for k in range(1, len(options)):
        out = jnp.where(index == k, options[k], out)
    return out


def by_distance(slices, at):
    n = len(slices)
    return [pick(slices, lax.rem(at - t + n, n)) for t in range(n)]


def in_order(pieces, at):
    n = len(pieces)
    return [pick(pieces, lax.rem(at - k + n, n)) for k in range(n)]


def by_flip(slices, at):
    return [pick(slices, lax.bitwise_xor(at, k)) for k in range(len(slices))]


def cut_rows(v, n):
    size = v.shape[0] // n
    return [v[size * k : size * k + size] for k in range(n)]


def cut_lanes(v, n):
    size = v.shape[-1] // n
    return [v[..., size * k : size * k + size] for k in range(n)]


def total(parts):
    out = parts[0].astype(F32)
    for p in parts[1:]:
        out = out + p.astype(F32)
    return out


class Links:
    def __init__(self, ma, an, width):
        z = min(4, an // 2)
        self.an = an
        self.size = {"y": ma, "z": z, "x": an // (2 * z), "c": 2}
        self.stride = {"c": 1, "x": 2, "z": 2 * self.size["x"]}
        self.tidy = width % (ma * BLOCK) == 0 and width % (8 * ma * an) == 0

    def places(self):
        an = lax.axis_index("an")
        found = [lax.axis_index("ma")]
        found += [(an // self.stride[a]) % self.size[a] for a in ("z", "x", "c")]
        return jnp.stack([f.astype(jnp.int32) for f in found])

    def fetch(self, value, axis, back):
        n = self.size[axis]
        if axis == "y":
            return lax.ppermute(value, "ma", [(i, (i + back) % n) for i in range(n)])
        s = self.stride[axis]
        pairs = []
        for i in range(self.an):
            at = (i // s) % n
            pairs.append((i, i + ((at + back) % n - at) * s))
        return lax.ppermute(value, "an", pairs)

    def flip(self, value, axis, bits):
        s = self.stride[axis]
        pairs = []
        for i in range(self.an):
            at = (i // s) % self.size[axis]
            pairs.append((i, i + ((at ^ bits) - at) * s))
        return lax.ppermute(value, "an", pairs)

    def gather(self, value, axis):
        return [value] + [self.fetch(value, axis, t) for t in range(1, self.size[axis])]

    def spread(self, parts, axis):
        n = self.size[axis]
        return [parts[0]] + [self.fetch(parts[t], axis, n - t) for t in range(1, n)]

    def step(self, fn, arrays, shapes, name, along, steps=1, away=False):
        arrays, along = hold((list(arrays), along))
        return hold((self.stage(fn, arrays, shapes, name, steps, away), along))

    def stage(self, fn, arrays, shapes, name, steps, away):
        outs = [jax.ShapeDtypeStruct(s, BF16) for s in shapes]
        place = self.places()
        if not self.tidy:
            got = fn(*[place[i] for i in range(4)], *arrays)
            return [g.astype(BF16).reshape(o.shape) for g, o in zip(got, outs)]
        count = len(arrays)

        def body(place_ref, *refs):
            got = fn(*[place_ref[i] for i in range(4)], *[r[...] for r in refs[:count]])
            for g, r in zip(got, refs[count:]):
                r[...] = g.astype(BF16)

        def spec(a):
            rest = len(a.shape) - 1
            return pl.BlockSpec(
                (a.shape[0] // steps,) + a.shape[1:], lambda i, p, rest=rest: (i,) + (0,) * rest
            )

        return pl.pallas_call(
            body,
            grid_spec=pltpu.PrefetchScalarGridSpec(
                num_scalar_prefetch=1,
                grid=(steps,),
                in_specs=[spec(a) for a in arrays],
                out_specs=[spec(o) for o in outs],
            ),
            out_shape=[pltpu.HBM(o.shape, o.dtype) for o in outs] if away else outs,
            compiler_params=pltpu.CompilerParams(vmem_limit_bytes=16 * 1024 * 1024),
            cost_estimate=brief,
            name=name,
        )(place, *arrays)


def gather_1(net, pieces, along):
    rows, cols = pieces[0].shape
    half = rows // 2
    n = len(pieces)

    def fn(y, z, x, c, *pieces):
        v = jnp.stack(in_order(pieces, z))
        return [v[:, :half], v[:, half:]]

    (a, b), along = net.step(fn, pieces, [(n, half, cols)] * 2, "gather_z", along)
    return (net.gather(a, "x"), net.gather(b, "y")), along


def gather_2(net, state, along):
    a, b = state
    n, half, cols = a[0].shape

    def fn(y, z, x, c, *parts):
        a_in = in_order(parts[: len(a)], x)
        b_in = in_order(parts[len(a) :], y)
        return [jnp.stack(a_in, axis=1), jnp.concatenate(b_in, axis=-1)]

    (a, b), along = net.step(
        fn, a + b, [(n, len(a), half, cols), (n, half, cols * len(b))], "gather_xy", along
    )
    return (net.gather(a, "y"), net.gather(b, "x")), along


def gather_3(net, state, along):
    a, b = state
    n, nx, half, cols = a[0].shape

    def fn(y, z, x, c, *parts):
        a_in = jnp.concatenate(in_order(parts[: len(a)], y), axis=-1)
        b_in = jnp.stack(in_order(parts[len(a) :], x), axis=1)
        return [jnp.concatenate([a_in, b_in], axis=2)]

    shape = (n, nx, 2 * half, cols * len(a))
    (own,), along = net.step(fn, a + b, [shape], "gather_yx", along, steps=n if net.tidy else 1)
    return net.gather(own, "c"), along


def scatter_1(net, own, theirs, along):
    nz, two, nx, hb, width = own.shape
    half = hb // 2
    ny = net.size["y"]

    def fn(y, z, x, c, own, theirs):
        v = total([own, theirs])
        a, b = v[..., :half, :], v[..., half:, :]
        return by_distance(cut_lanes(a, ny), y) + by_distance([b[:, :, k] for k in range(nx)], x)

    shapes = [(nz, two, nx, half, width // ny)] * ny + [(nz, two, half, width)] * nx
    parts, along = net.step(
        fn, [own, theirs], shapes, "scatter_yx", along, steps=nz if net.tidy else 1
    )
    return (net.spread(parts[:ny], "y"), net.spread(parts[ny:], "x")), along


def scatter_2(net, state, along):
    a, b = state
    nz, two, nx, half, cols = a[0].shape
    ny = net.size["y"]

    def fn(y, z, x, c, *parts):
        va, vb = total(parts[:ny]), total(parts[ny:])
        return by_distance([va[:, :, k] for k in range(nx)], x) + by_distance(cut_lanes(vb, ny), y)

    shapes = [(nz, two, half, cols)] * (nx + ny)
    parts, along = net.step(fn, a + b, shapes, "scatter_xy", along)
    return (net.spread(parts[:nx], "x"), net.spread(parts[nx:], "y")), along


def scatter_3(net, state, along):
    a, b = state
    nz, two, half, cols = a[0].shape

    def fn(y, z, x, c, *parts):
        v = jnp.concatenate([total(parts[: len(a)]), total(parts[len(a) :])], axis=2)
        return halves([v[k] for k in range(nz)], z)

    parts, along = net.step(fn, a + b, [(nz // 2, two, 2 * half, cols)] * 2, "scatter_z", along)
    return (parts[0], net.flip(parts[1], "z", 1)), along


def halves(slices, at):
    p = by_flip(slices, at)
    return [jnp.stack([p[0], p[2]]), jnp.stack([p[1], p[3]])]


def fold_z(net, state, along):
    kept, got = state

    def fn(y, z, x, c, kept, got):
        v = total([kept, got])
        return [v[0], v[1]]

    parts, along = net.step(fn, [kept, got], [kept.shape[1:]] * 2, "fold_z", along)
    return [parts[0], net.flip(parts[1], "z", 2)], along


def reduce_1(net, own, theirs, cut, along, away):
    rows, cols = own.shape
    ny, nx = net.size["y"], net.size["x"]

    def fn(y, z, x, c, own, theirs):
        v = total([own, theirs])
        return by_distance(cut_rows(v[:, :cut], ny), y) + by_distance(cut_rows(v[:, cut:], nx), x)

    shapes = [(rows // ny, cut)] * ny + [(rows // nx, cols - cut)] * nx
    parts, along = net.step(fn, [own, theirs], shapes, "reduce_yx", along, away=away)
    return (net.spread(parts[:ny], "y"), net.spread(parts[ny:], "x")), along


def reduce_2(net, state, along, away):
    a, b = state
    ny, nx = net.size["y"], net.size["x"]

    def fn(y, z, x, c, *parts):
        va, vb = total(parts[: len(a)]), total(parts[len(a) :])
        return by_distance(cut_rows(va, nx), x) + by_distance(cut_rows(vb, ny), y)

    shapes = [(a[0].shape[0] // nx, a[0].shape[1])] * nx
    shapes += [(b[0].shape[0] // ny, b[0].shape[1])] * ny
    parts, along = net.step(fn, a + b, shapes, "reduce_xy", along, away=away)
    return (net.spread(parts[:nx], "x"), net.spread(parts[nx:], "y")), along


def reduce_3(net, state, along):
    a, b = state
    n = net.size["z"]

    def fn(y, z, x, c, *parts):
        v = jnp.concatenate([total(parts[: len(a)]), total(parts[len(a) :])], axis=1)
        return halves(cut_rows(v, n), z)

    shape = (n // 2, a[0].shape[0] // n, a[0].shape[1] + b[0].shape[1])
    parts, along = net.step(fn, a + b, [shape] * 2, "reduce_z", along)
    return (parts[0], net.flip(parts[1], "z", 1)), along


def spread_0(net, parts, along):
    def fn(y, z, x, c, *parts):
        return [total(parts)]

    (front,), along = net.step(fn, parts, [parts[0].shape], "spread_sum", along)
    return [front, net.flip(front, "z", 2)], along


def spread_z(net, pieces, along):
    def fn(y, z, x, c, *pieces):
        return [jnp.stack(pieces)]

    (pair,), along = net.step(fn, pieces, [(2,) + pieces[0].shape], "spread_pair", along)
    return [pair, net.flip(pair, "z", 1)], along


def spread_1(net, pairs, cut, along):
    _, rows, cols = pairs[0].shape

    def fn(y, z, x, c, *pairs):
        found = [p[k].astype(F32) for k in range(2) for p in pairs]
        v = jnp.concatenate(by_flip(found, z), axis=0)
        return [v[:, :cut], v[:, cut:]]

    shapes = [(4 * rows, cut), (4 * rows, cols - cut)]
    (a, b), along = net.step(fn, pairs, shapes, "spread_z", along)
    return (net.gather(a, "x"), net.gather(b, "y")), along


def spread_2(net, state, along):
    a, b = state

    def fn(y, z, x, c, *parts):
        va = jnp.concatenate(in_order(parts[: len(a)], x), axis=0)
        vb = jnp.concatenate(in_order(parts[len(a) :], y), axis=0)
        return [va, vb]

    shapes = [(len(p) * p[0].shape[0], p[0].shape[1]) for p in (a, b)]
    (a, b), along = net.step(fn, a + b, shapes, "spread_xy", along)
    return (net.gather(a, "y"), net.gather(b, "x")), along


def spread_3(net, state, along):
    a, b = state

    def fn(y, z, x, c, *parts):
        va = jnp.concatenate(in_order(parts[: len(a)], y), axis=0)
        vb = jnp.concatenate(in_order(parts[len(a) :], x), axis=0)
        return [jnp.concatenate([va, vb], axis=1)]

    shape = (len(a) * a[0].shape[0], a[0].shape[1] + b[0].shape[1])
    (v,), along = net.step(fn, a + b, [shape], "spread_yx", along)
    return net.gather(v, "c"), along


def finish(net, value, rel, cuts, weights, gain, width, heads_from, into, so_far):
    half, cols = value.shape
    tile = BLOCK
    steps = half // tile
    widths = [sum(b - a for a, b in runs) for runs in cuts]
    narrow = widths[3] == BLOCK

    def body(place_ref, v_ref, wq_ref, wk_ref, wv_ref, gain_ref, *refs):
        outs = refs[-5:]
        v = v_ref[...].astype(F32)
        made = [jnp.concatenate([v[:, a:b] for a, b in runs], axis=1) for runs in cuts]
        for k, (out, m) in enumerate(zip(outs, made)):
            out[...] = m.T[:8] if k == 3 and narrow else m
        acc = made[0] * wq_ref[...].astype(F32)
        acc = acc + made[1] * wk_ref[...].astype(F32) + made[2] * wv_ref[...].astype(F32)
        part = jnp.broadcast_to(jnp.sum(acc, axis=1, keepdims=True), (tile, BLOCK)).T[:1]
        part = part / gain_ref[...]
        outs[4][...] = part if so_far is None else part + refs[0][...]

    def row(i, p):
        return (p[3] if rel == 0 else 1 - p[3]) * steps + i

    def cols_spec(w, at):
        return pl.BlockSpec((tile, w), lambda i, p: (row(i, p), at // w))

    def lanes_spec(rows):
        return pl.BlockSpec((rows, tile), lambda i, p: (0, row(i, p)))

    args = [value, *[far(w) for w in weights], gain.reshape(1, -1)]
    specs = [pl.BlockSpec((tile, cols), lambda i, p: (i, 0))]
    specs += [cols_spec(widths[0], heads_from)] * 3 + [lanes_spec(1)]
    alias = {}
    if so_far is not None:
        args.append(so_far)
        specs.append(lanes_spec(1))
    if into:
        alias = {1 + len(args) + k: k for k in range(len(into))}
        args += list(into)
        specs += [pl.BlockSpec(memory_space=pl.ANY)] * len(into)
    return pl.pallas_call(
        body,
        grid_spec=pltpu.PrefetchScalarGridSpec(
            num_scalar_prefetch=1,
            grid=(steps,),
            in_specs=specs,
            out_specs=[cols_spec(w, heads_from) for w in widths[:3]]
            + [lanes_spec(8) if narrow else cols_spec(widths[3], 0), lanes_spec(1)],
        ),
        out_shape=[pltpu.HBM((2 * half, width), F32)] * 3
        + [
            jax.ShapeDtypeStruct((8, 2 * half), F32) if narrow else pltpu.HBM((2 * half, width), F32),
            jax.ShapeDtypeStruct((1, 2 * half), F32),
        ],
        input_output_aliases=alias,
        compiler_params=pltpu.CompilerParams(vmem_limit_bytes=20 * 1024 * 1024),
        cost_estimate=brief,
        name="finish",
    )(net.places(), *args)


def project(tokens, gain, weights, groups):
    count, width = tokens.shape
    tile = min(256, count)
    pairs_here = width // BLOCK // groups

    def body(t_ref, gain_ref, *refs):
        out, nt_ref = refs[-2:]
        x = t_ref[...].astype(F32)
        inv = lax.rsqrt(jnp.mean(x * x, axis=1, keepdims=True) + epsilon)
        normed = x * inv * gain_ref[...]
        low = normed.astype(BF16)
        nt_ref[...] = normed.T.astype(BF16)
        for i, w in enumerate(refs[:-2]):
            r = dot(low, w[...]).astype(BF16)
            for p in range(groups * pairs_here):
                at = (3 * (p % pairs_here) + i) * BLOCK
                out[p // pairs_here, :, at : at + BLOCK] = r[:, BLOCK * p : BLOCK * p + BLOCK]

    return pl.pallas_call(
        body,
        grid=(count // tile,),
        in_specs=[
            pl.BlockSpec((tile, width), lambda i: (i, 0)),
            pl.BlockSpec((1, width), lambda i: (0, 0)),
        ]
        + [pl.BlockSpec((width, width), lambda i: (0, 0))] * 3,
        out_specs=[
            pl.BlockSpec((groups, tile, 3 * width // groups), lambda i: (0, i, 0)),
            pl.BlockSpec((width, tile), lambda i: (0, i)),
        ],
        out_shape=[
            pltpu.HBM((groups, count, 3 * width // groups), BF16),
            pltpu.HBM((width, count), BF16),
        ],
        compiler_params=pltpu.CompilerParams(vmem_limit_bytes=24 * 1024 * 1024),
        cost_estimate=brief,
        name="project",
    )(far(tokens), gain.reshape(1, -1), *[far(w) for w in weights])


def gelu_parts(pre):
    k0 = 0.7978845608028654
    k1 = 0.044715
    sq = pre * pre
    s = 0.5 * jnp.tanh(pre * (k0 + (k0 * k1) * sq)) + 0.5
    act = pre * s
    slope = s + (act - act * s) * (2.0 * k0 + (6.0 * k0 * k1) * sq)
    return act, slope


def before_ffn(mixed, w_out, tokens, gain, g):
    count, width = mixed.shape
    tile = min(256, count)

    def body(mixed_ref, w_ref, t_ref, gain_ref, g_ref, mid_ref, s_ref, st_ref, gt_ref):
        mid = t_ref[...].astype(F32) + dot(mixed_ref[...], w_ref[...])
        inv = lax.rsqrt(jnp.mean(mid * mid, axis=1, keepdims=True) + epsilon)
        second = mid * inv * gain_ref[...]
        mid_ref[...] = mid.astype(BF16)
        s_ref[...] = second.astype(BF16)
        st_ref[...] = second.T.astype(BF16)
        gt_ref[...] = g_ref[...].astype(F32).T.astype(BF16)

    def rows_of(w):
        return pl.BlockSpec((tile, w), lambda i: (i, 0))

    cols = pl.BlockSpec((width, tile), lambda i: (0, i))
    return pl.pallas_call(
        body,
        grid=(count // tile,),
        in_specs=[
            rows_of(width),
            pl.BlockSpec((width, width), lambda i: (0, 0)),
            rows_of(width),
            pl.BlockSpec((1, width), lambda i: (0, 0)),
            rows_of(width),
        ],
        out_specs=[rows_of(width), rows_of(width), cols, cols],
        out_shape=[
            pltpu.HBM((count, width), BF16),
            pltpu.HBM((count, width), BF16),
            pltpu.HBM((width, count), BF16),
            pltpu.HBM((width, count), BF16),
        ],
        compiler_params=pltpu.CompilerParams(vmem_limit_bytes=20 * 1024 * 1024),
        cost_estimate=brief,
        name="before_ffn",
    )(mixed, far(w_out), far(tokens), gain.reshape(1, -1), far(g))


def ffn(net, ups, downs, second, second_t, g, g_t, middle):
    nz, nx, hb, width = ups[0].shape
    count = g.shape[0]
    part = nx * hb
    tile = 256 if count % 256 == 0 else count
    lanes = 256 if width % 256 == 0 else width

    def body(
        place_ref, u0_ref, u1_ref, d0_ref, d1_ref, st_far, gt_far, g_far, s_far, m_far,
        out_ref, go_ref, gx_ref, gs_ref, act_ref, gu_ref, acc_ref, gsum_ref,
        st_ref, gt_ref, g_ref, s_ref, m_ref, sems,
    ):
        step = pl.program_id(0)
        st_copy, gt_copy, g_copy, s_copy, m_copy = [
            pltpu.make_async_copy(a, b, sems.at[i])
            for i, (a, b) in enumerate(
                (
                    (st_far, st_ref),
                    (gt_far, gt_ref),
                    (g_far, g_ref),
                    (s_far, s_ref),
                    (m_far, m_ref),
                )
            )
        ]

        @pl.when(step == 0)
        def _():
            for copy in (st_copy, gt_copy, g_copy, s_copy, m_copy):
                copy.start()
            st_copy.wait()
            gt_copy.wait()

        up_all, down_all = [
            jnp.concatenate([r[...].reshape(part, width) for r in refs], axis=0)
            for refs in ((u0_ref, u1_ref), (d0_ref, d1_ref))
        ]
        starts = list(range(0, count, tile))

        def both(t):
            return dot(up_all, st_ref[:, t : t + tile]), dot(down_all, gt_ref[:, t : t + tile])

        @pl.when(step == 0)
        def _():
            acc_ref[...] = jnp.zeros_like(acc_ref)
            gsum_ref[...] = jnp.zeros_like(gsum_ref)

        def sums(t):
            at = slice(t, t + tile)
            acc_ref[at] += dot(act_ref[:, at], down_all, CONTRACT_ROWS)
            gsum_ref[at] += dot(gu_ref[:, at], up_all, CONTRACT_ROWS)

        ahead = both(starts[0])
        for n, t in enumerate(starts):
            pre, gh = ahead
            if n + 1 < len(starts):
                ahead = both(starts[n + 1])
            act, slope = gelu_parts(pre)
            act_ref[:, t : t + tile] = act.astype(BF16)
            gu_ref[:, t : t + tile] = (gh * slope).astype(BF16)
            if n > 0:
                sums(starts[n - 1])
        sums(starts[-1])

        @pl.when(step == 0)
        def _():
            g_copy.wait()
            s_copy.wait()

        for k in range(0, width, lanes):
            cols = slice(k, k + lanes)
            gd = dot(act_ref[...], g_ref[:, cols]).astype(BF16)
            gu = dot(gu_ref[...], s_ref[:, cols]).astype(BF16)
            for rel in range(2):
                for i in range(nx):
                    at = part * rel + hb * i
                    out = (go_ref, gx_ref)[rel]
                    out[0, i, :, cols] = gd[at : at + hb]
                    out[1, i, :, cols] = gu[at : at + hb]

        @pl.when(step == nz - 1)
        def _():
            m_copy.wait()
            out_ref[...] = (m_ref[...].astype(F32) + acc_ref[...]).astype(BF16)
            gs_ref[...] = gsum_ref[...].astype(BF16)

    away = pl.BlockSpec(memory_space=pltpu.HBM)

    one = pl.BlockSpec((None, nx, hb, width), lambda i, p: (i, 0, 0, 0))
    two = pl.BlockSpec((None, 2, nx, hb, width), lambda i, p: (i, 0, 0, 0, 0))
    flat = pl.BlockSpec((count, width), lambda i, p: (0, 0))
    return pl.pallas_call(
        body,
        grid_spec=pltpu.PrefetchScalarGridSpec(
            num_scalar_prefetch=1,
            grid=(nz,),
            in_specs=[one] * 4 + [away] * 5,
            out_specs=[flat, two, two, flat],
            scratch_shapes=[
                pltpu.VMEM((2 * part, count), BF16),
                pltpu.VMEM((2 * part, count), BF16),
                pltpu.VMEM((count, width), F32),
                pltpu.VMEM((count, width), F32),
                pltpu.VMEM((width, count), BF16),
                pltpu.VMEM((width, count), BF16),
                pltpu.VMEM((count, width), BF16),
                pltpu.VMEM((count, width), BF16),
                pltpu.VMEM((count, width), BF16),
                pltpu.SemaphoreType.DMA((5,)),
            ],
        ),
        out_shape=[
            pltpu.HBM((count, width), BF16),
            pltpu.HBM((nz, 2, nx, hb, width), BF16),
            pltpu.HBM((nz, 2, nx, hb, width), BF16),
            pltpu.HBM((count, width), BF16),
        ],
        compiler_params=pltpu.CompilerParams(vmem_limit_bytes=42 * 1024 * 1024),
        cost_estimate=brief,
        name="ffn",
    )(net.places(), *ups, *downs, *[far(v) for v in (second_t, g_t, g, second, middle)])


def after_ffn(net, grad_second, middle, gain, g, w_out, mixed_t, cols):
    count, width = middle.shape
    half = width // 2
    tile = min(512, count)

    def body(
        place_ref, gs_ref, m_ref, gain_ref, g_ref, w_ref, mine_ref, theirs_ref,
        gm_ref, gx_ref, gg_ref, wo_ref, wx_ref, acc_ref,
    ):
        gs = gs_ref[...].astype(F32)
        m = m_ref[...].astype(F32)
        r = lax.rsqrt(jnp.mean(m * m, axis=1, keepdims=True) + epsilon)
        scaled = gs * gain_ref[...]
        mean = jnp.mean(scaled * m, axis=1, keepdims=True)
        gm = g_ref[...].astype(F32) + r * scaled - m * (r * r * r * mean)
        ga = gm.astype(BF16)
        gm_ref[...] = ga
        gx_ref[...] = dot(ga, w_ref[...], CONTRACT_LANES).astype(BF16)
        add = jnp.sum(gs * (m * r), axis=0, keepdims=True)
        step = pl.program_id(0)

        @pl.when(step == 0)
        def _():
            gg_ref[...] = add

        @pl.when(step != 0)
        def _():
            gg_ref[...] += add

        add_o = dot(jnp.concatenate([mine_ref[...], theirs_ref[...]], axis=0), ga)

        @pl.when(step == 0)
        def _():
            acc_ref[...] = add_o

        @pl.when(step != 0)
        def _():
            acc_ref[...] += add_o

        @pl.when(step == pl.num_programs(0) - 1)
        def _():
            wo_ref[...] = acc_ref[:half].astype(BF16)
            wx_ref[...] = acc_ref[half:].astype(BF16)

    def rows_of(w):
        return pl.BlockSpec((tile, w), lambda i, p: (i, 0))

    row = pl.BlockSpec((1, width), lambda i, p: (0, 0))
    grad = pl.BlockSpec((half, width), lambda i, p: (0, 0))
    return pl.pallas_call(
        body,
        grid_spec=pltpu.PrefetchScalarGridSpec(
            num_scalar_prefetch=1,
            grid=(count // tile,),
            in_specs=[
                rows_of(width),
                rows_of(width),
                row,
                rows_of(width),
                pl.BlockSpec((width, width), lambda i, p: (0, 0)),
                pl.BlockSpec((half, tile), lambda i, p: (p[3], i)),
                pl.BlockSpec((half, tile), lambda i, p: (1 - p[3], i)),
            ],
            out_specs=[rows_of(width), rows_of(width), row, grad, grad],
            scratch_shapes=[pltpu.VMEM((width, width), F32)],
        ),
        out_shape=[
            pltpu.HBM((count, width), BF16),
            jax.ShapeDtypeStruct((count, width), BF16),
            jax.ShapeDtypeStruct((1, width), F32),
            pltpu.HBM((half, cols), BF16),
            pltpu.HBM((half, cols), BF16),
        ],
        compiler_params=pltpu.CompilerParams(vmem_limit_bytes=24 * 1024 * 1024),
        cost_estimate=brief,
        name="after_ffn",
    )(net.places(), far(grad_second), far(middle), gain.reshape(1, -1), far(g), far(w_out), mixed_t, mixed_t)


def token_grad(dproj, weights, tokens, gain, grad_middle):
    count, width = tokens.shape
    tile = min(256, count)

    def body(*refs):
        d_refs = refs[: len(dproj)]
        w_refs = refs[len(dproj) : len(dproj) + 3]
        t_ref, gain_ref, gm_ref, out_ref = refs[len(dproj) + 3 :]
        gn = None
        for i, w in enumerate(w_refs):
            cols = []
            for d in d_refs:
                for p in range(d.shape[1] // (3 * BLOCK)):
                    at = (3 * p + i) * BLOCK
                    cols.append(d[:, at : at + BLOCK])
            r = dot(jnp.concatenate(cols, axis=1), w[...], CONTRACT_LANES)
            gn = r if gn is None else gn + r
        scaled = gn * gain_ref[...]
        x = t_ref[...].astype(F32)
        r = lax.rsqrt(jnp.mean(x * x, axis=1, keepdims=True) + epsilon)
        mean = jnp.mean(scaled * x, axis=1, keepdims=True)
        out_ref[...] = gm_ref[...].astype(F32) + r * scaled - x * (r * r * r * mean)

    def rows_of(w):
        return pl.BlockSpec((tile, w), lambda i: (i, 0))

    return pl.pallas_call(
        body,
        grid=(count // tile,),
        in_specs=[rows_of(d.shape[1]) for d in dproj]
        + [pl.BlockSpec(w.shape, lambda i: (0, 0)) for w in weights]
        + [rows_of(width), pl.BlockSpec((1, width), lambda i: (0, 0)), rows_of(width)],
        out_specs=rows_of(width),
        out_shape=pltpu.HBM((count, width), F32),
        compiler_params=pltpu.CompilerParams(vmem_limit_bytes=20 * 1024 * 1024),
        cost_estimate=brief,
        name="token_grad",
    )(*[far(d) for d in dproj], *[far(w) for w in weights], far(tokens), gain.reshape(1, -1), far(grad_middle))


def local(
    net,
    tokens,
    tasks,
    segments,
    buckets,
    w_query,
    w_key,
    w_value,
    w_out,
    w_up,
    w_down,
    bias_table,
    gain_attn,
    gain_ffn,
    cotangent,
):
    rows, length, width = tokens.shape
    groups, bucket_count, heads = bias_table.shape
    pairs = heads // 2
    count = rows * length
    parts = 3
    part = pairs // parts

    up_state = net.gather(w_up.T, "z")
    flat = tokens.reshape(count, width)
    proj, normed_t = project(flat, gain_attn, (w_query, w_key, w_value), parts)

    task_hot = (tasks[:, None] == jnp.arange(groups, dtype=jnp.int32)[None, :]).astype(F32)
    table_rows = jnp.einsum("rg,gbh->rbh", task_hot, bias_table, precision=highest)
    middle_offset = length - 1 + 3 * BLOCK
    near = buckets[middle_offset - WIDE + 1 : middle_offset + 1][::-1]
    bucket_hot = (near[None, :] == jnp.arange(bucket_count, dtype=jnp.int32)[:, None]).astype(F32)
    bias = jnp.einsum("rbh,bk->rhk", table_rows, bucket_hot, precision=highest)
    bias = bias.reshape(rows * pairs, 2, WIDE)
    seg = segments.reshape(count, 1)
    lane = jnp.arange(BLOCK, dtype=jnp.int32)[None, :]
    kseg = (lane == seg).astype(BF16)
    qseg = jnp.where((lane != seg) & (lane < 4), -1e30, 0.0).astype(BF16)

    def attend_part(first, pairs_here, proj, made):
        return attend(first, pairs_here, pairs, rows, length, proj, kseg, qseg, bias, made)

    up_state, (proj, w_down) = gather_1(net, up_state, (proj, w_down))
    down_state = net.gather(w_down, "z")
    sixth = max(1, pairs // 6)
    made = attend_part(0, sixth, proj, None)
    up_state, (made, proj) = gather_2(net, up_state, (made, proj))
    made = attend_part(sixth, 2 * sixth, proj, made)
    down_state, (made, proj) = gather_1(net, down_state, (made, proj))
    made = attend_part(3 * sixth, sixth, proj, made)
    ups, (made, proj) = gather_3(net, up_state, (made, proj))
    made = attend_part(4 * sixth, sixth, proj, made)
    down_state, (made, proj) = gather_2(net, down_state, (made, proj))
    made = attend_part(5 * sixth, pairs - 5 * sixth, proj, made)
    mixed, mixed_t = made[2:]
    g = cotangent.reshape(count, width)
    middle, second, second_t, g_t = before_ffn(mixed, w_out, flat, gain_ffn, g)
    downs, second = gather_3(net, down_state, second)

    ups, downs, second = hold((ups, downs, second))
    output, gf_own, gf_other, grad_second = ffn(
        net, ups, downs, second, second_t, g, g_t, middle
    )
    gf_other, grad_second = hold((gf_other, grad_second))
    gf_theirs = net.fetch(gf_other, "c", 1)
    cols1 = width * parts
    cols2 = width + BLOCK
    cut1 = cols1 // 2
    cut2 = width // 2
    grad_middle, grad_mixed, grad_gain_ffn, *r1 = after_ffn(
        net, grad_second, middle, gain_ffn, g, w_out, mixed_t, cols1
    )
    sf, grad_mixed = scatter_1(net, gf_own, gf_theirs, grad_mixed)

    def back_part(i, grad_mixed, cols, buffers, at):
        d, off, *r = attend_grad(
            net, part * i, part, pairs, rows, length, proj, made, grad_mixed, normed_t, cols, buffers, at
        )
        return d, off, r

    dproj = [None] * parts
    doff = [None] * parts
    dproj[0], doff[0], r1 = back_part(0, grad_mixed, cols1, r1, width)
    dproj[1], doff[1], r1 = back_part(1, grad_mixed, cols1, r1, 2 * width)
    grad_mixed, r1, sf = hold((grad_mixed, r1, sf))
    r1_theirs = net.fetch(r1[1], "c", 1)
    state1, grad_mixed = reduce_1(net, r1[0], r1_theirs, cut1, grad_mixed, True)
    dproj[2], doff[2], r2 = back_part(2, grad_mixed, cols2, None, 0)
    state1, (doff, r2, dproj) = reduce_2(net, state1, (doff, r2, dproj), False)

    per_row = jnp.concatenate([d.reshape(part, rows, 2, WIDE) for d in doff], axis=0)
    per_row = per_row.transpose(1, 0, 2, 3).reshape(rows, heads, WIDE)
    grad_bucket = jnp.einsum("rhk,bk->rbh", per_row, bucket_hot, precision=highest)
    grad_table = jnp.einsum("rg,rbh->gbh", task_hot, grad_bucket, precision=highest)
    small = jnp.concatenate([grad_table.reshape(-1, width), grad_gain_ffn], axis=0)
    table_cols = small.shape[0] - 1
    small = jnp.pad(small.T, ((0, 0), (0, BLOCK - small.shape[0]))).astype(BF16)
    c = net.places()[3]
    half = width // 2
    r2 = [
        lax.dynamic_update_slice(
            r, lax.dynamic_slice_in_dim(small, at * half, half, axis=0), (0, width)
        )
        for r, at in zip(r2, (c, 1 - c))
    ]
    r2, dproj = hold((r2, dproj))
    r2_theirs = net.fetch(r2[1], "c", 1)
    grad_tokens = token_grad(
        dproj, (w_query, w_key, w_value), flat, gain_attn, grad_middle
    )
    state1, (r2, grad_tokens) = reduce_3(net, state1, (r2, grad_tokens))
    state2, grad_tokens = reduce_1(net, r2[0], r2_theirs, cut2, grad_tokens, False)
    state1, grad_tokens = fold_z(net, state1, grad_tokens)
    state2, grad_tokens = reduce_2(net, state2, grad_tokens, False)
    def head_runs(first, count_here, i):
        return [
            (first + (3 * p + i) * BLOCK, first + (3 * p + i + 1) * BLOCK)
            for p in range(count_here)
        ]

    front = pairs - (pairs - 2 * part)
    weights = (w_query, w_key, w_value)
    cuts1 = [head_runs(width, front, i) for i in range(3)] + [[(0, width)]]
    cuts2 = [head_runs(0, pairs - front, i) for i in range(3)] + [[(width, width + BLOCK)]]

    def finish_1(value, rel, into):
        return finish(net, value, rel, cuts1, weights, gain_attn, width, 0, into, None)

    def finish_2(value, rel, into):
        return finish(
            net, value, rel, cuts2, weights, gain_attn, width, front * BLOCK, into, made1[4]
        )

    state2, grad_tokens = reduce_3(net, state2, grad_tokens)
    last1, grad_tokens = spread_0(net, state1, grad_tokens)
    sf, grad_tokens = scatter_2(net, sf, grad_tokens)
    state2, grad_tokens = fold_z(net, state2, grad_tokens)
    last1, grad_tokens = spread_z(net, last1, grad_tokens)
    last2, grad_tokens = spread_0(net, state2, grad_tokens)
    last1, grad_tokens = spread_1(net, last1, cut1, grad_tokens)
    last2, grad_tokens = spread_z(net, last2, grad_tokens)
    sf, grad_tokens = scatter_3(net, sf, grad_tokens)
    last1, grad_tokens = spread_2(net, last1, grad_tokens)
    last2, grad_tokens = spread_1(net, last2, cut2, grad_tokens)
    sf, grad_tokens = fold_z(net, sf, grad_tokens)
    last1, grad_tokens = spread_3(net, last1, grad_tokens)
    made1 = finish_1(last1[0], 0, None)
    last2, (grad_tokens, made1) = spread_2(net, last2, (grad_tokens, made1))
    made1 = finish_1(last1[1], 1, made1)
    last2, (grad_tokens, sf, made1) = spread_3(net, last2, (grad_tokens, sf, made1))
    made2 = finish_2(last2[0], 0, made1[:3])
    grad_ffn = total(sf)
    grad_down, grad_up = grad_ffn[0], grad_ffn[1].T

    made2 = finish_2(last2[1], 1, made2)
    grad_query, grad_key, grad_value, small, gain_sum = made2
    grad_w_out = made1[3]
    grad_table = small[:table_cols].reshape(groups, bucket_count, heads)
    return (
        output.reshape(rows, length, width),
        grad_tokens.reshape(rows, length, width),
        grad_query,
        grad_key,
        grad_value,
        grad_w_out,
        grad_up,
        grad_down,
        grad_table,
        gain_sum.reshape(-1),
        small[table_cols],
    )


def solution(mesh):
    in_specs = (
        P(("ma", "an"), None, None),
        P(("ma", "an")),
        P(("ma", "an"), None),
        P(),
        P(),
        P(),
        P(),
        P(),
        P("ma", "an"),
        P("an", "ma"),
        P(),
        P(),
        P(),
        P(("ma", "an"), None, None),
    )
    out_specs = (
        P(("ma", "an"), None, None),
        P(("ma", "an"), None, None),
        P(),
        P(),
        P(),
        P(),
        P("ma", "an"),
        P("an", "ma"),
        P(),
        P(),
        P(),
    )

    def whole(*args):
        net = Links(mesh.shape["ma"], mesh.shape["an"], args[0].shape[-1])
        return local(net, *args)

    return jax.shard_map(whole, mesh=mesh, in_specs=in_specs, out_specs=out_specs, check_vma=False)
```

```python
import jax
import jax.numpy as jnp
from jax import lax
from jax.sharding import PartitionSpec as P
from jax.experimental import pallas as pl
from jax.experimental.pallas import tpu as pltpu

epsilon = 1e-06
highest = lax.Precision.HIGHEST
F32 = jnp.float32
BF16 = jnp.bfloat16
BLOCK = 128
REACH = 2
WIDE = 6 * BLOCK
CONTRACT_LANES = (((1,), (1,)), ((), ()))
CONTRACT_ROWS = (((0,), (0,)), ((), ()))
PLAIN = (((1,), (0,)), ((), ()))
hold = lax.optimization_barrier
brief = pl.CostEstimate(flops=1000, bytes_accessed=1000, transcendentals=0)


def far(x):
    return pltpu.with_memory_space_constraint(x, pltpu.HBM)


def dot(a, b, dims=PLAIN):
    return lax.dot_general(a, b, dims, preferred_element_type=F32)


def attend_body(p_ref, kseg_ref, qseg_ref, f_ref, *refs):
    u_ref, s_ref, o_ref, ot_ref = refs[-4:]
    length = p_ref.shape[0]
    blocks = length // BLOCK
    lane = lax.broadcasted_iota(jnp.int32, (length, BLOCK), 1)
    q_aug = jnp.concatenate([p_ref[:, :BLOCK] * BF16(0.125), qseg_ref[...]], axis=1)
    k = p_ref[:, BLOCK : 2 * BLOCK]
    v_t = p_ref[:, 2 * BLOCK :].astype(F32).T.astype(BF16)
    k_aug = [
        jnp.concatenate([jnp.where((lane >= 64) == (h == 1), k, BF16(0)), kseg_ref[...]], axis=1)
        for h in range(2)
    ]
    v_aug = [
        jnp.concatenate([v_t[64 * h : 64 * h + 64], jnp.ones((16, length), BF16)], axis=0)
        for h in range(2)
    ]
    tiles = [
        pltpu.roll(
            jnp.broadcast_to(f_ref[0, h : h + 1, :], (BLOCK, WIDE)), 0, 1, stride=1, stride_axis=0
        )
        for h in range(2)
    ]

    def score(h, s):
        return dot(k_aug[h], q_aug[256 * s : 256 * s + 256], CONTRACT_LANES)

    def weigh(h, s, st):
        for half in range(2):
            qb = 2 * s + half
            scored = {}
            peak = None
            for kb in range(blocks):
                o = kb - qb
                if abs(o) > REACH:
                    continue
                b = (
                    st[BLOCK * kb : BLOCK * kb + BLOCK, BLOCK * half : BLOCK * half + BLOCK]
                    + tiles[h][:, 384 - BLOCK * o : 512 - BLOCK * o]
                )
                scored[kb] = b
                peak = b if peak is None else jnp.maximum(peak, b)
            peak = jnp.max(peak, axis=0, keepdims=True)
            for kb in range(blocks):
                if kb in scored:
                    e = jnp.exp(scored[kb] - peak).astype(BF16)
                else:
                    e = jnp.zeros((BLOCK, BLOCK), BF16)
                u_ref[0, h, BLOCK * kb : BLOCK * kb + BLOCK, BLOCK * qb : BLOCK * qb + BLOCK] = e

    def mix(h, s):
        ot = dot(v_aug[h], u_ref[0, h, :, 256 * s : 256 * s + 256])
        r = 1.0 / ot[64:65]
        s_ref[0, h : h + 1, 256 * s : 256 * s + 256] = r
        return ot[:64] * r

    units = [(h, s) for h in range(2) for s in range(blocks // 2)]
    made = {}
    ahead = score(*units[0])
    for i, unit in enumerate(units):
        st = ahead
        if i + 1 < len(units):
            ahead = score(*units[i + 1])
        weigh(*unit, st)
        if i > 0:
            made[units[i - 1]] = mix(*units[i - 1])
    made[units[-1]] = mix(*units[-1])
    outs = [
        jnp.concatenate([made[h, s] for s in range(blocks // 2)], axis=1) for h in range(2)
    ]
    o_t = jnp.concatenate(outs, axis=0)
    o_ref[...] = o_t.T.astype(BF16)
    ot_ref[...] = o_t.astype(BF16)


def pair_spec(length, per_group, first):
    return pl.BlockSpec(
        (None, length, 3 * BLOCK),
        lambda p, r: ((first + p) // per_group, r, (first + p) % per_group),
    )


def attend(first, count, pairs, rows, length, proj, kseg, qseg, bias, made):
    steps = rows * pairs
    args = [far(proj), kseg, qseg, bias]
    specs = [
        pair_spec(length, pairs // proj.shape[0], first),
        pl.BlockSpec((length, BLOCK), lambda p, r: (r, 0)),
        pl.BlockSpec((length, BLOCK), lambda p, r: (r, 0)),
        pl.BlockSpec((1, 2, WIDE), lambda p, r: (r * pairs + first + p, 0, 0)),
    ]
    alias = {}
    if made is not None:
        alias = {len(args) + i: i for i in range(4)}
        args += [far(made[0]), made[1], made[2], made[3]]
        specs += [pl.BlockSpec(memory_space=pl.ANY)] * 4
    return pl.pallas_call(
        attend_body,
        grid=(count, rows),
        in_specs=specs,
        out_specs=[
            pl.BlockSpec((1, 2, length, length), lambda p, r: ((first + p) * rows + r, 0, 0, 0)),
            pl.BlockSpec((1, 2, length), lambda p, r: ((first + p) * rows + r, 0, 0)),
            pl.BlockSpec((length, BLOCK), lambda p, r: (r, first + p)),
            pl.BlockSpec((BLOCK, length), lambda p, r: (first + p, r)),
        ],
        out_shape=[
            pltpu.HBM((steps, 2, length, length), BF16),
            jax.ShapeDtypeStruct((steps, 2, length), F32),
            jax.ShapeDtypeStruct((rows * length, pairs * BLOCK), BF16),
            jax.ShapeDtypeStruct((pairs * BLOCK, rows * length), BF16),
        ],
        input_output_aliases=alias,
        compiler_params=pltpu.CompilerParams(vmem_limit_bytes=16 * 1024 * 1024),
        cost_estimate=brief,
        name="attend",
    )(*args)


def attend_grad_body(
    place_ref, p_ref, u_ref, s_ref, o_ref, g_ref, mine_ref, theirs_ref, *refs
):
    dp_ref, df_ref, go_ref, gx_ref, ds_ref, acc_ref = refs[-6:]
    length = p_ref.shape[0]
    blocks = length // BLOCK
    lane = lax.broadcasted_iota(jnp.int32, (length, BLOCK), 1)
    q = p_ref[:, :BLOCK] * BF16(0.125)
    k = p_ref[:, BLOCK : 2 * BLOCK]
    v = p_ref[:, 2 * BLOCK :]
    k_t = k.astype(F32).T.astype(BF16)
    inv = jnp.concatenate(
        [jnp.broadcast_to(s_ref[0, h : h + 1, :], (64, length)) for h in range(2)], axis=0
    ).T
    g = g_ref[...].astype(F32) * inv
    prod = g * o_ref[...].astype(F32)
    g_low = g.astype(BF16)
    prod_hi = prod.astype(BF16)
    prod_lo = (prod - prod_hi.astype(F32)).astype(BF16)
    row = lax.broadcasted_iota(jnp.int32, (2 * BLOCK, BLOCK), 0)
    col = lax.broadcasted_iota(jnp.int32, (2 * BLOCK, BLOCK), 1)
    pick = jnp.where((((row // 64) % 2) == (col // 2)) & (col < 4), -1.0, 0.0).astype(BF16)
    centre = dot(jnp.concatenate([prod_hi, prod_lo], axis=1), pick)
    centre_hi = centre.astype(BF16)
    centre_lo = (centre - centre_hi.astype(F32)).astype(BF16)
    g_aug = jnp.concatenate([g_low, jnp.where(lane % 2 == 0, centre_hi, centre_lo)], axis=1)
    zero = BF16(0)
    mine = [(lane >= 64) == (h == 1) for h in range(2)]
    v_aug = [
        jnp.concatenate(
            [jnp.where(mine[h], v, zero), jnp.where((lane // 2) == h, BF16(1), zero)], axis=1
        )
        for h in range(2)
    ]
    diag = [[None] * (2 * REACH + 1) for _ in range(2)]
    dq_t, dv, dk = [], [], []

    def score(h, s):
        return dot(v_aug[h], g_aug[256 * s : 256 * s + 256], CONTRACT_LANES)

    def weigh(h, s, dp):
        for half in range(2):
            qb = 2 * s + half
            for kb in range(blocks):
                o = kb - qb
                krows = slice(BLOCK * kb, BLOCK * kb + BLOCK)
                qcols = slice(BLOCK * qb, BLOCK * qb + BLOCK)
                if abs(o) > REACH:
                    ds_ref[h, krows, qcols] = jnp.zeros((BLOCK, BLOCK), BF16)
                    continue
                ds = (
                    u_ref[0, h, krows, qcols].astype(F32)
                    * dp[krows, BLOCK * half : BLOCK * half + BLOCK]
                )
                ds_ref[h, krows, qcols] = ds.astype(BF16)
                d = diag[h][o + REACH]
                diag[h][o + REACH] = ds if d is None else d + ds

    def values(h):
        dv.append(dot(u_ref[0, h], jnp.where(mine[h], g_low, zero)))

    def keys(h):
        dk.append(dot(ds_ref[h], jnp.where(mine[h], q, zero)))

    def queries(h):
        dq_t.append(dot(k_t[64 * h : 64 * h + 64], ds_ref[h]))

    def offsets(h):
        wide = jnp.concatenate([jnp.zeros((BLOCK, BLOCK), F32)] + diag[h][::-1], axis=1)
        step = BLOCK // 2
        while step:
            wide = wide[:step] + pltpu.roll(wide[step:], WIDE - step, 1)
            step //= 2
        df_ref[0, h : h + 1, :] = wide

    strips = range(blocks // 2)
    dps = [[score(h, s) for s in strips] for h in range(2)]
    values(0)
    for s in strips:
        weigh(0, s, dps[0][s])
    values(1)
    keys(0)
    queries(0)
    for s in strips:
        weigh(1, s, dps[1][s])
    offsets(0)
    keys(1)
    queries(1)
    offsets(1)
    dv = dv[0] + dv[1]
    dk = dk[0] + dk[1]
    dq = jnp.concatenate(dq_t, axis=0).T * 0.125
    d_all = jnp.concatenate([dq.astype(BF16), dk.astype(BF16), dv.astype(BF16)], axis=1)
    dp_ref[...] = d_all
    half = mine_ref.shape[0]
    row_step = pl.program_id(1)
    add = dot(jnp.concatenate([mine_ref[...], theirs_ref[...]], axis=0), d_all)

    @pl.when(row_step == 0)
    def _():
        acc_ref[...] = add

    @pl.when(row_step != 0)
    def _():
        acc_ref[...] += add

    @pl.when(row_step == pl.num_programs(1) - 1)
    def _():
        go_ref[...] = acc_ref[:half].astype(BF16)
        gx_ref[...] = acc_ref[half:].astype(BF16)


def attend_grad(
    net, first, count, pairs, rows, length, proj, made, grad_mixed, normed_t, cols, buffers, at
):
    saved, inverse, mixed, _ = made
    steps = rows * count
    half = normed_t.shape[0] // 2
    wide = 3 * BLOCK
    args = [far(proj), far(saved), inverse, mixed, grad_mixed, far(normed_t), far(normed_t)]
    specs = [
        pl.BlockSpec(
            (None, length, wide),
            lambda p, r, w, per=pairs // proj.shape[0]: ((first + p) // per, r, (first + p) % per),
        ),
        pl.BlockSpec((1, 2, length, length), lambda p, r, w: ((first + p) * rows + r, 0, 0, 0)),
        pl.BlockSpec((1, 2, length), lambda p, r, w: ((first + p) * rows + r, 0, 0)),
        pl.BlockSpec((length, BLOCK), lambda p, r, w: (r, first + p)),
        pl.BlockSpec((length, BLOCK), lambda p, r, w: (r, first + p)),
        pl.BlockSpec((half, length), lambda p, r, w: (w[3], r)),
        pl.BlockSpec((half, length), lambda p, r, w: (1 - w[3], r)),
    ]
    alias = {}
    if buffers is not None:
        alias = {1 + len(args) + i: 2 + i for i in range(2)}
        args += [far(b) for b in buffers]
        specs += [pl.BlockSpec(memory_space=pl.ANY)] * 2
    g_spec = pl.BlockSpec((half, wide), lambda p, r, w: (0, at // wide + p))
    return pl.pallas_call(
        attend_grad_body,
        grid_spec=pltpu.PrefetchScalarGridSpec(
            num_scalar_prefetch=1,
            grid=(count, rows),
            in_specs=specs,
            out_specs=[
                pl.BlockSpec((length, wide), lambda p, r, w: (r, p)),
                pl.BlockSpec((1, 2, WIDE), lambda p, r, w: (p * rows + r, 0, 0)),
                g_spec,
                g_spec,
            ],
            scratch_shapes=[
                pltpu.VMEM((2, length, length), BF16),
                pltpu.VMEM((2 * half, wide), F32),
            ],
        ),
        out_shape=[
            pltpu.HBM((rows * length, count * wide), BF16),
            jax.ShapeDtypeStruct((steps, 2, WIDE), F32),
            pltpu.HBM((half, cols), BF16),
            pltpu.HBM((half, cols), BF16),
        ],
        input_output_aliases=alias,
        compiler_params=pltpu.CompilerParams(vmem_limit_bytes=24 * 1024 * 1024),
        cost_estimate=brief,
        name="attend_grad",
    )(net.places(), *args)


def pick(options, index):
    out = options[0]
    for k in range(1, len(options)):
        out = jnp.where(index == k, options[k], out)
    return out


def by_distance(slices, at):
    n = len(slices)
    return [pick(slices, lax.rem(at - t + n, n)) for t in range(n)]


def in_order(pieces, at):
    n = len(pieces)
    return [pick(pieces, lax.rem(at - k + n, n)) for k in range(n)]


def by_flip(slices, at):
    return [pick(slices, lax.bitwise_xor(at, k)) for k in range(len(slices))]


def cut_rows(v, n):
    size = v.shape[0] // n
    return [v[size * k : size * k + size] for k in range(n)]


def cut_lanes(v, n):
    size = v.shape[-1] // n
    return [v[..., size * k : size * k + size] for k in range(n)]


def total(parts):
    out = parts[0].astype(F32)
    for p in parts[1:]:
        out = out + p.astype(F32)
    return out


class Links:
    def __init__(self, ma, an, width):
        z = min(4, an // 2)
        self.an = an
        self.size = {"y": ma, "z": z, "x": an // (2 * z), "c": 2}
        self.stride = {"c": 1, "x": 2, "z": 2 * self.size["x"]}
        self.tidy = width % (ma * BLOCK) == 0 and width % (8 * ma * an) == 0

    def places(self):
        an = lax.axis_index("an")
        found = [lax.axis_index("ma")]
        found += [(an // self.stride[a]) % self.size[a] for a in ("z", "x", "c")]
        return jnp.stack([f.astype(jnp.int32) for f in found])

    def fetch(self, value, axis, back):
        n = self.size[axis]
        if axis == "y":
            return lax.ppermute(value, "ma", [(i, (i + back) % n) for i in range(n)])
        s = self.stride[axis]
        pairs = []
        for i in range(self.an):
            at = (i // s) % n
            pairs.append((i, i + ((at + back) % n - at) * s))
        return lax.ppermute(value, "an", pairs)

    def flip(self, value, axis, bits):
        s = self.stride[axis]
        pairs = []
        for i in range(self.an):
            at = (i // s) % self.size[axis]
            pairs.append((i, i + ((at ^ bits) - at) * s))
        return lax.ppermute(value, "an", pairs)

    def gather(self, value, axis):
        return [value] + [self.fetch(value, axis, t) for t in range(1, self.size[axis])]

    def spread(self, parts, axis):
        n = self.size[axis]
        return [parts[0]] + [self.fetch(parts[t], axis, n - t) for t in range(1, n)]

    def step(self, fn, arrays, shapes, name, along, steps=1, away=False):
        arrays, along = hold((list(arrays), along))
        return hold((self.stage(fn, arrays, shapes, name, steps, away), along))

    def stage(self, fn, arrays, shapes, name, steps, away):
        outs = [jax.ShapeDtypeStruct(s, BF16) for s in shapes]
        place = self.places()
        if not self.tidy:
            got = fn(*[place[i] for i in range(4)], *arrays)
            return [g.astype(BF16).reshape(o.shape) for g, o in zip(got, outs)]
        count = len(arrays)

        def body(place_ref, *refs):
            got = fn(*[place_ref[i] for i in range(4)], *[r[...] for r in refs[:count]])
            for g, r in zip(got, refs[count:]):
                r[...] = g.astype(BF16)

        def spec(a):
            rest = len(a.shape) - 1
            return pl.BlockSpec(
                (a.shape[0] // steps,) + a.shape[1:], lambda i, p, rest=rest: (i,) + (0,) * rest
            )

        return pl.pallas_call(
            body,
            grid_spec=pltpu.PrefetchScalarGridSpec(
                num_scalar_prefetch=1,
                grid=(steps,),
                in_specs=[spec(a) for a in arrays],
                out_specs=[spec(o) for o in outs],
            ),
            out_shape=[pltpu.HBM(o.shape, o.dtype) for o in outs] if away else outs,
            compiler_params=pltpu.CompilerParams(vmem_limit_bytes=16 * 1024 * 1024),
            cost_estimate=brief,
            name=name,
        )(place, *arrays)


def gather_1(net, pieces, along):
    rows, cols = pieces[0].shape
    half = rows // 2
    n = len(pieces)

    def fn(y, z, x, c, *pieces):
        v = jnp.stack(in_order(pieces, z))
        return [v[:, :half], v[:, half:]]

    (a, b), along = net.step(fn, pieces, [(n, half, cols)] * 2, "gather_z", along)
    return (net.gather(a, "x"), net.gather(b, "y")), along


def gather_2(net, state, along):
    a, b = state
    n, half, cols = a[0].shape

    def fn(y, z, x, c, *parts):
        a_in = in_order(parts[: len(a)], x)
        b_in = in_order(parts[len(a) :], y)
        return [jnp.stack(a_in, axis=1), jnp.concatenate(b_in, axis=-1)]

    (a, b), along = net.step(
        fn, a + b, [(n, len(a), half, cols), (n, half, cols * len(b))], "gather_xy", along
    )
    return (net.gather(a, "y"), net.gather(b, "x")), along


def gather_3(net, state, along):
    a, b = state
    n, nx, half, cols = a[0].shape

    def fn(y, z, x, c, *parts):
        a_in = jnp.concatenate(in_order(parts[: len(a)], y), axis=-1)
        b_in = jnp.stack(in_order(parts[len(a) :], x), axis=1)
        return [jnp.concatenate([a_in, b_in], axis=2)]

    shape = (n, nx, 2 * half, cols * len(a))
    (own,), along = net.step(fn, a + b, [shape], "gather_yx", along, steps=n if net.tidy else 1)
    return net.gather(own, "c"), along


def scatter_1(net, own, theirs, along):
    nz, two, nx, hb, width = own.shape
    half = hb // 2
    ny = net.size["y"]

    def fn(y, z, x, c, own, theirs):
        v = total([own, theirs])
        a, b = v[..., :half, :], v[..., half:, :]
        return by_distance(cut_lanes(a, ny), y) + by_distance([b[:, :, k] for k in range(nx)], x)

    shapes = [(nz, two, nx, half, width // ny)] * ny + [(nz, two, half, width)] * nx
    parts, along = net.step(
        fn, [own, theirs], shapes, "scatter_yx", along, steps=nz if net.tidy else 1
    )
    return (net.spread(parts[:ny], "y"), net.spread(parts[ny:], "x")), along


def scatter_2(net, state, along):
    a, b = state
    nz, two, nx, half, cols = a[0].shape
    ny = net.size["y"]

    def fn(y, z, x, c, *parts):
        va, vb = total(parts[:ny]), total(parts[ny:])
        return by_distance([va[:, :, k] for k in range(nx)], x) + by_distance(cut_lanes(vb, ny), y)

    shapes = [(nz, two, half, cols)] * (nx + ny)
    parts, along = net.step(fn, a + b, shapes, "scatter_xy", along)
    return (net.spread(parts[:nx], "x"), net.spread(parts[nx:], "y")), along


def scatter_3(net, state, along):
    a, b = state
    nz, two, half, cols = a[0].shape

    def fn(y, z, x, c, *parts):
        v = jnp.concatenate([total(parts[: len(a)]), total(parts[len(a) :])], axis=2)
        return halves([v[k] for k in range(nz)], z)

    parts, along = net.step(fn, a + b, [(nz // 2, two, 2 * half, cols)] * 2, "scatter_z", along)
    return (parts[0], net.flip(parts[1], "z", 1)), along


def halves(slices, at):
    p = by_flip(slices, at)
    return [jnp.stack([p[0], p[2]]), jnp.stack([p[1], p[3]])]


def fold_z(net, state, along):
    kept, got = state

    def fn(y, z, x, c, kept, got):
        v = total([kept, got])
        return [v[0], v[1]]

    parts, along = net.step(fn, [kept, got], [kept.shape[1:]] * 2, "fold_z", along)
    return [parts[0], net.flip(parts[1], "z", 2)], along


def reduce_1(net, own, theirs, cut, along, away):
    rows, cols = own.shape
    ny, nx = net.size["y"], net.size["x"]

    def fn(y, z, x, c, own, theirs):
        v = total([own, theirs])
        return by_distance(cut_rows(v[:, :cut], ny), y) + by_distance(cut_rows(v[:, cut:], nx), x)

    shapes = [(rows // ny, cut)] * ny + [(rows // nx, cols - cut)] * nx
    parts, along = net.step(fn, [own, theirs], shapes, "reduce_yx", along, away=away)
    return (net.spread(parts[:ny], "y"), net.spread(parts[ny:], "x")), along


def reduce_2(net, state, along, away):
    a, b = state
    ny, nx = net.size["y"], net.size["x"]

    def fn(y, z, x, c, *parts):
        va, vb = total(parts[: len(a)]), total(parts[len(a) :])
        return by_distance(cut_rows(va, nx), x) + by_distance(cut_rows(vb, ny), y)

    shapes = [(a[0].shape[0] // nx, a[0].shape[1])] * nx
    shapes += [(b[0].shape[0] // ny, b[0].shape[1])] * ny
    parts, along = net.step(fn, a + b, shapes, "reduce_xy", along, away=away)
    return (net.spread(parts[:nx], "x"), net.spread(parts[nx:], "y")), along


def reduce_3(net, state, along):
    a, b = state
    n = net.size["z"]

    def fn(y, z, x, c, *parts):
        v = jnp.concatenate([total(parts[: len(a)]), total(parts[len(a) :])], axis=1)
        return halves(cut_rows(v, n), z)

    shape = (n // 2, a[0].shape[0] // n, a[0].shape[1] + b[0].shape[1])
    parts, along = net.step(fn, a + b, [shape] * 2, "reduce_z", along)
    return (parts[0], net.flip(parts[1], "z", 1)), along


def spread_0(net, parts, along):
    def fn(y, z, x, c, *parts):
        return [total(parts)]

    (front,), along = net.step(fn, parts, [parts[0].shape], "spread_sum", along)
    return [front, net.flip(front, "z", 2)], along


def spread_z(net, pieces, along):
    def fn(y, z, x, c, *pieces):
        return [jnp.stack(pieces)]

    (pair,), along = net.step(fn, pieces, [(2,) + pieces[0].shape], "spread_pair", along)
    return [pair, net.flip(pair, "z", 1)], along


def spread_1(net, pairs, cut, along):
    _, rows, cols = pairs[0].shape

    def fn(y, z, x, c, *pairs):
        found = [p[k].astype(F32) for k in range(2) for p in pairs]
        v = jnp.concatenate(by_flip(found, z), axis=0)
        return [v[:, :cut], v[:, cut:]]

    shapes = [(4 * rows, cut), (4 * rows, cols - cut)]
    (a, b), along = net.step(fn, pairs, shapes, "spread_z", along)
    return (net.gather(a, "x"), net.gather(b, "y")), along


def spread_2(net, state, along):
    a, b = state

    def fn(y, z, x, c, *parts):
        va = jnp.concatenate(in_order(parts[: len(a)], x), axis=0)
        vb = jnp.concatenate(in_order(parts[len(a) :], y), axis=0)
        return [va, vb]

    shapes = [(len(p) * p[0].shape[0], p[0].shape[1]) for p in (a, b)]
    (a, b), along = net.step(fn, a + b, shapes, "spread_xy", along)
    return (net.gather(a, "y"), net.gather(b, "x")), along


def spread_3(net, state, along):
    a, b = state

    def fn(y, z, x, c, *parts):
        va = jnp.concatenate(in_order(parts[: len(a)], y), axis=0)
        vb = jnp.concatenate(in_order(parts[len(a) :], x), axis=0)
        return [jnp.concatenate([va, vb], axis=1)]

    shape = (len(a) * a[0].shape[0], a[0].shape[1] + b[0].shape[1])
    (v,), along = net.step(fn, a + b, [shape], "spread_yx", along)
    return net.gather(v, "c"), along


def finish(net, value, rel, cuts, weights, gain, width, heads_from, into, so_far):
    half, cols = value.shape
    tile = BLOCK
    steps = half // tile
    widths = [sum(b - a for a, b in runs) for runs in cuts]
    narrow = widths[3] == BLOCK

    def body(place_ref, v_ref, wq_ref, wk_ref, wv_ref, gain_ref, *refs):
        outs = refs[-5:]
        v = v_ref[...].astype(F32)
        made = [jnp.concatenate([v[:, a:b] for a, b in runs], axis=1) for runs in cuts]
        for k, (out, m) in enumerate(zip(outs, made)):
            out[...] = m.T[:8] if k == 3 and narrow else m
        acc = made[0] * wq_ref[...].astype(F32)
        acc = acc + made[1] * wk_ref[...].astype(F32) + made[2] * wv_ref[...].astype(F32)
        part = jnp.broadcast_to(jnp.sum(acc, axis=1, keepdims=True), (tile, BLOCK)).T[:1]
        part = part / gain_ref[...]
        outs[4][...] = part if so_far is None else part + refs[0][...]

    def row(i, p):
        return (p[3] if rel == 0 else 1 - p[3]) * steps + i

    def cols_spec(w, at):
        return pl.BlockSpec((tile, w), lambda i, p: (row(i, p), at // w))

    def lanes_spec(rows):
        return pl.BlockSpec((rows, tile), lambda i, p: (0, row(i, p)))

    args = [value, *[far(w) for w in weights], gain.reshape(1, -1)]
    specs = [pl.BlockSpec((tile, cols), lambda i, p: (i, 0))]
    specs += [cols_spec(widths[0], heads_from)] * 3 + [lanes_spec(1)]
    alias = {}
    if so_far is not None:
        args.append(so_far)
        specs.append(lanes_spec(1))
    if into:
        alias = {1 + len(args) + k: k for k in range(len(into))}
        args += list(into)
        specs += [pl.BlockSpec(memory_space=pl.ANY)] * len(into)
    return pl.pallas_call(
        body,
        grid_spec=pltpu.PrefetchScalarGridSpec(
            num_scalar_prefetch=1,
            grid=(steps,),
            in_specs=specs,
            out_specs=[cols_spec(w, heads_from) for w in widths[:3]]
            + [lanes_spec(8) if narrow else cols_spec(widths[3], 0), lanes_spec(1)],
        ),
        out_shape=[pltpu.HBM((2 * half, width), F32)] * 3
        + [
            jax.ShapeDtypeStruct((8, 2 * half), F32) if narrow else pltpu.HBM((2 * half, width), F32),
            jax.ShapeDtypeStruct((1, 2 * half), F32),
        ],
        input_output_aliases=alias,
        compiler_params=pltpu.CompilerParams(vmem_limit_bytes=20 * 1024 * 1024),
        cost_estimate=brief,
        name="finish",
    )(net.places(), *args)


def project(tokens, gain, weights, groups):
    count, width = tokens.shape
    tile = min(256, count)
    pairs_here = width // BLOCK // groups

    def body(t_ref, gain_ref, *refs):
        out, nt_ref = refs[-2:]
        x = t_ref[...].astype(F32)
        inv = lax.rsqrt(jnp.mean(x * x, axis=1, keepdims=True) + epsilon)
        normed = x * inv * gain_ref[...]
        low = normed.astype(BF16)
        nt_ref[...] = normed.T.astype(BF16)
        for i, w in enumerate(refs[:-2]):
            r = dot(low, w[...]).astype(BF16)
            for p in range(groups * pairs_here):
                at = (3 * (p % pairs_here) + i) * BLOCK
                out[p // pairs_here, :, at : at + BLOCK] = r[:, BLOCK * p : BLOCK * p + BLOCK]

    return pl.pallas_call(
        body,
        grid=(count // tile,),
        in_specs=[
            pl.BlockSpec((tile, width), lambda i: (i, 0)),
            pl.BlockSpec((1, width), lambda i: (0, 0)),
        ]
        + [pl.BlockSpec((width, width), lambda i: (0, 0))] * 3,
        out_specs=[
            pl.BlockSpec((groups, tile, 3 * width // groups), lambda i: (0, i, 0)),
            pl.BlockSpec((width, tile), lambda i: (0, i)),
        ],
        out_shape=[
            pltpu.HBM((groups, count, 3 * width // groups), BF16),
            pltpu.HBM((width, count), BF16),
        ],
        compiler_params=pltpu.CompilerParams(vmem_limit_bytes=24 * 1024 * 1024),
        cost_estimate=brief,
        name="project",
    )(far(tokens), gain.reshape(1, -1), *[far(w) for w in weights])


def gelu_parts(pre):
    k0 = 0.7978845608028654
    k1 = 0.044715
    sq = pre * pre
    s = 0.5 * jnp.tanh(pre * (k0 + (k0 * k1) * sq)) + 0.5
    act = pre * s
    slope = s + (act - act * s) * (2.0 * k0 + (6.0 * k0 * k1) * sq)
    return act, slope


def before_ffn(mixed, w_out, tokens, gain, g):
    count, width = mixed.shape
    tile = min(256, count)

    def body(mixed_ref, w_ref, t_ref, gain_ref, g_ref, mid_ref, s_ref, st_ref, gt_ref):
        mid = t_ref[...].astype(F32) + dot(mixed_ref[...], w_ref[...])
        inv = lax.rsqrt(jnp.mean(mid * mid, axis=1, keepdims=True) + epsilon)
        second = mid * inv * gain_ref[...]
        mid_ref[...] = mid.astype(BF16)
        s_ref[...] = second.astype(BF16)
        st_ref[...] = second.T.astype(BF16)
        gt_ref[...] = g_ref[...].astype(F32).T.astype(BF16)

    def rows_of(w):
        return pl.BlockSpec((tile, w), lambda i: (i, 0))

    cols = pl.BlockSpec((width, tile), lambda i: (0, i))
    return pl.pallas_call(
        body,
        grid=(count // tile,),
        in_specs=[
            rows_of(width),
            pl.BlockSpec((width, width), lambda i: (0, 0)),
            rows_of(width),
            pl.BlockSpec((1, width), lambda i: (0, 0)),
            rows_of(width),
        ],
        out_specs=[rows_of(width), rows_of(width), cols, cols],
        out_shape=[
            pltpu.HBM((count, width), BF16),
            pltpu.HBM((count, width), BF16),
            pltpu.HBM((width, count), BF16),
            pltpu.HBM((width, count), BF16),
        ],
        compiler_params=pltpu.CompilerParams(vmem_limit_bytes=20 * 1024 * 1024),
        cost_estimate=brief,
        name="before_ffn",
    )(mixed, far(w_out), far(tokens), gain.reshape(1, -1), far(g))


def ffn(net, ups, downs, second, second_t, g, g_t, middle):
    nz, nx, hb, width = ups[0].shape
    count = g.shape[0]
    part = nx * hb
    tile = 256 if count % 256 == 0 else count
    lanes = 256 if width % 256 == 0 else width

    def body(
        place_ref, u0_ref, u1_ref, d0_ref, d1_ref, st_far, gt_far, g_far, s_far, m_far,
        out_ref, go_ref, gx_ref, gs_ref, act_ref, gu_ref, acc_ref, gsum_ref,
        st_ref, gt_ref, g_ref, s_ref, m_ref, sems,
    ):
        step = pl.program_id(0)
        st_copy, gt_copy, g_copy, s_copy, m_copy = [
            pltpu.make_async_copy(a, b, sems.at[i])
            for i, (a, b) in enumerate(
                (
                    (st_far, st_ref),
                    (gt_far, gt_ref),
                    (g_far, g_ref),
                    (s_far, s_ref),
                    (m_far, m_ref),
                )
            )
        ]

        @pl.when(step == 0)
        def _():
            for copy in (st_copy, gt_copy, g_copy, s_copy, m_copy):
                copy.start()
            st_copy.wait()
            gt_copy.wait()

        up_all, down_all = [
            jnp.concatenate([r[...].reshape(part, width) for r in refs], axis=0)
            for refs in ((u0_ref, u1_ref), (d0_ref, d1_ref))
        ]
        starts = list(range(0, count, tile))

        def both(t):
            return dot(up_all, st_ref[:, t : t + tile]), dot(down_all, gt_ref[:, t : t + tile])

        @pl.when(step == 0)
        def _():
            acc_ref[...] = jnp.zeros_like(acc_ref)
            gsum_ref[...] = jnp.zeros_like(gsum_ref)

        def sums(t):
            at = slice(t, t + tile)
            acc_ref[at] += dot(act_ref[:, at], down_all, CONTRACT_ROWS)
            gsum_ref[at] += dot(gu_ref[:, at], up_all, CONTRACT_ROWS)

        ahead = both(starts[0])
        for n, t in enumerate(starts):
            pre, gh = ahead
            if n + 1 < len(starts):
                ahead = both(starts[n + 1])
            act, slope = gelu_parts(pre)
            act_ref[:, t : t + tile] = act.astype(BF16)
            gu_ref[:, t : t + tile] = (gh * slope).astype(BF16)
            if n > 0:
                sums(starts[n - 1])
        sums(starts[-1])

        @pl.when(step == 0)
        def _():
            g_copy.wait()
            s_copy.wait()

        for k in range(0, width, lanes):
            cols = slice(k, k + lanes)
            gd = dot(act_ref[...], g_ref[:, cols]).astype(BF16)
            gu = dot(gu_ref[...], s_ref[:, cols]).astype(BF16)
            for rel in range(2):
                for i in range(nx):
                    at = part * rel + hb * i
                    out = (go_ref, gx_ref)[rel]
                    out[0, i, :, cols] = gd[at : at + hb]
                    out[1, i, :, cols] = gu[at : at + hb]

        @pl.when(step == nz - 1)
        def _():
            m_copy.wait()
            out_ref[...] = (m_ref[...].astype(F32) + acc_ref[...]).astype(BF16)
            gs_ref[...] = gsum_ref[...].astype(BF16)

    away = pl.BlockSpec(memory_space=pltpu.HBM)

    one = pl.BlockSpec((None, nx, hb, width), lambda i, p: (i, 0, 0, 0))
    two = pl.BlockSpec((None, 2, nx, hb, width), lambda i, p: (i, 0, 0, 0, 0))
    flat = pl.BlockSpec((count, width), lambda i, p: (0, 0))
    return pl.pallas_call(
        body,
        grid_spec=pltpu.PrefetchScalarGridSpec(
            num_scalar_prefetch=1,
            grid=(nz,),
            in_specs=[one] * 4 + [away] * 5,
            out_specs=[flat, two, two, flat],
            scratch_shapes=[
                pltpu.VMEM((2 * part, count), BF16),
                pltpu.VMEM((2 * part, count), BF16),
                pltpu.VMEM((count, width), F32),
                pltpu.VMEM((count, width), F32),
                pltpu.VMEM((width, count), BF16),
                pltpu.VMEM((width, count), BF16),
                pltpu.VMEM((count, width), BF16),
                pltpu.VMEM((count, width), BF16),
                pltpu.VMEM((count, width), BF16),
                pltpu.SemaphoreType.DMA((5,)),
            ],
        ),
        out_shape=[
            pltpu.HBM((count, width), BF16),
            pltpu.HBM((nz, 2, nx, hb, width), BF16),
            pltpu.HBM((nz, 2, nx, hb, width), BF16),
            pltpu.HBM((count, width), BF16),
        ],
        compiler_params=pltpu.CompilerParams(vmem_limit_bytes=42 * 1024 * 1024),
        cost_estimate=brief,
        name="ffn",
    )(net.places(), *ups, *downs, *[far(v) for v in (second_t, g_t, g, second, middle)])


def after_ffn(net, grad_second, middle, gain, g, w_out, mixed_t, cols):
    count, width = middle.shape
    half = width // 2
    tile = min(512, count)

    def body(
        place_ref, gs_ref, m_ref, gain_ref, g_ref, w_ref, mine_ref, theirs_ref,
        gm_ref, gx_ref, gg_ref, wo_ref, wx_ref, acc_ref,
    ):
        gs = gs_ref[...].astype(F32)
        m = m_ref[...].astype(F32)
        r = lax.rsqrt(jnp.mean(m * m, axis=1, keepdims=True) + epsilon)
        scaled = gs * gain_ref[...]
        mean = jnp.mean(scaled * m, axis=1, keepdims=True)
        gm = g_ref[...].astype(F32) + r * scaled - m * (r * r * r * mean)
        ga = gm.astype(BF16)
        gm_ref[...] = ga
        gx_ref[...] = dot(ga, w_ref[...], CONTRACT_LANES).astype(BF16)
        add = jnp.sum(gs * (m * r), axis=0, keepdims=True)
        step = pl.program_id(0)

        @pl.when(step == 0)
        def _():
            gg_ref[...] = add

        @pl.when(step != 0)
        def _():
            gg_ref[...] += add

        add_o = dot(jnp.concatenate([mine_ref[...], theirs_ref[...]], axis=0), ga)

        @pl.when(step == 0)
        def _():
            acc_ref[...] = add_o

        @pl.when(step != 0)
        def _():
            acc_ref[...] += add_o

        @pl.when(step == pl.num_programs(0) - 1)
        def _():
            wo_ref[...] = acc_ref[:half].astype(BF16)
            wx_ref[...] = acc_ref[half:].astype(BF16)

    def rows_of(w):
        return pl.BlockSpec((tile, w), lambda i, p: (i, 0))

    row = pl.BlockSpec((1, width), lambda i, p: (0, 0))
    grad = pl.BlockSpec((half, width), lambda i, p: (0, 0))
    return pl.pallas_call(
        body,
        grid_spec=pltpu.PrefetchScalarGridSpec(
            num_scalar_prefetch=1,
            grid=(count // tile,),
            in_specs=[
                rows_of(width),
                rows_of(width),
                row,
                rows_of(width),
                pl.BlockSpec((width, width), lambda i, p: (0, 0)),
                pl.BlockSpec((half, tile), lambda i, p: (p[3], i)),
                pl.BlockSpec((half, tile), lambda i, p: (1 - p[3], i)),
            ],
            out_specs=[rows_of(width), rows_of(width), row, grad, grad],
            scratch_shapes=[pltpu.VMEM((width, width), F32)],
        ),
        out_shape=[
            pltpu.HBM((count, width), BF16),
            jax.ShapeDtypeStruct((count, width), BF16),
            jax.ShapeDtypeStruct((1, width), F32),
            pltpu.HBM((half, cols), BF16),
            pltpu.HBM((half, cols), BF16),
        ],
        compiler_params=pltpu.CompilerParams(vmem_limit_bytes=24 * 1024 * 1024),
        cost_estimate=brief,
        name="after_ffn",
    )(net.places(), far(grad_second), far(middle), gain.reshape(1, -1), far(g), far(w_out), mixed_t, mixed_t)


def token_grad(dproj, weights, tokens, gain, grad_middle):
    count, width = tokens.shape
    tile = min(256, count)

    def body(*refs):
        d_refs = refs[: len(dproj)]
        w_refs = refs[len(dproj) : len(dproj) + 3]
        t_ref, gain_ref, gm_ref, out_ref = refs[len(dproj) + 3 :]
        gn = None
        for i, w in enumerate(w_refs):
            cols = []
            for d in d_refs:
                for p in range(d.shape[1] // (3 * BLOCK)):
                    at = (3 * p + i) * BLOCK
                    cols.append(d[:, at : at + BLOCK])
            r = dot(jnp.concatenate(cols, axis=1), w[...], CONTRACT_LANES)
            gn = r if gn is None else gn + r
        scaled = gn * gain_ref[...]
        x = t_ref[...].astype(F32)
        r = lax.rsqrt(jnp.mean(x * x, axis=1, keepdims=True) + epsilon)
        mean = jnp.mean(scaled * x, axis=1, keepdims=True)
        out_ref[...] = gm_ref[...].astype(F32) + r * scaled - x * (r * r * r * mean)

    def rows_of(w):
        return pl.BlockSpec((tile, w), lambda i: (i, 0))

    return pl.pallas_call(
        body,
        grid=(count // tile,),
        in_specs=[rows_of(d.shape[1]) for d in dproj]
        + [pl.BlockSpec(w.shape, lambda i: (0, 0)) for w in weights]
        + [rows_of(width), pl.BlockSpec((1, width), lambda i: (0, 0)), rows_of(width)],
        out_specs=rows_of(width),
        out_shape=pltpu.HBM((count, width), F32),
        compiler_params=pltpu.CompilerParams(vmem_limit_bytes=20 * 1024 * 1024),
        cost_estimate=brief,
        name="token_grad",
    )(*[far(d) for d in dproj], *[far(w) for w in weights], far(tokens), gain.reshape(1, -1), far(grad_middle))


def local(
    net,
    tokens,
    tasks,
    segments,
    buckets,
    w_query,
    w_key,
    w_value,
    w_out,
    w_up,
    w_down,
    bias_table,
    gain_attn,
    gain_ffn,
    cotangent,
):
    rows, length, width = tokens.shape
    groups, bucket_count, heads = bias_table.shape
    pairs = heads // 2
    count = rows * length
    parts = 3
    part = pairs // parts

    up_state = net.gather(w_up.T, "z")
    flat = tokens.reshape(count, width)
    proj, normed_t = project(flat, gain_attn, (w_query, w_key, w_value), parts)

    task_hot = (tasks[:, None] == jnp.arange(groups, dtype=jnp.int32)[None, :]).astype(F32)
    table_rows = jnp.einsum("rg,gbh->rbh", task_hot, bias_table, precision=highest)
    middle_offset = length - 1 + 3 * BLOCK
    near = buckets[middle_offset - WIDE + 1 : middle_offset + 1][::-1]
    bucket_hot = (near[None, :] == jnp.arange(bucket_count, dtype=jnp.int32)[:, None]).astype(F32)
    bias = jnp.einsum("rbh,bk->rhk", table_rows, bucket_hot, precision=highest)
    bias = bias.reshape(rows * pairs, 2, WIDE)
    seg = segments.reshape(count, 1)
    lane = jnp.arange(BLOCK, dtype=jnp.int32)[None, :]
    kseg = (lane == seg).astype(BF16)
    qseg = jnp.where((lane != seg) & (lane < 4), -1e30, 0.0).astype(BF16)

    def attend_part(first, pairs_here, proj, made):
        return attend(first, pairs_here, pairs, rows, length, proj, kseg, qseg, bias, made)

    up_state, (proj, w_down) = gather_1(net, up_state, (proj, w_down))
    down_state = net.gather(w_down, "z")
    made = attend_part(0, part, proj, None)
    up_state, (made, proj) = gather_2(net, up_state, (made, proj))
    made = attend_part(part, part, proj, made)
    down_state, (made, proj) = gather_1(net, down_state, (made, proj))
    made = attend_part(2 * part, pairs - 2 * part, proj, made)
    ups, made = gather_3(net, up_state, made)
    down_state, made = gather_2(net, down_state, made)
    mixed, mixed_t = made[2:]
    g = cotangent.reshape(count, width)
    middle, second, second_t, g_t = before_ffn(mixed, w_out, flat, gain_ffn, g)
    downs, second = gather_3(net, down_state, second)

    ups, downs, second = hold((ups, downs, second))
    output, gf_own, gf_other, grad_second = ffn(
        net, ups, downs, second, second_t, g, g_t, middle
    )
    gf_other, grad_second = hold((gf_other, grad_second))
    gf_theirs = net.fetch(gf_other, "c", 1)
    cols1 = width * parts
    cols2 = width + BLOCK
    cut1 = cols1 // 2
    cut2 = width // 2
    grad_middle, grad_mixed, grad_gain_ffn, *r1 = after_ffn(
        net, grad_second, middle, gain_ffn, g, w_out, mixed_t, cols1
    )
    sf, grad_mixed = scatter_1(net, gf_own, gf_theirs, grad_mixed)

    def back_part(i, grad_mixed, cols, buffers, at):
        d, off, *r = attend_grad(
            net, part * i, part, pairs, rows, length, proj, made, grad_mixed, normed_t, cols, buffers, at
        )
        return d, off, r

    dproj = [None] * parts
    doff = [None] * parts
    dproj[0], doff[0], r1 = back_part(0, grad_mixed, cols1, r1, width)
    dproj[1], doff[1], r1 = back_part(1, grad_mixed, cols1, r1, 2 * width)
    grad_mixed, r1, sf = hold((grad_mixed, r1, sf))
    r1_theirs = net.fetch(r1[1], "c", 1)
    state1, grad_mixed = reduce_1(net, r1[0], r1_theirs, cut1, grad_mixed, True)
    dproj[2], doff[2], r2 = back_part(2, grad_mixed, cols2, None, 0)
    state1, (doff, r2, dproj) = reduce_2(net, state1, (doff, r2, dproj), False)

    per_row = jnp.concatenate([d.reshape(part, rows, 2, WIDE) for d in doff], axis=0)
    per_row = per_row.transpose(1, 0, 2, 3).reshape(rows, heads, WIDE)
    grad_bucket = jnp.einsum("rhk,bk->rbh", per_row, bucket_hot, precision=highest)
    grad_table = jnp.einsum("rg,rbh->gbh", task_hot, grad_bucket, precision=highest)
    small = jnp.concatenate([grad_table.reshape(-1, width), grad_gain_ffn], axis=0)
    table_cols = small.shape[0] - 1
    small = jnp.pad(small.T, ((0, 0), (0, BLOCK - small.shape[0]))).astype(BF16)
    c = net.places()[3]
    half = width // 2
    r2 = [
        lax.dynamic_update_slice(
            r, lax.dynamic_slice_in_dim(small, at * half, half, axis=0), (0, width)
        )
        for r, at in zip(r2, (c, 1 - c))
    ]
    r2, dproj = hold((r2, dproj))
    r2_theirs = net.fetch(r2[1], "c", 1)
    grad_tokens = token_grad(
        dproj, (w_query, w_key, w_value), flat, gain_attn, grad_middle
    )
    state1, (r2, grad_tokens) = reduce_3(net, state1, (r2, grad_tokens))
    state2, grad_tokens = reduce_1(net, r2[0], r2_theirs, cut2, grad_tokens, False)
    state1, grad_tokens = fold_z(net, state1, grad_tokens)
    state2, grad_tokens = reduce_2(net, state2, grad_tokens, False)
    def head_runs(first, count_here, i):
        return [
            (first + (3 * p + i) * BLOCK, first + (3 * p + i + 1) * BLOCK)
            for p in range(count_here)
        ]

    front = pairs - (pairs - 2 * part)
    weights = (w_query, w_key, w_value)
    cuts1 = [head_runs(width, front, i) for i in range(3)] + [[(0, width)]]
    cuts2 = [head_runs(0, pairs - front, i) for i in range(3)] + [[(width, width + BLOCK)]]

    def finish_1(value, rel, into):
        return finish(net, value, rel, cuts1, weights, gain_attn, width, 0, into, None)

    def finish_2(value, rel, into):
        return finish(
            net, value, rel, cuts2, weights, gain_attn, width, front * BLOCK, into, made1[4]
        )

    state2, grad_tokens = reduce_3(net, state2, grad_tokens)
    last1, grad_tokens = spread_0(net, state1, grad_tokens)
    sf, grad_tokens = scatter_2(net, sf, grad_tokens)
    state2, grad_tokens = fold_z(net, state2, grad_tokens)
    last1, grad_tokens = spread_z(net, last1, grad_tokens)
    last2, grad_tokens = spread_0(net, state2, grad_tokens)
    last1, grad_tokens = spread_1(net, last1, cut1, grad_tokens)
    last2, grad_tokens = spread_z(net, last2, grad_tokens)
    sf, grad_tokens = scatter_3(net, sf, grad_tokens)
    last1, grad_tokens = spread_2(net, last1, grad_tokens)
    last2, grad_tokens = spread_1(net, last2, cut2, grad_tokens)
    sf, grad_tokens = fold_z(net, sf, grad_tokens)
    last1, grad_tokens = spread_3(net, last1, grad_tokens)
    made1 = finish_1(last1[0], 0, None)
    last2, (grad_tokens, made1) = spread_2(net, last2, (grad_tokens, made1))
    made1 = finish_1(last1[1], 1, made1)
    last2, (grad_tokens, sf, made1) = spread_3(net, last2, (grad_tokens, sf, made1))
    made2 = finish_2(last2[0], 0, made1[:3])
    grad_ffn = total(sf)
    grad_down, grad_up = grad_ffn[0], grad_ffn[1].T

    made2 = finish_2(last2[1], 1, made2)
    grad_query, grad_key, grad_value, small, gain_sum = made2
    grad_w_out = made1[3]
    grad_table = small[:table_cols].reshape(groups, bucket_count, heads)
    return (
        output.reshape(rows, length, width),
        grad_tokens.reshape(rows, length, width),
        grad_query,
        grad_key,
        grad_value,
        grad_w_out,
        grad_up,
        grad_down,
        grad_table,
        gain_sum.reshape(-1),
        small[table_cols],
    )


def solution(mesh):
    in_specs = (
        P(("ma", "an"), None, None),
        P(("ma", "an")),
        P(("ma", "an"), None),
        P(),
        P(),
        P(),
        P(),
        P(),
        P("ma", "an"),
        P("an", "ma"),
        P(),
        P(),
        P(),
        P(("ma", "an"), None, None),
    )
    out_specs = (
        P(("ma", "an"), None, None),
        P(("ma", "an"), None, None),
        P(),
        P(),
        P(),
        P(),
        P("ma", "an"),
        P("an", "ma"),
        P(),
        P(),
        P(),
    )

    def whole(*args):
        net = Links(mesh.shape["ma"], mesh.shape["an"], args[0].shape[-1])
        return local(net, *args)

    return jax.shard_map(whole, mesh=mesh, in_specs=in_specs, out_specs=out_specs, check_vma=False)
```

```python
import jax
import jax.numpy as jnp
from jax import lax
from jax.sharding import PartitionSpec as P
from jax.experimental import pallas as pl
from jax.experimental.pallas import tpu as pltpu

epsilon = 1e-06
highest = lax.Precision.HIGHEST
F32 = jnp.float32
BF16 = jnp.bfloat16
BLOCK = 128
REACH = 2
WIDE = 6 * BLOCK
CONTRACT_LANES = (((1,), (1,)), ((), ()))
CONTRACT_ROWS = (((0,), (0,)), ((), ()))
PLAIN = (((1,), (0,)), ((), ()))
hold = lax.optimization_barrier
brief = pl.CostEstimate(flops=1000, bytes_accessed=1000, transcendentals=0)


def far(x):
    return pltpu.with_memory_space_constraint(x, pltpu.HBM)


def dot(a, b, dims=PLAIN):
    return lax.dot_general(a, b, dims, preferred_element_type=F32)


def attend_body(p_ref, kseg_ref, qseg_ref, f_ref, *refs):
    u_ref, s_ref, o_ref, ot_ref = refs[-4:]
    length = p_ref.shape[0]
    blocks = length // BLOCK
    lane = lax.broadcasted_iota(jnp.int32, (length, BLOCK), 1)
    q_aug = jnp.concatenate([p_ref[:, :BLOCK] * BF16(0.125), qseg_ref[...]], axis=1)
    k = p_ref[:, BLOCK : 2 * BLOCK]
    v_t = p_ref[:, 2 * BLOCK :].astype(F32).T.astype(BF16)
    k_aug = [
        jnp.concatenate([jnp.where((lane >= 64) == (h == 1), k, BF16(0)), kseg_ref[...]], axis=1)
        for h in range(2)
    ]
    v_aug = [
        jnp.concatenate([v_t[64 * h : 64 * h + 64], jnp.ones((16, length), BF16)], axis=0)
        for h in range(2)
    ]
    tiles = [
        pltpu.roll(
            jnp.broadcast_to(f_ref[0, h : h + 1, :], (BLOCK, WIDE)), 0, 1, stride=1, stride_axis=0
        )
        for h in range(2)
    ]

    def score(h, s):
        return dot(k_aug[h], q_aug[256 * s : 256 * s + 256], CONTRACT_LANES)

    def weigh(h, s, st):
        for half in range(2):
            qb = 2 * s + half
            scored = {}
            peak = None
            for kb in range(blocks):
                o = kb - qb
                if abs(o) > REACH:
                    continue
                b = (
                    st[BLOCK * kb : BLOCK * kb + BLOCK, BLOCK * half : BLOCK * half + BLOCK]
                    + tiles[h][:, 384 - BLOCK * o : 512 - BLOCK * o]
                )
                scored[kb] = b
                peak = b if peak is None else jnp.maximum(peak, b)
            peak = jnp.max(peak, axis=0, keepdims=True)
            for kb in range(blocks):
                if kb in scored:
                    e = jnp.exp(scored[kb] - peak).astype(BF16)
                else:
                    e = jnp.zeros((BLOCK, BLOCK), BF16)
                u_ref[0, h, BLOCK * kb : BLOCK * kb + BLOCK, BLOCK * qb : BLOCK * qb + BLOCK] = e

    def mix(h, s):
        ot = dot(v_aug[h], u_ref[0, h, :, 256 * s : 256 * s + 256])
        r = 1.0 / ot[64:65]
        s_ref[0, h : h + 1, 256 * s : 256 * s + 256] = r
        return ot[:64] * r

    units = [(h, s) for h in range(2) for s in range(blocks // 2)]
    made = {}
    ahead = score(*units[0])
    for i, unit in enumerate(units):
        st = ahead
        if i + 1 < len(units):
            ahead = score(*units[i + 1])
        weigh(*unit, st)
        if i > 0:
            made[units[i - 1]] = mix(*units[i - 1])
    made[units[-1]] = mix(*units[-1])
    outs = [
        jnp.concatenate([made[h, s] for s in range(blocks // 2)], axis=1) for h in range(2)
    ]
    o_t = jnp.concatenate(outs, axis=0)
    o_ref[...] = o_t.T.astype(BF16)
    ot_ref[...] = o_t.astype(BF16)


def pair_spec(length, per_group, first):
    return pl.BlockSpec(
        (None, length, 3 * BLOCK),
        lambda p, r: ((first + p) // per_group, r, (first + p) % per_group),
    )


def attend(first, count, pairs, rows, length, proj, kseg, qseg, bias, made):
    steps = rows * pairs
    args = [far(proj), kseg, qseg, bias]
    specs = [
        pair_spec(length, pairs // proj.shape[0], first),
        pl.BlockSpec((length, BLOCK), lambda p, r: (r, 0)),
        pl.BlockSpec((length, BLOCK), lambda p, r: (r, 0)),
        pl.BlockSpec((1, 2, WIDE), lambda p, r: (r * pairs + first + p, 0, 0)),
    ]
    alias = {}
    if made is not None:
        alias = {len(args) + i: i for i in range(4)}
        args += [far(made[0]), made[1], made[2], made[3]]
        specs += [pl.BlockSpec(memory_space=pl.ANY)] * 4
    return pl.pallas_call(
        attend_body,
        grid=(count, rows),
        in_specs=specs,
        out_specs=[
            pl.BlockSpec((1, 2, length, length), lambda p, r: ((first + p) * rows + r, 0, 0, 0)),
            pl.BlockSpec((1, 2, length), lambda p, r: ((first + p) * rows + r, 0, 0)),
            pl.BlockSpec((length, BLOCK), lambda p, r: (r, first + p)),
            pl.BlockSpec((BLOCK, length), lambda p, r: (first + p, r)),
        ],
        out_shape=[
            pltpu.HBM((steps, 2, length, length), BF16),
            jax.ShapeDtypeStruct((steps, 2, length), F32),
            jax.ShapeDtypeStruct((rows * length, pairs * BLOCK), BF16),
            jax.ShapeDtypeStruct((pairs * BLOCK, rows * length), BF16),
        ],
        input_output_aliases=alias,
        compiler_params=pltpu.CompilerParams(vmem_limit_bytes=16 * 1024 * 1024),
        cost_estimate=brief,
        name="attend",
    )(*args)


def attend_grad_body(
    place_ref, p_ref, u_ref, s_ref, o_ref, g_ref, mine_ref, theirs_ref, *refs
):
    dp_ref, df_ref, go_ref, gx_ref, ds_ref, acc_ref = refs[-6:]
    length = p_ref.shape[0]
    blocks = length // BLOCK
    lane = lax.broadcasted_iota(jnp.int32, (length, BLOCK), 1)
    q = p_ref[:, :BLOCK] * BF16(0.125)
    k = p_ref[:, BLOCK : 2 * BLOCK]
    v = p_ref[:, 2 * BLOCK :]
    k_t = k.astype(F32).T.astype(BF16)
    inv = jnp.concatenate(
        [jnp.broadcast_to(s_ref[0, h : h + 1, :], (64, length)) for h in range(2)], axis=0
    ).T
    g = g_ref[...].astype(F32) * inv
    prod = g * o_ref[...].astype(F32)
    g_low = g.astype(BF16)
    prod_hi = prod.astype(BF16)
    prod_lo = (prod - prod_hi.astype(F32)).astype(BF16)
    row = lax.broadcasted_iota(jnp.int32, (2 * BLOCK, BLOCK), 0)
    col = lax.broadcasted_iota(jnp.int32, (2 * BLOCK, BLOCK), 1)
    pick = jnp.where((((row // 64) % 2) == (col // 2)) & (col < 4), -1.0, 0.0).astype(BF16)
    centre = dot(jnp.concatenate([prod_hi, prod_lo], axis=1), pick)
    centre_hi = centre.astype(BF16)
    centre_lo = (centre - centre_hi.astype(F32)).astype(BF16)
    g_aug = jnp.concatenate([g_low, jnp.where(lane % 2 == 0, centre_hi, centre_lo)], axis=1)
    zero = BF16(0)
    mine = [(lane >= 64) == (h == 1) for h in range(2)]
    v_aug = [
        jnp.concatenate(
            [jnp.where(mine[h], v, zero), jnp.where((lane // 2) == h, BF16(1), zero)], axis=1
        )
        for h in range(2)
    ]
    diag = [[None] * (2 * REACH + 1) for _ in range(2)]
    dq_t, dv, dk = [], [], []

    def score(h, s):
        return dot(v_aug[h], g_aug[256 * s : 256 * s + 256], CONTRACT_LANES)

    def weigh(h, s, dp):
        for half in range(2):
            qb = 2 * s + half
            for kb in range(blocks):
                o = kb - qb
                krows = slice(BLOCK * kb, BLOCK * kb + BLOCK)
                qcols = slice(BLOCK * qb, BLOCK * qb + BLOCK)
                if abs(o) > REACH:
                    ds_ref[h, krows, qcols] = jnp.zeros((BLOCK, BLOCK), BF16)
                    continue
                ds = (
                    u_ref[0, h, krows, qcols].astype(F32)
                    * dp[krows, BLOCK * half : BLOCK * half + BLOCK]
                )
                ds_ref[h, krows, qcols] = ds.astype(BF16)
                d = diag[h][o + REACH]
                diag[h][o + REACH] = ds if d is None else d + ds

    def values(h):
        dv.append(dot(u_ref[0, h], jnp.where(mine[h], g_low, zero)))

    def keys(h):
        dk.append(dot(ds_ref[h], jnp.where(mine[h], q, zero)))

    def queries(h):
        dq_t.append(dot(k_t[64 * h : 64 * h + 64], ds_ref[h]))

    def offsets(h):
        wide = jnp.concatenate([jnp.zeros((BLOCK, BLOCK), F32)] + diag[h][::-1], axis=1)
        step = BLOCK // 2
        while step:
            wide = wide[:step] + pltpu.roll(wide[step:], WIDE - step, 1)
            step //= 2
        df_ref[0, h : h + 1, :] = wide

    strips = range(blocks // 2)
    dps = [[score(h, s) for s in strips] for h in range(2)]
    values(0)
    for s in strips:
        weigh(0, s, dps[0][s])
    values(1)
    keys(0)
    queries(0)
    for s in strips:
        weigh(1, s, dps[1][s])
    offsets(0)
    keys(1)
    queries(1)
    offsets(1)
    dv = dv[0] + dv[1]
    dk = dk[0] + dk[1]
    dq = jnp.concatenate(dq_t, axis=0).T * 0.125
    d_all = jnp.concatenate([dq.astype(BF16), dk.astype(BF16), dv.astype(BF16)], axis=1)
    dp_ref[...] = d_all
    half = mine_ref.shape[0]
    row_step = pl.program_id(1)
    add = dot(jnp.concatenate([mine_ref[...], theirs_ref[...]], axis=0), d_all)

    @pl.when(row_step == 0)
    def _():
        acc_ref[...] = add

    @pl.when(row_step != 0)
    def _():
        acc_ref[...] += add

    @pl.when(row_step == pl.num_programs(1) - 1)
    def _():
        go_ref[...] = acc_ref[:half].astype(BF16)
        gx_ref[...] = acc_ref[half:].astype(BF16)


def attend_grad(
    net, first, count, pairs, rows, length, proj, made, grad_mixed, normed_t, cols, buffers, at
):
    saved, inverse, mixed, _ = made
    steps = rows * count
    half = normed_t.shape[0] // 2
    wide = 3 * BLOCK
    args = [far(proj), far(saved), inverse, mixed, grad_mixed, far(normed_t), far(normed_t)]
    specs = [
        pl.BlockSpec(
            (None, length, wide),
            lambda p, r, w, per=pairs // proj.shape[0]: ((first + p) // per, r, (first + p) % per),
        ),
        pl.BlockSpec((1, 2, length, length), lambda p, r, w: ((first + p) * rows + r, 0, 0, 0)),
        pl.BlockSpec((1, 2, length), lambda p, r, w: ((first + p) * rows + r, 0, 0)),
        pl.BlockSpec((length, BLOCK), lambda p, r, w: (r, first + p)),
        pl.BlockSpec((length, BLOCK), lambda p, r, w: (r, first + p)),
        pl.BlockSpec((half, length), lambda p, r, w: (w[3], r)),
        pl.BlockSpec((half, length), lambda p, r, w: (1 - w[3], r)),
    ]
    alias = {}
    if buffers is not None:
        alias = {1 + len(args) + i: 2 + i for i in range(2)}
        args += [far(b) for b in buffers]
        specs += [pl.BlockSpec(memory_space=pl.ANY)] * 2
    g_spec = pl.BlockSpec((half, wide), lambda p, r, w: (0, at // wide + p))
    return pl.pallas_call(
        attend_grad_body,
        grid_spec=pltpu.PrefetchScalarGridSpec(
            num_scalar_prefetch=1,
            grid=(count, rows),
            in_specs=specs,
            out_specs=[
                pl.BlockSpec((length, wide), lambda p, r, w: (r, p)),
                pl.BlockSpec((1, 2, WIDE), lambda p, r, w: (p * rows + r, 0, 0)),
                g_spec,
                g_spec,
            ],
            scratch_shapes=[
                pltpu.VMEM((2, length, length), BF16),
                pltpu.VMEM((2 * half, wide), F32),
            ],
        ),
        out_shape=[
            pltpu.HBM((rows * length, count * wide), BF16),
            jax.ShapeDtypeStruct((steps, 2, WIDE), F32),
            pltpu.HBM((half, cols), BF16),
            pltpu.HBM((half, cols), BF16),
        ],
        input_output_aliases=alias,
        compiler_params=pltpu.CompilerParams(vmem_limit_bytes=24 * 1024 * 1024),
        cost_estimate=brief,
        name="attend_grad",
    )(net.places(), *args)


def pick(options, index):
    out = options[0]
    for k in range(1, len(options)):
        out = jnp.where(index == k, options[k], out)
    return out


def by_distance(slices, at):
    n = len(slices)
    return [pick(slices, lax.rem(at - t + n, n)) for t in range(n)]


def in_order(pieces, at):
    n = len(pieces)
    return [pick(pieces, lax.rem(at - k + n, n)) for k in range(n)]


def by_flip(slices, at):
    return [pick(slices, lax.bitwise_xor(at, k)) for k in range(len(slices))]


def cut_rows(v, n):
    size = v.shape[0] // n
    return [v[size * k : size * k + size] for k in range(n)]


def cut_lanes(v, n):
    size = v.shape[-1] // n
    return [v[..., size * k : size * k + size] for k in range(n)]


def total(parts):
    out = parts[0].astype(F32)
    for p in parts[1:]:
        out = out + p.astype(F32)
    return out


class Links:
    def __init__(self, ma, an, width):
        z = min(4, an // 2)
        self.an = an
        self.size = {"y": ma, "z": z, "x": an // (2 * z), "c": 2}
        self.stride = {"c": 1, "x": 2, "z": 2 * self.size["x"]}
        self.tidy = width % (ma * BLOCK) == 0 and width % (8 * ma * an) == 0

    def places(self):
        an = lax.axis_index("an")
        found = [lax.axis_index("ma")]
        found += [(an // self.stride[a]) % self.size[a] for a in ("z", "x", "c")]
        return jnp.stack([f.astype(jnp.int32) for f in found])

    def fetch(self, value, axis, back):
        n = self.size[axis]
        if axis == "y":
            return lax.ppermute(value, "ma", [(i, (i + back) % n) for i in range(n)])
        s = self.stride[axis]
        pairs = []
        for i in range(self.an):
            at = (i // s) % n
            pairs.append((i, i + ((at + back) % n - at) * s))
        return lax.ppermute(value, "an", pairs)

    def flip(self, value, axis, bits):
        s = self.stride[axis]
        pairs = []
        for i in range(self.an):
            at = (i // s) % self.size[axis]
            pairs.append((i, i + ((at ^ bits) - at) * s))
        return lax.ppermute(value, "an", pairs)

    def gather(self, value, axis):
        return [value] + [self.fetch(value, axis, t) for t in range(1, self.size[axis])]

    def spread(self, parts, axis):
        n = self.size[axis]
        return [parts[0]] + [self.fetch(parts[t], axis, n - t) for t in range(1, n)]

    def step(self, fn, arrays, shapes, name, along, steps=1, away=False, early=()):
        arrays, along = hold((list(arrays), along))
        arrays = list(early) + arrays
        return hold((self.stage(fn, arrays, shapes, name, steps, away), along))

    def stage(self, fn, arrays, shapes, name, steps, away):
        outs = [jax.ShapeDtypeStruct(s, BF16) for s in shapes]
        place = self.places()
        if not self.tidy:
            got = fn(*[place[i] for i in range(4)], *arrays)
            return [g.astype(BF16).reshape(o.shape) for g, o in zip(got, outs)]
        count = len(arrays)

        def body(place_ref, *refs):
            got = fn(*[place_ref[i] for i in range(4)], *[r[...] for r in refs[:count]])
            for g, r in zip(got, refs[count:]):
                r[...] = g.astype(BF16)

        def spec(a):
            rest = len(a.shape) - 1
            return pl.BlockSpec(
                (a.shape[0] // steps,) + a.shape[1:], lambda i, p, rest=rest: (i,) + (0,) * rest
            )

        return pl.pallas_call(
            body,
            grid_spec=pltpu.PrefetchScalarGridSpec(
                num_scalar_prefetch=1,
                grid=(steps,),
                in_specs=[spec(a) for a in arrays],
                out_specs=[spec(o) for o in outs],
            ),
            out_shape=[pltpu.HBM(o.shape, o.dtype) for o in outs] if away else outs,
            compiler_params=pltpu.CompilerParams(vmem_limit_bytes=16 * 1024 * 1024),
            cost_estimate=brief,
            name=name,
        )(place, *arrays)


def gather_1(net, pieces, along):
    rows, cols = pieces[0].shape
    half = rows // 2
    n = len(pieces)

    def fn(y, z, x, c, *pieces):
        v = jnp.stack(in_order(pieces, z))
        return [v[:, :half], v[:, half:]]

    (a, b), along = net.step(fn, pieces, [(n, half, cols)] * 2, "gather_z", along)
    return (net.gather(a, "x"), net.gather(b, "y")), along


def gather_2(net, state, along):
    a, b = state
    n, half, cols = a[0].shape

    def fn(y, z, x, c, *parts):
        a_in = in_order(parts[: len(a)], x)
        b_in = in_order(parts[len(a) :], y)
        return [jnp.stack(a_in, axis=1), jnp.concatenate(b_in, axis=-1)]

    (a, b), along = net.step(
        fn, a + b, [(n, len(a), half, cols), (n, half, cols * len(b))], "gather_xy", along
    )
    return (net.gather(a, "y"), net.gather(b, "x")), along


def gather_3(net, state, along):
    a, b = state
    n, nx, half, cols = a[0].shape

    def fn(y, z, x, c, *parts):
        a_in = jnp.concatenate(in_order(parts[: len(a)], y), axis=-1)
        b_in = jnp.stack(in_order(parts[len(a) :], x), axis=1)
        return [jnp.concatenate([a_in, b_in], axis=2)]

    shape = (n, nx, 2 * half, cols * len(a))
    (own,), along = net.step(fn, a + b, [shape], "gather_yx", along, steps=n if net.tidy else 1)
    return net.gather(own, "c"), along


def scatter_1(net, own, theirs, along):
    nz, two, nx, hb, width = own.shape
    half = hb // 2
    ny = net.size["y"]

    def fn(y, z, x, c, own, theirs):
        v = total([own, theirs])
        a, b = v[..., :half, :], v[..., half:, :]
        return by_distance(cut_lanes(a, ny), y) + by_distance([b[:, :, k] for k in range(nx)], x)

    shapes = [(nz, two, nx, half, width // ny)] * ny + [(nz, two, half, width)] * nx
    parts, along = net.step(
        fn, [own, theirs], shapes, "scatter_yx", along, steps=nz if net.tidy else 1
    )
    return (net.spread(parts[:ny], "y"), net.spread(parts[ny:], "x")), along


def scatter_2(net, state, along):
    a, b = state
    nz, two, nx, half, cols = a[0].shape
    ny = net.size["y"]

    def fn(y, z, x, c, *parts):
        va, vb = total(parts[:ny]), total(parts[ny:])
        return by_distance([va[:, :, k] for k in range(nx)], x) + by_distance(cut_lanes(vb, ny), y)

    shapes = [(nz, two, half, cols)] * (nx + ny)
    parts, along = net.step(fn, a + b, shapes, "scatter_xy", along)
    return (net.spread(parts[:nx], "x"), net.spread(parts[nx:], "y")), along


def scatter_3(net, state, along):
    a, b = state
    nz, two, half, cols = a[0].shape

    def fn(y, z, x, c, *parts):
        v = jnp.concatenate([total(parts[: len(a)]), total(parts[len(a) :])], axis=2)
        return halves([v[k] for k in range(nz)], z)

    parts, along = net.step(fn, a + b, [(nz // 2, two, 2 * half, cols)] * 2, "scatter_z", along)
    return (parts[0], net.flip(parts[1], "z", 1)), along


def halves(slices, at):
    p = by_flip(slices, at)
    return [jnp.stack([p[0], p[2]]), jnp.stack([p[1], p[3]])]


def fold_z(net, state, along):
    kept, got = state

    def fn(y, z, x, c, kept, got):
        v = total([kept, got])
        return [v[0], v[1]]

    parts, along = net.step(fn, [kept, got], [kept.shape[1:]] * 2, "fold_z", along)
    return [parts[0], net.flip(parts[1], "z", 2)], along


def reduce_1(net, own, theirs, cut, along, away):
    rows, cols = own.shape
    ny, nx = net.size["y"], net.size["x"]

    def fn(y, z, x, c, own, theirs):
        v = total([own, theirs])
        return by_distance(cut_rows(v[:, :cut], ny), y) + by_distance(cut_rows(v[:, cut:], nx), x)

    shapes = [(rows // ny, cut)] * ny + [(rows // nx, cols - cut)] * nx
    parts, along = net.step(
        fn, [theirs], shapes, "reduce_yx", along, away=away, early=[own]
    )
    return (net.spread(parts[:ny], "y"), net.spread(parts[ny:], "x")), along


def reduce_2(net, state, along, away):
    a, b = state
    ny, nx = net.size["y"], net.size["x"]

    def fn(y, z, x, c, *parts):
        va, vb = total(parts[: len(a)]), total(parts[len(a) :])
        return by_distance(cut_rows(va, nx), x) + by_distance(cut_rows(vb, ny), y)

    shapes = [(a[0].shape[0] // nx, a[0].shape[1])] * nx
    shapes += [(b[0].shape[0] // ny, b[0].shape[1])] * ny
    parts, along = net.step(fn, a + b, shapes, "reduce_xy", along, away=away)
    return (net.spread(parts[:nx], "x"), net.spread(parts[nx:], "y")), along


def reduce_3(net, state, along):
    a, b = state
    n = net.size["z"]

    def fn(y, z, x, c, *parts):
        v = jnp.concatenate([total(parts[: len(a)]), total(parts[len(a) :])], axis=1)
        return halves(cut_rows(v, n), z)

    shape = (n // 2, a[0].shape[0] // n, a[0].shape[1] + b[0].shape[1])
    parts, along = net.step(fn, a + b, [shape] * 2, "reduce_z", along)
    return (parts[0], net.flip(parts[1], "z", 1)), along


def spread_0(net, parts, along):
    def fn(y, z, x, c, *parts):
        return [total(parts)]

    (front,), along = net.step(fn, parts, [parts[0].shape], "spread_sum", along)
    return [front, net.flip(front, "z", 2)], along


def spread_z(net, pieces, along):
    def fn(y, z, x, c, *pieces):
        return [jnp.stack(pieces)]

    (pair,), along = net.step(fn, pieces, [(2,) + pieces[0].shape], "spread_pair", along)
    return [pair, net.flip(pair, "z", 1)], along


def spread_1(net, pairs, cut, along):
    _, rows, cols = pairs[0].shape

    def fn(y, z, x, c, *pairs):
        found = [p[k].astype(F32) for k in range(2) for p in pairs]
        v = jnp.concatenate(by_flip(found, z), axis=0)
        return [v[:, :cut], v[:, cut:]]

    shapes = [(4 * rows, cut), (4 * rows, cols - cut)]
    (a, b), along = net.step(fn, pairs, shapes, "spread_z", along)
    return (net.gather(a, "x"), net.gather(b, "y")), along


def spread_2(net, state, along):
    a, b = state

    def fn(y, z, x, c, *parts):
        va = jnp.concatenate(in_order(parts[: len(a)], x), axis=0)
        vb = jnp.concatenate(in_order(parts[len(a) :], y), axis=0)
        return [va, vb]

    shapes = [(len(p) * p[0].shape[0], p[0].shape[1]) for p in (a, b)]
    (a, b), along = net.step(fn, a + b, shapes, "spread_xy", along)
    return (net.gather(a, "y"), net.gather(b, "x")), along


def spread_3(net, state, along):
    a, b = state

    def fn(y, z, x, c, *parts):
        va = jnp.concatenate(in_order(parts[: len(a)], y), axis=0)
        vb = jnp.concatenate(in_order(parts[len(a) :], x), axis=0)
        return [jnp.concatenate([va, vb], axis=1)]

    shape = (len(a) * a[0].shape[0], a[0].shape[1] + b[0].shape[1])
    (v,), along = net.step(fn, a + b, [shape], "spread_yx", along)
    return net.gather(v, "c"), along


def finish(net, value, rel, cuts, weights, gain, width, heads_from, into, so_far):
    half, cols = value.shape
    tile = BLOCK
    steps = half // tile
    widths = [sum(b - a for a, b in runs) for runs in cuts]
    narrow = widths[3] == BLOCK

    def body(place_ref, v_ref, wq_ref, wk_ref, wv_ref, gain_ref, *refs):
        outs = refs[-5:]
        v = v_ref[...].astype(F32)
        made = [jnp.concatenate([v[:, a:b] for a, b in runs], axis=1) for runs in cuts]
        for k, (out, m) in enumerate(zip(outs, made)):
            out[...] = m.T[:8] if k == 3 and narrow else m
        acc = made[0] * wq_ref[...].astype(F32)
        acc = acc + made[1] * wk_ref[...].astype(F32) + made[2] * wv_ref[...].astype(F32)
        part = jnp.broadcast_to(jnp.sum(acc, axis=1, keepdims=True), (tile, BLOCK)).T[:1]
        part = part / gain_ref[...]
        outs[4][...] = part if so_far is None else part + refs[0][...]

    def row(i, p):
        return (p[3] if rel == 0 else 1 - p[3]) * steps + i

    def cols_spec(w, at):
        return pl.BlockSpec((tile, w), lambda i, p: (row(i, p), at // w))

    def lanes_spec(rows):
        return pl.BlockSpec((rows, tile), lambda i, p: (0, row(i, p)))

    args = [value, *[far(w) for w in weights], gain.reshape(1, -1)]
    specs = [pl.BlockSpec((tile, cols), lambda i, p: (i, 0))]
    specs += [cols_spec(widths[0], heads_from)] * 3 + [lanes_spec(1)]
    alias = {}
    if so_far is not None:
        args.append(so_far)
        specs.append(lanes_spec(1))
    if into:
        alias = {1 + len(args) + k: k for k in range(len(into))}
        args += list(into)
        specs += [pl.BlockSpec(memory_space=pl.ANY)] * len(into)
    return pl.pallas_call(
        body,
        grid_spec=pltpu.PrefetchScalarGridSpec(
            num_scalar_prefetch=1,
            grid=(steps,),
            in_specs=specs,
            out_specs=[cols_spec(w, heads_from) for w in widths[:3]]
            + [lanes_spec(8) if narrow else cols_spec(widths[3], 0), lanes_spec(1)],
        ),
        out_shape=[pltpu.HBM((2 * half, width), F32)] * 3
        + [
            jax.ShapeDtypeStruct((8, 2 * half), F32) if narrow else pltpu.HBM((2 * half, width), F32),
            jax.ShapeDtypeStruct((1, 2 * half), F32),
        ],
        input_output_aliases=alias,
        compiler_params=pltpu.CompilerParams(vmem_limit_bytes=20 * 1024 * 1024),
        cost_estimate=brief,
        name="finish",
    )(net.places(), *args)


def project(tokens, gain, weights, groups):
    count, width = tokens.shape
    tile = min(256, count)
    pairs_here = width // BLOCK // groups

    def body(t_ref, gain_ref, *refs):
        out, nt_ref = refs[-2:]
        x = t_ref[...].astype(F32)
        inv = lax.rsqrt(jnp.mean(x * x, axis=1, keepdims=True) + epsilon)
        normed = x * inv * gain_ref[...]
        low = normed.astype(BF16)
        nt_ref[...] = normed.T.astype(BF16)
        for i, w in enumerate(refs[:-2]):
            r = dot(low, w[...]).astype(BF16)
            for p in range(groups * pairs_here):
                at = (3 * (p % pairs_here) + i) * BLOCK
                out[p // pairs_here, :, at : at + BLOCK] = r[:, BLOCK * p : BLOCK * p + BLOCK]

    return pl.pallas_call(
        body,
        grid=(count // tile,),
        in_specs=[
            pl.BlockSpec((tile, width), lambda i: (i, 0)),
            pl.BlockSpec((1, width), lambda i: (0, 0)),
        ]
        + [pl.BlockSpec((width, width), lambda i: (0, 0))] * 3,
        out_specs=[
            pl.BlockSpec((groups, tile, 3 * width // groups), lambda i: (0, i, 0)),
            pl.BlockSpec((width, tile), lambda i: (0, i)),
        ],
        out_shape=[
            pltpu.HBM((groups, count, 3 * width // groups), BF16),
            pltpu.HBM((width, count), BF16),
        ],
        compiler_params=pltpu.CompilerParams(vmem_limit_bytes=24 * 1024 * 1024),
        cost_estimate=brief,
        name="project",
    )(far(tokens), gain.reshape(1, -1), *[far(w) for w in weights])


def gelu_parts(pre):
    k0 = 0.7978845608028654
    k1 = 0.044715
    sq = pre * pre
    s = 0.5 * jnp.tanh(pre * (k0 + (k0 * k1) * sq)) + 0.5
    act = pre * s
    slope = s + (act - act * s) * (2.0 * k0 + (6.0 * k0 * k1) * sq)
    return act, slope


def before_ffn(mixed, w_out, tokens, gain, g):
    count, width = mixed.shape
    tile = min(256, count)

    def body(mixed_ref, w_ref, t_ref, gain_ref, g_ref, mid_ref, s_ref, st_ref, gt_ref):
        mid = t_ref[...].astype(F32) + dot(mixed_ref[...], w_ref[...])
        inv = lax.rsqrt(jnp.mean(mid * mid, axis=1, keepdims=True) + epsilon)
        second = mid * inv * gain_ref[...]
        mid_ref[...] = mid.astype(BF16)
        s_ref[...] = second.astype(BF16)
        st_ref[...] = second.T.astype(BF16)
        gt_ref[...] = g_ref[...].astype(F32).T.astype(BF16)

    def rows_of(w):
        return pl.BlockSpec((tile, w), lambda i: (i, 0))

    cols = pl.BlockSpec((width, tile), lambda i: (0, i))
    return pl.pallas_call(
        body,
        grid=(count // tile,),
        in_specs=[
            rows_of(width),
            pl.BlockSpec((width, width), lambda i: (0, 0)),
            rows_of(width),
            pl.BlockSpec((1, width), lambda i: (0, 0)),
            rows_of(width),
        ],
        out_specs=[rows_of(width), rows_of(width), cols, cols],
        out_shape=[
            pltpu.HBM((count, width), BF16),
            pltpu.HBM((count, width), BF16),
            pltpu.HBM((width, count), BF16),
            pltpu.HBM((width, count), BF16),
        ],
        compiler_params=pltpu.CompilerParams(vmem_limit_bytes=20 * 1024 * 1024),
        cost_estimate=brief,
        name="before_ffn",
    )(mixed, far(w_out), far(tokens), gain.reshape(1, -1), far(g))


def ffn(net, ups, downs, second, second_t, g, g_t, middle):
    nz, nx, hb, width = ups[0].shape
    count = g.shape[0]
    part = nx * hb
    tile = 256 if count % 256 == 0 else count
    lanes = 256 if width % 256 == 0 else width

    def body(
        place_ref, u0_ref, u1_ref, d0_ref, d1_ref, st_far, gt_far, g_far, s_far, m_far,
        out_ref, go_ref, gx_ref, gs_ref, act_ref, gu_ref, acc_ref, gsum_ref,
        st_ref, gt_ref, g_ref, s_ref, m_ref, sems,
    ):
        step = pl.program_id(0)
        st_copy, gt_copy, g_copy, s_copy, m_copy = [
            pltpu.make_async_copy(a, b, sems.at[i])
            for i, (a, b) in enumerate(
                (
                    (st_far, st_ref),
                    (gt_far, gt_ref),
                    (g_far, g_ref),
                    (s_far, s_ref),
                    (m_far, m_ref),
                )
            )
        ]

        @pl.when(step == 0)
        def _():
            for copy in (st_copy, gt_copy, g_copy, s_copy, m_copy):
                copy.start()
            st_copy.wait()
            gt_copy.wait()

        up_all, down_all = [
            jnp.concatenate([r[...].reshape(part, width) for r in refs], axis=0)
            for refs in ((u0_ref, u1_ref), (d0_ref, d1_ref))
        ]
        starts = list(range(0, count, tile))

        def both(t):
            return dot(up_all, st_ref[:, t : t + tile]), dot(down_all, gt_ref[:, t : t + tile])

        @pl.when(step == 0)
        def _():
            acc_ref[...] = jnp.zeros_like(acc_ref)
            gsum_ref[...] = jnp.zeros_like(gsum_ref)

        def sums(t):
            at = slice(t, t + tile)
            acc_ref[at] += dot(act_ref[:, at], down_all, CONTRACT_ROWS)
            gsum_ref[at] += dot(gu_ref[:, at], up_all, CONTRACT_ROWS)

        ahead = both(starts[0])
        for n, t in enumerate(starts):
            pre, gh = ahead
            if n + 1 < len(starts):
                ahead = both(starts[n + 1])
            act, slope = gelu_parts(pre)
            act_ref[:, t : t + tile] = act.astype(BF16)
            gu_ref[:, t : t + tile] = (gh * slope).astype(BF16)
            if n > 0:
                sums(starts[n - 1])
        sums(starts[-1])

        @pl.when(step == 0)
        def _():
            g_copy.wait()
            s_copy.wait()

        for k in range(0, width, lanes):
            cols = slice(k, k + lanes)
            gd = dot(act_ref[...], g_ref[:, cols]).astype(BF16)
            gu = dot(gu_ref[...], s_ref[:, cols]).astype(BF16)
            for rel in range(2):
                for i in range(nx):
                    at = part * rel + hb * i
                    out = (go_ref, gx_ref)[rel]
                    out[0, i, :, cols] = gd[at : at + hb]
                    out[1, i, :, cols] = gu[at : at + hb]

        @pl.when(step == nz - 1)
        def _():
            m_copy.wait()
            out_ref[...] = (m_ref[...].astype(F32) + acc_ref[...]).astype(BF16)
            gs_ref[...] = gsum_ref[...].astype(BF16)

    away = pl.BlockSpec(memory_space=pltpu.HBM)

    one = pl.BlockSpec((None, nx, hb, width), lambda i, p: (i, 0, 0, 0))
    two = pl.BlockSpec((None, 2, nx, hb, width), lambda i, p: (i, 0, 0, 0, 0))
    flat = pl.BlockSpec((count, width), lambda i, p: (0, 0))
    return pl.pallas_call(
        body,
        grid_spec=pltpu.PrefetchScalarGridSpec(
            num_scalar_prefetch=1,
            grid=(nz,),
            in_specs=[one] * 4 + [away] * 5,
            out_specs=[flat, two, two, flat],
            scratch_shapes=[
                pltpu.VMEM((2 * part, count), BF16),
                pltpu.VMEM((2 * part, count), BF16),
                pltpu.VMEM((count, width), F32),
                pltpu.VMEM((count, width), F32),
                pltpu.VMEM((width, count), BF16),
                pltpu.VMEM((width, count), BF16),
                pltpu.VMEM((count, width), BF16),
                pltpu.VMEM((count, width), BF16),
                pltpu.VMEM((count, width), BF16),
                pltpu.SemaphoreType.DMA((5,)),
            ],
        ),
        out_shape=[
            pltpu.HBM((count, width), BF16),
            pltpu.HBM((nz, 2, nx, hb, width), BF16),
            pltpu.HBM((nz, 2, nx, hb, width), BF16),
            pltpu.HBM((count, width), BF16),
        ],
        compiler_params=pltpu.CompilerParams(vmem_limit_bytes=42 * 1024 * 1024),
        cost_estimate=brief,
        name="ffn",
    )(net.places(), *ups, *downs, *[far(v) for v in (second_t, g_t, g, second, middle)])


def after_ffn(net, grad_second, middle, gain, g, w_out, mixed_t, cols):
    count, width = middle.shape
    half = width // 2
    tile = min(512, count)

    def body(
        place_ref, gs_ref, m_ref, gain_ref, g_ref, w_ref, mine_ref, theirs_ref,
        gm_ref, gx_ref, gg_ref, wo_ref, wx_ref, acc_ref,
    ):
        gs = gs_ref[...].astype(F32)
        m = m_ref[...].astype(F32)
        r = lax.rsqrt(jnp.mean(m * m, axis=1, keepdims=True) + epsilon)
        scaled = gs * gain_ref[...]
        mean = jnp.mean(scaled * m, axis=1, keepdims=True)
        gm = g_ref[...].astype(F32) + r * scaled - m * (r * r * r * mean)
        ga = gm.astype(BF16)
        gm_ref[...] = ga
        gx_ref[...] = dot(ga, w_ref[...], CONTRACT_LANES).astype(BF16)
        add = jnp.sum(gs * (m * r), axis=0, keepdims=True)
        step = pl.program_id(0)

        @pl.when(step == 0)
        def _():
            gg_ref[...] = add

        @pl.when(step != 0)
        def _():
            gg_ref[...] += add

        add_o = dot(jnp.concatenate([mine_ref[...], theirs_ref[...]], axis=0), ga)

        @pl.when(step == 0)
        def _():
            acc_ref[...] = add_o

        @pl.when(step != 0)
        def _():
            acc_ref[...] += add_o

        @pl.when(step == pl.num_programs(0) - 1)
        def _():
            wo_ref[...] = acc_ref[:half].astype(BF16)
            wx_ref[...] = acc_ref[half:].astype(BF16)

    def rows_of(w):
        return pl.BlockSpec((tile, w), lambda i, p: (i, 0))

    row = pl.BlockSpec((1, width), lambda i, p: (0, 0))
    grad = pl.BlockSpec((half, width), lambda i, p: (0, 0))
    return pl.pallas_call(
        body,
        grid_spec=pltpu.PrefetchScalarGridSpec(
            num_scalar_prefetch=1,
            grid=(count // tile,),
            in_specs=[
                rows_of(width),
                rows_of(width),
                row,
                rows_of(width),
                pl.BlockSpec((width, width), lambda i, p: (0, 0)),
                pl.BlockSpec((half, tile), lambda i, p: (p[3], i)),
                pl.BlockSpec((half, tile), lambda i, p: (1 - p[3], i)),
            ],
            out_specs=[rows_of(width), rows_of(width), row, grad, grad],
            scratch_shapes=[pltpu.VMEM((width, width), F32)],
        ),
        out_shape=[
            pltpu.HBM((count, width), BF16),
            jax.ShapeDtypeStruct((count, width), BF16),
            jax.ShapeDtypeStruct((1, width), F32),
            pltpu.HBM((half, cols), BF16),
            pltpu.HBM((half, cols), BF16),
        ],
        compiler_params=pltpu.CompilerParams(vmem_limit_bytes=24 * 1024 * 1024),
        cost_estimate=brief,
        name="after_ffn",
    )(net.places(), far(grad_second), far(middle), gain.reshape(1, -1), far(g), far(w_out), mixed_t, mixed_t)


def token_grad(dproj, weights, tokens, gain, grad_middle):
    count, width = tokens.shape
    tile = min(256, count)

    def body(*refs):
        d_refs = refs[: len(dproj)]
        w_refs = refs[len(dproj) : len(dproj) + 3]
        t_ref, gain_ref, gm_ref, out_ref = refs[len(dproj) + 3 :]
        gn = None
        for i, w in enumerate(w_refs):
            cols = []
            for d in d_refs:
                for p in range(d.shape[1] // (3 * BLOCK)):
                    at = (3 * p + i) * BLOCK
                    cols.append(d[:, at : at + BLOCK])
            r = dot(jnp.concatenate(cols, axis=1), w[...], CONTRACT_LANES)
            gn = r if gn is None else gn + r
        scaled = gn * gain_ref[...]
        x = t_ref[...].astype(F32)
        r = lax.rsqrt(jnp.mean(x * x, axis=1, keepdims=True) + epsilon)
        mean = jnp.mean(scaled * x, axis=1, keepdims=True)
        out_ref[...] = gm_ref[...].astype(F32) + r * scaled - x * (r * r * r * mean)

    def rows_of(w):
        return pl.BlockSpec((tile, w), lambda i: (i, 0))

    return pl.pallas_call(
        body,
        grid=(count // tile,),
        in_specs=[rows_of(d.shape[1]) for d in dproj]
        + [pl.BlockSpec(w.shape, lambda i: (0, 0)) for w in weights]
        + [rows_of(width), pl.BlockSpec((1, width), lambda i: (0, 0)), rows_of(width)],
        out_specs=rows_of(width),
        out_shape=pltpu.HBM((count, width), F32),
        compiler_params=pltpu.CompilerParams(vmem_limit_bytes=20 * 1024 * 1024),
        cost_estimate=brief,
        name="token_grad",
    )(*[far(d) for d in dproj], *[far(w) for w in weights], far(tokens), gain.reshape(1, -1), far(grad_middle))


def local(
    net,
    tokens,
    tasks,
    segments,
    buckets,
    w_query,
    w_key,
    w_value,
    w_out,
    w_up,
    w_down,
    bias_table,
    gain_attn,
    gain_ffn,
    cotangent,
):
    rows, length, width = tokens.shape
    groups, bucket_count, heads = bias_table.shape
    pairs = heads // 2
    count = rows * length
    parts = 3
    part = pairs // parts

    up_state = net.gather(w_up.T, "z")
    flat = tokens.reshape(count, width)
    proj, normed_t = project(flat, gain_attn, (w_query, w_key, w_value), parts)

    task_hot = (tasks[:, None] == jnp.arange(groups, dtype=jnp.int32)[None, :]).astype(F32)
    table_rows = jnp.einsum("rg,gbh->rbh", task_hot, bias_table, precision=highest)
    middle_offset = length - 1 + 3 * BLOCK
    near = buckets[middle_offset - WIDE + 1 : middle_offset + 1][::-1]
    bucket_hot = (near[None, :] == jnp.arange(bucket_count, dtype=jnp.int32)[:, None]).astype(F32)
    bias = jnp.einsum("rbh,bk->rhk", table_rows, bucket_hot, precision=highest)
    bias = bias.reshape(rows * pairs, 2, WIDE)
    seg = segments.reshape(count, 1)
    lane = jnp.arange(BLOCK, dtype=jnp.int32)[None, :]
    kseg = (lane == seg).astype(BF16)
    qseg = jnp.where((lane != seg) & (lane < 4), -1e30, 0.0).astype(BF16)

    def attend_part(first, pairs_here, proj, made):
        return attend(first, pairs_here, pairs, rows, length, proj, kseg, qseg, bias, made)

    up_state, (proj, w_down) = gather_1(net, up_state, (proj, w_down))
    down_state = net.gather(w_down, "z")
    made = attend_part(0, part, proj, None)
    up_state, (made, proj) = gather_2(net, up_state, (made, proj))
    made = attend_part(part, part, proj, made)
    down_state, (made, proj) = gather_1(net, down_state, (made, proj))
    made = attend_part(2 * part, pairs - 2 * part, proj, made)
    ups, made = gather_3(net, up_state, made)
    down_state, made = gather_2(net, down_state, made)
    mixed, mixed_t = made[2:]
    g = cotangent.reshape(count, width)
    middle, second, second_t, g_t = before_ffn(mixed, w_out, flat, gain_ffn, g)
    downs, second = gather_3(net, down_state, second)

    ups, downs, second = hold((ups, downs, second))
    output, gf_own, gf_other, grad_second = ffn(
        net, ups, downs, second, second_t, g, g_t, middle
    )
    gf_other, grad_second = hold((gf_other, grad_second))
    gf_theirs = net.fetch(gf_other, "c", 1)
    cols1 = width * parts
    cols2 = width + BLOCK
    cut1 = cols1 // 2
    cut2 = width // 2
    grad_middle, grad_mixed, grad_gain_ffn, *r1 = after_ffn(
        net, grad_second, middle, gain_ffn, g, w_out, mixed_t, cols1
    )
    sf, grad_mixed = scatter_1(net, gf_own, gf_theirs, grad_mixed)

    def back_part(i, grad_mixed, cols, buffers, at):
        d, off, *r = attend_grad(
            net, part * i, part, pairs, rows, length, proj, made, grad_mixed, normed_t, cols, buffers, at
        )
        return d, off, r

    dproj = [None] * parts
    doff = [None] * parts
    dproj[0], doff[0], r1 = back_part(0, grad_mixed, cols1, r1, width)
    dproj[1], doff[1], r1 = back_part(1, grad_mixed, cols1, r1, 2 * width)
    grad_mixed, r1, sf = hold((grad_mixed, r1, sf))
    r1_theirs = net.fetch(r1[1], "c", 1)
    state1, grad_mixed = reduce_1(net, r1[0], r1_theirs, cut1, grad_mixed, True)
    dproj[2], doff[2], r2 = back_part(2, grad_mixed, cols2, None, 0)
    state1, (doff, r2, dproj) = reduce_2(net, state1, (doff, r2, dproj), False)

    per_row = jnp.concatenate([d.reshape(part, rows, 2, WIDE) for d in doff], axis=0)
    per_row = per_row.transpose(1, 0, 2, 3).reshape(rows, heads, WIDE)
    grad_bucket = jnp.einsum("rhk,bk->rbh", per_row, bucket_hot, precision=highest)
    grad_table = jnp.einsum("rg,rbh->gbh", task_hot, grad_bucket, precision=highest)
    small = jnp.concatenate([grad_table.reshape(-1, width), grad_gain_ffn], axis=0)
    table_cols = small.shape[0] - 1
    small = jnp.pad(small.T, ((0, 0), (0, BLOCK - small.shape[0]))).astype(BF16)
    c = net.places()[3]
    half = width // 2
    r2 = [
        lax.dynamic_update_slice(
            r, lax.dynamic_slice_in_dim(small, at * half, half, axis=0), (0, width)
        )
        for r, at in zip(r2, (c, 1 - c))
    ]
    r2, dproj = hold((r2, dproj))
    r2_theirs = net.fetch(r2[1], "c", 1)
    grad_tokens = token_grad(
        dproj, (w_query, w_key, w_value), flat, gain_attn, grad_middle
    )
    state1, (r2, grad_tokens) = reduce_3(net, state1, (r2, grad_tokens))
    state2, grad_tokens = reduce_1(net, r2[0], r2_theirs, cut2, grad_tokens, False)
    state1, grad_tokens = fold_z(net, state1, grad_tokens)
    state2, grad_tokens = reduce_2(net, state2, grad_tokens, False)
    def head_runs(first, count_here, i):
        return [
            (first + (3 * p + i) * BLOCK, first + (3 * p + i + 1) * BLOCK)
            for p in range(count_here)
        ]

    front = pairs - (pairs - 2 * part)
    weights = (w_query, w_key, w_value)
    cuts1 = [head_runs(width, front, i) for i in range(3)] + [[(0, width)]]
    cuts2 = [head_runs(0, pairs - front, i) for i in range(3)] + [[(width, width + BLOCK)]]

    def finish_1(value, rel, into):
        return finish(net, value, rel, cuts1, weights, gain_attn, width, 0, into, None)

    def finish_2(value, rel, into):
        return finish(
            net, value, rel, cuts2, weights, gain_attn, width, front * BLOCK, into, made1[4]
        )

    state2, grad_tokens = reduce_3(net, state2, grad_tokens)
    last1, grad_tokens = spread_0(net, state1, grad_tokens)
    sf, grad_tokens = scatter_2(net, sf, grad_tokens)
    state2, grad_tokens = fold_z(net, state2, grad_tokens)
    last1, grad_tokens = spread_z(net, last1, grad_tokens)
    last2, grad_tokens = spread_0(net, state2, grad_tokens)
    last1, grad_tokens = spread_1(net, last1, cut1, grad_tokens)
    last2, grad_tokens = spread_z(net, last2, grad_tokens)
    sf, grad_tokens = scatter_3(net, sf, grad_tokens)
    last1, grad_tokens = spread_2(net, last1, grad_tokens)
    last2, grad_tokens = spread_1(net, last2, cut2, grad_tokens)
    sf, grad_tokens = fold_z(net, sf, grad_tokens)
    last1, grad_tokens = spread_3(net, last1, grad_tokens)
    made1 = finish_1(last1[0], 0, None)
    last2, (grad_tokens, made1) = spread_2(net, last2, (grad_tokens, made1))
    made1 = finish_1(last1[1], 1, made1)
    last2, (grad_tokens, sf, made1) = spread_3(net, last2, (grad_tokens, sf, made1))
    made2 = finish_2(last2[0], 0, made1[:3])
    grad_ffn = total(sf)
    grad_down, grad_up = grad_ffn[0], grad_ffn[1].T

    made2 = finish_2(last2[1], 1, made2)
    grad_query, grad_key, grad_value, small, gain_sum = made2
    grad_w_out = made1[3]
    grad_table = small[:table_cols].reshape(groups, bucket_count, heads)
    return (
        output.reshape(rows, length, width),
        grad_tokens.reshape(rows, length, width),
        grad_query,
        grad_key,
        grad_value,
        grad_w_out,
        grad_up,
        grad_down,
        grad_table,
        gain_sum.reshape(-1),
        small[table_cols],
    )


def solution(mesh):
    in_specs = (
        P(("ma", "an"), None, None),
        P(("ma", "an")),
        P(("ma", "an"), None),
        P(),
        P(),
        P(),
        P(),
        P(),
        P("ma", "an"),
        P("an", "ma"),
        P(),
        P(),
        P(),
        P(("ma", "an"), None, None),
    )
    out_specs = (
        P(("ma", "an"), None, None),
        P(("ma", "an"), None, None),
        P(),
        P(),
        P(),
        P(),
        P("ma", "an"),
        P("an", "ma"),
        P(),
        P(),
        P(),
    )

    def whole(*args):
        net = Links(mesh.shape["ma"], mesh.shape["an"], args[0].shape[-1])
        return local(net, *args)

    return jax.shard_map(whole, mesh=mesh, in_specs=in_specs, out_specs=out_specs, check_vma=False)
```
